512 devices in a mesh: sx: 32 (over z, x_lo), sy: 16 (over x_hi, y, core).
Axes of the slice: x: 4 (x_hi: 2, x_lo: 2; x = x_hi * 2 + x_lo), y: 4, z: 16, core: 2. Of those that a mesh axis runs over, the one named last changes fastest.
Arguments:
- gap: float32 [32, 16, 384], P('sx', 'sy')
- kinv: float32 [32, 16, 768, 768], P('sx', 'sy')
- schur: float32 [32, 16, 768, 768], P('sx', 'sy')
- corner_modes: float32 [32, 16, 24, 768], P('sx', 'sy'), may hold values from -0.4375 to 0.4375
- coarse_inverse: float32 [3072, 3072], P(('sx', 'sy'))
- edge_map: int32 [32, 16, 768], P('sx', 'sy'), may hold values from 0 to 767, each once within a row
- corner_map: int32 [32, 16, 24], P('sx', 'sy'), may hold values from 0 to 3072, as said below
- links: int32 [32, 16, 2], P('sx', 'sy'), may hold values 0 or 1
Outputs:
- multipliers: float32 [32, 16, 384], P('sx', 'sy')
- residual: float32 [32, 16, 384], P('sx', 'sy')
The draws below stay inside these ranges and needn't reach their ends.
Inputs may be any that keep to these rules, and one draw needn't show every extreme that they name: `corner_map`: each coarse degree of freedom is named by the corners of at most four subdomains; corners in the last row or column of the slab's node grid are clamped and hold 3072; the coarse index of a node's dof d is its node number times 6 plus d.
All inputs are finite; a program needn't handle non-finite values. No bound on the sum of `links` on one device may be relied on, other than what follows from the above.
Results may differ from the reference program's by a relative error of at most 0.0003.
Values sent between devices are 32-bit elements; how exact they have to be, the bound alone decides.
No kernel may reach another device: no remote copies, remote signals or barrier semaphores. Data moves between devices by JAX's collectives and lax.ppermute only.
A program may use at most 64 MiB of HBM per device.

```python
import math
import jax
import jax.numpy as jnp
from jax import lax

B = 768
CD = 6
ITERS = 3
E = 192
NCO = 24
ROWS = 32
COLS = 16
NSUB = 512
NCOARSE = 3072


def symmetric_build(noise, diag_vals, order):
    eye = jnp.eye(order, dtype=jnp.float32)
    off = (noise + jnp.swapaxes(noise, -1, -2)) * (0.35 / math.sqrt(2.0 * order))
    full = off * (1.0 - eye) + diag_vals[..., :, None] * eye
    return full


def draw_kinv(key, part):
    key = jax.random.fold_in(key, 11)

    def single(sub):
        k1, k2 = jax.random.split(sub, 2)
        diag_vals = jnp.exp(jax.random.uniform(k1, (B,), jnp.float32, 0.0, math.log(3.0)))
        noise = jax.random.normal(k2, (B, B), jnp.float32)
        return symmetric_build(noise, diag_vals, B)
    keys = jax.random.split(key, NSUB)
    return lax.map(single, keys).reshape(ROWS, COLS, B, B)


def draw_schur(key, part):
    key = jax.random.fold_in(key, 23)

    def single(sub):
        k1, k2 = jax.random.split(sub, 2)
        diag_vals = jnp.exp(jax.random.uniform(k1, (B,), jnp.float32, 0.0, math.log(3.0)))
        noise = jax.random.normal(k2, (B, B), jnp.float32)
        return symmetric_build(noise, diag_vals, B)
    keys = jax.random.split(key, NSUB)
    return lax.map(single, keys).reshape(ROWS, COLS, B, B)


def draw_coarse_inverse(key, part):
    key = jax.random.fold_in(key, 37)
    k1, k2 = jax.random.split(key, 2)
    diag_vals = jnp.exp(jax.random.uniform(k1, (NCOARSE,), jnp.float32, 0.0, math.log(3.0)))
    noise = jax.random.normal(k2, (NCOARSE, NCOARSE), jnp.float32)
    return symmetric_build(noise, diag_vals, NCOARSE)


def draw_gap(key, part):
    key = jax.random.fold_in(key, 51)
    k1, k2 = jax.random.split(key)
    flat = (jnp.arange(ROWS)[:, None] * COLS + jnp.arange(COLS)[None, :]).astype(jnp.float32)
    position = (flat / max(NSUB - 1, 1))[..., None]
    spread_scale = jnp.exp(jax.random.uniform(k1, (ROWS, COLS, 2 * E), jnp.float32, 0.0, math.log(3.5)))
    base = jnp.clip(jax.random.normal(k2, (ROWS, COLS, 2 * E), jnp.float32), -4.0, 4.0)
    rise = jnp.exp(position * math.log(3.0))
    return base * rise * spread_scale


def draw_corner_map(key, part):
    key = jax.random.fold_in(key, 67)
    numbers = jax.random.permutation(key, NSUB).astype(jnp.int32)
    row_ids = jnp.arange(ROWS, dtype=jnp.int32)[:, None, None]
    col_ids = jnp.arange(COLS, dtype=jnp.int32)[None, :, None]
    down = jnp.array([0, 0, 1, 1], jnp.int32)[None, None, :]
    right = jnp.array([0, 1, 0, 1], jnp.int32)[None, None, :]
    node_row = row_ids + down
    node_col = col_ids + right
    valid = (node_row < ROWS) & (node_col < COLS)
    node = numbers[jnp.minimum(node_row, ROWS - 1) * COLS + jnp.minimum(node_col, COLS - 1)]
    index = node[..., None] * CD + jnp.arange(CD, dtype=jnp.int32)[None, None, None, :]
    index = jnp.where(valid[..., None], index, NCOARSE)
    return index.reshape(ROWS, COLS, NCO).astype(jnp.int32)


def place_ends(drawn, own_key, least, top_value):
    longest = drawn.shape.index(max(drawn.shape))
    spots = []
    for shift in (0, 1):
        where = [jax.random.randint(jax.random.fold_in(own_key, axis), (), 0, length) for axis, length in enumerate(drawn.shape)]
        where[longest] = (where[longest] + shift) % drawn.shape[longest]
        spots.append(tuple(where))
    return drawn.at[spots[0]].set(least).at[spots[1]].set(top_value)


def levels(key, extent, pieces, low, largest):
    gain, own = 1.0, jax.random.fold_in(key, 6)
    for dim, parts in pieces:
        draws = jnp.exp(jax.random.uniform(jax.random.fold_in(own, dim), (parts,), jnp.float32, low / len(pieces), largest / len(pieces)))
        gain = gain * jnp.repeat(draws, extent[dim] // parts).reshape([-1 if axis == dim else 1 for axis in range(len(extent))])
    return gain


def gaussian(stream_key, shape, scale, most, shards=(), kind=jnp.bfloat16):
    gain = levels(stream_key, shape, shards, -0.22, 0.18) if shards else 1.0
    values = jax.random.normal(stream_key, shape, jnp.float32) * scale * gain
    return jnp.minimum(jnp.maximum(values, -most), most).astype(kind)


def setup_inputs(seed: int = 0) -> dict:
    key_of = jax.random.split(jax.random.key(seed), 9)
    return {
        "gap": draw_gap(jax.random.fold_in(key_of[8], 71), 0),
        "kinv": draw_kinv(jax.random.fold_in(key_of[8], 71), 0),
        "schur": draw_schur(jax.random.fold_in(key_of[8], 71), 0),
        "corner_modes": gaussian(key_of[3], (ROWS, COLS, NCO, B), (B // 4) ** -0.5, 0.4375, ((0, 32), (1, 16)), jnp.float32),
        "coarse_inverse": draw_coarse_inverse(jax.random.fold_in(key_of[8], 71), 0),
        "edge_map": jax.vmap(lambda own: jax.random.permutation(own, B))(jax.random.split(key_of[5], ROWS * COLS)).reshape((ROWS, COLS, B)).astype(jnp.int32),
        "corner_map": draw_corner_map(jax.random.fold_in(key_of[8], 71), 0),
        "links": place_ends((jax.random.randint(key_of[7], (ROWS, COLS, 2), 0, 8) < 7).astype(jnp.int32), jax.random.fold_in(key_of[7], 1), 0, 1),
    }


def place(values, index):
    return jnp.zeros((B,), jnp.float32).at[index].set(values)


def reference(gap, kinv, schur, corner_modes, coarse_inverse, edge_map, corner_map, links):
    edge = B // 4
    highest = lax.Precision.HIGHEST
    cols = jnp.arange(COLS)[None, :]
    rows = jnp.arange(ROWS)[:, None]
    east_ok = ((cols < COLS - 1) & (links[..., 0] == 1)).astype(jnp.float32)
    south_ok = ((rows < ROWS - 1) & (links[..., 1] == 1)).astype(jnp.float32)
    mask = jnp.concatenate([jnp.broadcast_to(east_ok[..., None], (ROWS, COLS, edge)),
                            jnp.broadcast_to(south_ok[..., None], (ROWS, COLS, edge))], -1)

    def spread(field):
        east = field[..., :edge]
        south = field[..., edge:]
        from_west = jnp.pad(east, ((0, 0), (1, 0), (0, 0)))[:, :-1]
        from_north = jnp.pad(south, ((1, 0), (0, 0), (0, 0)))[:-1]
        iface = jnp.concatenate([east, south, -from_west, -from_north], -1)
        return jax.vmap(jax.vmap(place))(iface, edge_map)

    def jump(local):
        iface = jnp.take_along_axis(local, edge_map, axis=-1)
        from_east = jnp.pad(iface[..., 2 * edge:3 * edge], ((0, 0), (0, 1), (0, 0)))[:, 1:]
        from_south = jnp.pad(iface[..., 3 * edge:], ((0, 1), (0, 0), (0, 0)))[1:]
        return jnp.concatenate([iface[..., :edge] - from_east, iface[..., edge:2 * edge] - from_south], -1) * mask

    def apply(mats, vec):
        return jnp.einsum('rcij,rcj->rci', mats, vec, precision=highest)

    def operator(field):
        spread_w = spread(field)
        inner = apply(kinv, spread_w)
        loads = jnp.einsum('rcki,rci->rck', corner_modes, spread_w, precision=highest)
        coarse = jnp.zeros((NCOARSE + 1,), jnp.float32).at[corner_map.reshape(-1)].add(loads.reshape(-1))[:NCOARSE]
        solved = jnp.dot(coarse_inverse, coarse, precision=highest)
        corner_vals = jnp.concatenate([solved, jnp.zeros((1,), jnp.float32)])[corner_map]
        return jump(inner + jnp.einsum('rcki,rck->rci', corner_modes, corner_vals, precision=highest))

    def precondition(field):
        return 0.25 * jump(apply(schur, spread(field)))

    multipliers = jnp.zeros_like(gap)
    residual = mask * gap
    precond = precondition(residual)
    direction = precond
    norm_now = jnp.sum(residual * precond)
    for step in range(ITERS):
        image = operator(direction)
        alpha = norm_now / jnp.sum(direction * image)
        multipliers = multipliers + alpha * direction
        residual = residual - alpha * image
        if step + 1 < ITERS:
            precond = precondition(residual)
            norm_next = jnp.sum(residual * precond)
            direction = precond + (norm_next / norm_now) * direction
            norm_now = norm_next
    return multipliers, residual
```

```python
import jax
import jax.numpy as jnp
from jax import lax
from jax.experimental import pallas as pl
from jax.experimental.pallas import tpu as pltpu
from jax.sharding import PartitionSpec as P

ITERS = 3
LANES = 128
SLOT = 256
TILE = 8
CORNERS = 24
HIGHEST = lax.Precision.HIGHEST
VMEM = pl.BlockSpec(memory_space=pltpu.VMEM)
SMEM = pl.BlockSpec(memory_space=pltpu.SMEM)
LIMIT = 40 * 1024 * 1024

RES, MUL, DIR, IFACE, PARTNER, MASK, SCAL, NSTATE = 0, 8, 16, 24, 32, 40, 48, 56
GAMMA, LOAD = 48, 49


def call(kernel, inputs, outputs, specs=None, name=None):
    return pl.pallas_call(
        kernel,
        out_shape=[jax.ShapeDtypeStruct(shape, jnp.float32) for shape in outputs],
        in_specs=specs or [VMEM] * len(inputs),
        out_specs=[VMEM] * len(outputs),
        compiler_params=pltpu.CompilerParams(vmem_limit_bytes=LIMIT),
        name=name,
    )(*inputs)


def iota(shape, dim):
    return lax.broadcasted_iota(jnp.int32, shape, dim)


def as_tile(row):
    return jnp.concatenate([row[:, LANES * c : LANES * (c + 1)] for c in range(TILE)], axis=0)


def as_row(tile):
    return jnp.concatenate([tile[c : c + 1, :] for c in range(TILE)], axis=1)


def total(value):
    return jnp.sum(jnp.sum(value, axis=1, keepdims=True), axis=0, keepdims=True)


def apply_matrix(tile, map_tile, map_row, matrix_ref):
    width = matrix_ref.shape[0]
    values = jnp.transpose(tile)
    places = jnp.transpose(map_tile)
    lanes = iota((LANES, LANES), 1)
    pieces = []
    for t in range(width // LANES):
        acc = jnp.zeros((LANES, LANES), jnp.float32)
        for c in range(TILE):
            hit = places[:, c : c + 1] == lanes + t * LANES
            acc = acc + jnp.where(hit, values[:, c : c + 1], 0.0)
        pieces.append(jnp.sum(acc, axis=0, keepdims=True))
    out = jnp.zeros((TILE, TILE * LANES), jnp.float32)
    for b in range(width // LANES):
        rows = slice(b * LANES, (b + 1) * LANES)
        acc = matrix_ref[rows, 0:LANES] * pieces[0]
        for t in range(1, width // LANES):
            acc = acc + matrix_ref[rows, t * LANES : (t + 1) * LANES] * pieces[t]
        column = jnp.sum(acc, axis=1, keepdims=True)
        for s in range(LANES // TILE):
            index = iota((TILE, TILE * LANES), 0) + (b * LANES + s * TILE)
            out = out + jnp.where(map_row == index, column[s * TILE : (s + 1) * TILE, :], 0.0)
    return jnp.sum(out, axis=0, keepdims=True)


def coarse_load(weighted, modes_ref, near_ref, rt_ref, l_ref, nrows):
    own = jnp.sum(modes_ref[...] * weighted, axis=1, keepdims=True)
    near = near_ref[...] * weighted
    loads = [own]
    for q in range(4):
        loads.append(-jnp.sum(near[:, SLOT * q : SLOT * (q + 1)], axis=1, keepdims=True))
    loads.append(jnp.zeros((LANES - 5 * CORNERS, 1), jnp.float32))
    column = jnp.concatenate(loads, axis=0)
    return jnp.dot(rt_ref[0:nrows, :], column * l_ref[...], precision=HIGHEST)


def apply_schur(tile, map_tile, map_row, mask_row, schur_ref, modes_ref, near_ref, rt_ref, l_ref, out_ref, nrows, ncols):
    y_row = apply_matrix(tile, map_tile, map_row, schur_ref)
    load = coarse_load(0.25 * mask_row * y_row, modes_ref, near_ref, rt_ref, l_ref, nrows)
    y = as_tile(y_row)
    gamma = jnp.broadcast_to(0.25 * total(tile * y), (1, LANES))
    here = lax.axis_index("sy")
    rest = jnp.zeros((3, LANES), jnp.float32)
    for j in range(ncols):
        edge = jnp.where(here + 1 == j, y[0:2], jnp.where(here - 1 == j, y[4:6], 0.0))
        out_ref[j, 0:TILE, :] = jnp.concatenate([load[2 * j : 2 * j + 2], edge, gamma, rest], axis=0)
    return y


def pack_kernel(links_ref, modes_ref, map_ref, gap_ref, cmap_ref, out_modes, to_east, to_south, to_west, to_north):
    nrows, ncols = lax.axis_size("sx"), lax.axis_size("sy")
    modes = jnp.concatenate([modes_ref[...], jnp.zeros((8, modes_ref.shape[1]), jnp.float32)], axis=0)
    first = modes.astype(jnp.bfloat16)
    left = modes - first.astype(jnp.float32)
    second = left.astype(jnp.bfloat16)
    third = (left - second.astype(jnp.float32)).astype(jnp.bfloat16)
    map_row = map_ref[...]
    acc = jnp.zeros((CORNERS + 8, TILE * LANES), jnp.float32)
    for b in range(modes_ref.shape[1] // LANES):
        cols = slice(b * LANES, (b + 1) * LANES)
        index = iota((LANES, TILE * LANES), 0) + b * LANES
        hit = jnp.where(map_row == index, 1.0, 0.0).astype(jnp.bfloat16)
        for part in (first, second, third):
            acc = acc + jnp.dot(part[:, cols], hit, preferred_element_type=jnp.float32)
    acc = acc[0:CORNERS]
    out_modes[...] = acc
    east = ((lax.axis_index("sy") < ncols - 1) & (links_ref[0, 0] == 1)).astype(jnp.float32)
    south = ((lax.axis_index("sx") < nrows - 1) & (links_ref[0, 1] == 1)).astype(jnp.float32)
    gap = gap_ref[...]
    cmap = jnp.concatenate([cmap_ref[...], jnp.zeros((1, LANES), jnp.float32)], axis=1)
    rest = jnp.zeros((5, SLOT), jnp.float32)
    none = jnp.zeros((1, SLOT), jnp.float32)
    for q, ref in enumerate((to_east, to_south, to_west, to_north)):
        ref[0:CORNERS, :] = acc[:, SLOT * q : SLOT * (q + 1)]
        if q < 2:
            scale = (east, south)[q]
            values = jnp.concatenate([gap[2 * q : 2 * q + 1], gap[2 * q + 1 : 2 * q + 2]], axis=1) * scale
            mask = jnp.full((1, SLOT), 1.0, jnp.float32) * scale
        else:
            values, mask = none, none
        ref[CORNERS : CORNERS + 8, :] = jnp.concatenate([values, mask, cmap, rest], axis=0)


def start_kernel(
    own_east, own_south, from_east, from_south, from_west, from_north, cmap_ref, map_ref, map_tile_ref, schur_ref, modes_ref,
    blocks_ref, out_ref, state, near, r_ref, rt_ref, l_ref, mask_row_ref,
):
    nrows, ncols = lax.axis_size("sx"), lax.axis_size("sy")
    block = CORNERS // 4 * ncols
    row, cm = CORNERS, CORNERS + 2
    sources = (from_east, from_south, from_west, from_north)
    for q, ref in enumerate(sources):
        near[:, SLOT * q : SLOT * (q + 1)] = ref[0:CORNERS, :]
    values = [own_east[row : row + 1], own_south[row : row + 1], -from_west[row : row + 1], -from_north[row : row + 1]]
    masks = [ref[row + 1 : row + 2] for ref in (own_east, own_south, from_west, from_north)]
    residual = as_tile(jnp.concatenate(values, axis=1))
    mask_row = jnp.concatenate(masks, axis=1)
    mask_row_ref[...] = mask_row
    maps = [cmap_ref[...]] + [ref[cm : cm + 1, 0:LANES] for ref in sources]
    columns = jnp.transpose(jnp.concatenate(maps + [jnp.zeros((3, LANES), jnp.float32)], axis=0))
    column = [columns[0:CORNERS, g : g + 1] for g in range(5)]
    column.append(jnp.full((LANES - 5 * CORNERS, 1), float(block * nrows), jnp.float32))
    column = jnp.concatenate(column, axis=0)
    group = jnp.floor((column + 0.5) * (1.0 / block))
    inside = column - group * block
    lanes = iota((LANES, LANES), 1).astype(jnp.float32)
    hit_row = jnp.where((group == lanes) & (lanes < nrows), 1.0, 0.0)
    r_ref[...] = hit_row
    rt_ref[...] = jnp.transpose(hit_row)
    l_ref[...] = jnp.where(inside == lanes, 1.0, 0.0)
    y = apply_schur(
        residual, map_tile_ref[...], map_ref[...], mask_row, schur_ref, modes_ref, near, rt_ref, l_ref, out_ref, nrows, ncols
    )
    for j in range(ncols):
        out_ref[j, TILE : 3 * TILE, :] = blocks_ref[j]
    state[...] = jnp.zeros(state.shape, jnp.float32)
    state[RES : RES + TILE, :] = residual
    state[IFACE : IFACE + TILE, :] = y
    state[MASK : MASK + TILE, :] = as_tile(mask_row)


def rows_kernel(arrived, state_in, out_ref, state):
    nrows, ncols = lax.axis_size("sx"), lax.axis_size("sy")
    here, above = lax.axis_index("sy"), lax.axis_index("sx")
    summed = arrived[0, 0:TILE, :]
    for j in range(1, ncols):
        summed = summed + arrived[j, 0:TILE, :]
    west = arrived[jnp.maximum(here - 1, 0), 2:4, :]
    east = arrived[jnp.minimum(here + 1, ncols - 1), 2:4, :]
    state[...] = state_in[...]
    none = jnp.zeros((2, LANES), jnp.float32)
    state[PARTNER : PARTNER + TILE, :] = jnp.concatenate([east, none, west, none], axis=0)
    y = state_in[IFACE : IFACE + TILE, :]
    for i in range(nrows):
        edge = jnp.where(above + 1 == i, y[2:4], jnp.where(above - 1 == i, y[6:8], 0.0))
        out_ref[i, :, :] = jnp.concatenate([summed[0:2], edge, summed[4:8]], axis=0)


def direction_kernel(step, arrived, state_in, map_ref, map_tile_ref, kinv_ref, blocks_ref, out_ref, state):
    nrows, ncols = lax.axis_size("sx"), lax.axis_size("sy")
    here, above = lax.axis_index("sy"), lax.axis_index("sx")
    summed = arrived[0]
    for i in range(1, nrows):
        summed = summed + arrived[i]
    north = arrived[jnp.maximum(above - 1, 0), 2:4, :]
    south = arrived[jnp.minimum(above + 1, nrows - 1), 2:4, :]
    partner = state_in[PARTNER : PARTNER + TILE, :]
    partner = jnp.concatenate([partner[0:2], south, partner[4:6], north], axis=0)
    direction = 0.25 * state_in[MASK : MASK + TILE, :] * (state_in[IFACE : IFACE + TILE, :] - partner)
    load = summed[0:2]
    gamma = summed[4:5]
    if step:
        beta = gamma / state_in[GAMMA : GAMMA + 1, :]
        direction = direction + beta * state_in[DIR : DIR + TILE, :]
        load = load + beta * state_in[LOAD : LOAD + 2, :]
    inner = as_tile(apply_matrix(direction, map_tile_ref[...], map_ref[...], kinv_ref))
    energy = jnp.broadcast_to(total(direction * inner), (1, LANES))
    ndof = CORNERS // 4
    solved = jnp.zeros((2 * TILE, LANES), jnp.float32)
    pattern = jnp.concatenate([load] * TILE, axis=0)
    lanes = iota((2 * TILE, LANES), 1)
    halves = iota((2 * TILE, LANES), 0) // 2
    valid = iota((2 * TILE, LANES), 0) < 2 * ndof
    for j in range(ncols):
        column = jnp.sum(blocks_ref[j, TILE : 3 * TILE, :] * pattern, axis=1, keepdims=True)
        solved = solved + jnp.where((lanes == halves + j * ndof) & valid, column, 0.0)
    solved = jnp.sum(solved, axis=0, keepdims=True)
    rest = jnp.zeros((2, LANES), jnp.float32)
    for j in range(ncols):
        edge = jnp.where(here + 1 == j, inner[0:2], jnp.where(here - 1 == j, inner[4:6], 0.0))
        out_ref[j, :, :] = jnp.concatenate([solved, load, edge, energy, rest], axis=0)
    state[...] = state_in[...]
    state[DIR : DIR + TILE, :] = direction
    state[IFACE : IFACE + TILE, :] = inner
    state[SCAL : SCAL + TILE, :] = jnp.concatenate([gamma, load, jnp.zeros((5, LANES), jnp.float32)], axis=0)


def solve_kernel(arrived, state_in, out_ref, state, whole_load):
    nrows, ncols = lax.axis_size("sx"), lax.axis_size("sy")
    here, above = lax.axis_index("sy"), lax.axis_index("sx")
    summed = arrived[0]
    for j in range(1, ncols):
        summed = summed + arrived[j]
    whole_load[...] = jnp.concatenate([arrived[j, 1:3, :] for j in range(ncols)], axis=0)
    west = arrived[jnp.maximum(here - 1, 0), 3:5, :]
    east = arrived[jnp.minimum(here + 1, ncols - 1), 3:5, :]
    state[...] = state_in[...]
    none = jnp.zeros((2, LANES), jnp.float32)
    state[PARTNER : PARTNER + TILE, :] = jnp.concatenate([east, none, west, none], axis=0)
    inner = state_in[IFACE : IFACE + TILE, :]
    rest = jnp.zeros((4, LANES), jnp.float32)
    for i in range(nrows):
        edge = jnp.where(above + 1 == i, inner[2:4], jnp.where(above - 1 == i, inner[6:8], 0.0))
        out_ref[i, :, :] = jnp.concatenate([summed[0:1], edge, summed[5:6], rest], axis=0)


def advance(arrived, state_in, whole_load, modes_ref, near_ref, r_ref, l_ref):
    nrows = lax.axis_size("sx")
    above = lax.axis_index("sx")
    energy = arrived[0]
    for i in range(1, nrows):
        energy = energy + arrived[i]
    energy = energy[3:4]
    north = arrived[jnp.maximum(above - 1, 0), 1:3, :]
    south = arrived[jnp.minimum(above + 1, nrows - 1), 1:3, :]
    solved = jnp.concatenate([arrived[i, 0:1, :] for i in range(nrows)], axis=0)
    energy = energy + total(whole_load[...] * solved)
    alpha = state_in[GAMMA : GAMMA + 1, :] / energy
    found = jnp.dot(r_ref[:, 0:nrows], solved, precision=HIGHEST)
    corners = jnp.sum(found * l_ref[...], axis=1, keepdims=True)
    coarse = jnp.sum(corners[0:CORNERS] * modes_ref[...], axis=0, keepdims=True)
    near = []
    for q in range(4):
        values = corners[CORNERS * (q + 1) : CORNERS * (q + 2)]
        near.append(jnp.sum(values * near_ref[:, SLOT * q : SLOT * (q + 1)], axis=0, keepdims=True))
    coarse = as_tile(coarse - jnp.concatenate(near, axis=1))
    partner = state_in[PARTNER : PARTNER + TILE, :]
    partner = jnp.concatenate([partner[0:2], south, partner[4:6], north], axis=0)
    image = state_in[MASK : MASK + TILE, :] * (state_in[IFACE : IFACE + TILE, :] - partner + coarse)
    multipliers = state_in[MUL : MUL + TILE, :] + alpha * state_in[DIR : DIR + TILE, :]
    residual = state_in[RES : RES + TILE, :] - alpha * image
    return multipliers, residual


def next_kernel(
    arrived, state_in, whole_load, modes_ref, near_ref, r_ref, rt_ref, l_ref, mask_row_ref, map_ref, map_tile_ref, schur_ref,
    out_ref, state,
):
    nrows, ncols = lax.axis_size("sx"), lax.axis_size("sy")
    multipliers, residual = advance(arrived, state_in, whole_load, modes_ref, near_ref, r_ref, l_ref)
    y = apply_schur(
        residual, map_tile_ref[...], map_ref[...], mask_row_ref[...], schur_ref, modes_ref, near_ref, rt_ref, l_ref, out_ref,
        nrows, ncols,
    )
    state[...] = state_in[...]
    state[RES : RES + TILE, :] = residual
    state[MUL : MUL + TILE, :] = multipliers
    state[IFACE : IFACE + TILE, :] = y


def last_kernel(arrived, state_in, whole_load, modes_ref, near_ref, r_ref, l_ref, out_multipliers, out_residual):
    multipliers, residual = advance(arrived, state_in, whole_load, modes_ref, near_ref, r_ref, l_ref)
    out_multipliers[...] = multipliers
    out_residual[...] = residual


def shifted(block, axis, distance):
    devices = range(lax.axis_size(axis))
    route = [(i - distance, i) for i in devices if i - distance in devices]
    return lax.ppermute(block, axis, route)


def on_device(gap, kinv, schur, corner_modes, coarse_inverse, edge_map, corner_map, links):
    nrows, ncols = lax.axis_size("sx"), lax.axis_size("sy")
    width = kinv.shape[-1]
    edge = width // 4
    ndof = coarse_inverse.shape[0]
    block = coarse_inverse.shape[1] // nrows
    kinv = kinv.reshape(width, width)
    schur = schur.reshape(width, width)
    modes = corner_modes.reshape(-1, width)
    map_pad = jnp.pad(edge_map.reshape(4, edge), ((0, 0), (0, SLOT - edge)), constant_values=-1)
    map_tile = map_pad.reshape(TILE, LANES)
    map_row = map_pad.reshape(1, TILE * LANES)
    gap_pad = jnp.pad(gap.reshape(2, edge), ((0, 0), (0, SLOT - edge))).reshape(4, LANES)
    cmap = jnp.pad(corner_map.reshape(1, -1).astype(jnp.float32), ((0, 0), (0, LANES - CORNERS)))
    blocks = coarse_inverse.reshape(ndof, ncols, 2, block).transpose(1, 0, 2, 3).reshape(ncols, 2 * ndof, block)
    blocks = jnp.pad(blocks, ((0, 0), (0, 2 * TILE - 2 * ndof), (0, LANES - block)))

    own_modes, east, south, west, north = call(
        pack_kernel,
        (links.reshape(1, 2), modes, map_row, gap_pad, cmap),
        [(CORNERS, TILE * LANES)] + [(CORNERS + 8, SLOT)] * 4,
        [SMEM] + [VMEM] * 4,
        name="pack",
    )
    from_west = shifted(east, "sy", 1)
    from_east = shifted(west, "sy", -1)
    from_north = shifted(south, "sx", 1)
    from_south = shifted(north, "sx", -1)
    square = (LANES, LANES)
    out, state, near, r, rt, l, mask_row = call(
        start_kernel,
        (
            east, south, from_east, from_south, from_west, from_north, cmap, map_row, map_tile, schur, own_modes, blocks,
        ),
        [
            (ncols, 3 * TILE, LANES), (NSTATE, LANES), (CORNERS, TILE * LANES), square, square, square, (1, TILE * LANES),
        ],
        name="start",
    )
    to_sy, to_sx = (ncols, TILE, LANES), (nrows, TILE, LANES)
    state_shape = (NSTATE, LANES)
    for step in range(ITERS):
        arrived = lax.all_to_all(out, "sy", 0, 0, tiled=True)
        if step == 0:
            solver = arrived
        out, state = call(rows_kernel, (arrived, state), [to_sx, state_shape], name="rows")
        arrived = lax.all_to_all(out, "sx", 0, 0, tiled=True)

        def kernel(*refs, step=step):
            direction_kernel(step, *refs)

        out, state = call(
            kernel, (arrived, state, map_row, map_tile, kinv, solver), [to_sy, state_shape], name="direction"
        )
        arrived = lax.all_to_all(out, "sy", 0, 0, tiled=True)
        out, state, load = call(
            solve_kernel, (arrived, state), [to_sx, state_shape, (nrows, LANES)], name="solve"
        )
        arrived = lax.all_to_all(out, "sx", 0, 0, tiled=True)
        common = (arrived, state, load, own_modes, near, r)
        if step + 1 < ITERS:
            out, state = call(
                next_kernel, common + (rt, l, mask_row, map_row, map_tile, schur), [to_sy, state_shape], name="next"
            )
        else:
            results = call(last_kernel, common + (l,), [(TILE, LANES)] * 2, name="last")
    return tuple(value.reshape(4, SLOT)[:2, :edge].reshape(gap.shape) for value in results)


def solution(mesh):
    placed = (
        P("sx", "sy", None),
        P("sx", "sy", None, None),
        P("sx", "sy", None, None),
        P("sx", "sy", None, None),
        P(("sx", "sy"), None),
        P("sx", "sy", None),
        P("sx", "sy", None),
        P("sx", "sy", None),
    )
    return jax.shard_map(
        on_device,
        mesh=mesh,
        in_specs=placed,
        out_specs=(P("sx", "sy", None), P("sx", "sy", None)),
        check_vma=False,
    )
```

```python
import jax
import jax.numpy as jnp
from jax import lax
from jax.experimental import pallas as pl
from jax.experimental.pallas import tpu as pltpu
from jax.sharding import Mesh
from jax.sharding import PartitionSpec as P

ITERS = 3
LANES = 128
SLOT = 256
TILE = 8
CORNERS = 24
NDOF = 6
HIGHEST = lax.Precision.HIGHEST
VMEM = pl.BlockSpec(memory_space=pltpu.VMEM)
ANY = pl.BlockSpec(memory_space=pl.ANY)
LIMIT = 40 * 1024 * 1024

ROWS_AXES = ("z", "xl")
PLANE = ("xl", "sy")

RES, MUL, DIR, IFACE, PARTNER, MASK, SCAL, NSTATE = 0, 8, 16, 24, 32, 40, 48, 56
GAMMA, LOAD = 48, 49


def call(kernel, inputs, outputs, in_specs=None, out_specs=None, scratch=(), name=None):
    shapes = [shape if hasattr(shape, "dtype") else jax.ShapeDtypeStruct(shape, jnp.float32) for shape in outputs]
    return pl.pallas_call(
        kernel,
        out_shape=shapes,
        in_specs=in_specs or [VMEM] * len(inputs),
        out_specs=out_specs or [VMEM] * len(outputs),
        scratch_shapes=list(scratch),
        compiler_params=pltpu.CompilerParams(vmem_limit_bytes=LIMIT),
        name=name,
    )(*inputs)


def iota(shape, dim):
    return lax.broadcasted_iota(jnp.int32, shape, dim)


def as_tile(row):
    return jnp.concatenate([row[:, LANES * c : LANES * (c + 1)] for c in range(TILE)], axis=0)


def total(value):
    return jnp.sum(jnp.sum(value, axis=1, keepdims=True), axis=0, keepdims=True)


def slots(row, count, fill):
    width = row.shape[1]
    wide = jnp.broadcast_to(row, (TILE, width))
    lanes = iota((1, SLOT), 1)
    edge = SLOT * 3 // 4
    pieces = []
    for q in range(count):
        moved = wide if q == 0 else pltpu.roll(wide, width - edge * q, 1)
        pieces.append(jnp.where(lanes < edge, moved[0:1, 0:SLOT], fill))
    return pieces


def apply_matrix(tile, map_tile, map_row, matrix_ref):
    width = matrix_ref.shape[0]
    values = jnp.transpose(tile)
    places = jnp.transpose(map_tile)
    lanes = iota((LANES, LANES), 1)
    pieces = []
    for t in range(width // LANES):
        acc = jnp.zeros((LANES, LANES), jnp.float32)
        for c in range(TILE):
            hit = places[:, c : c + 1] == lanes + t * LANES
            acc = acc + jnp.where(hit, values[:, c : c + 1], 0.0)
        pieces.append(jnp.sum(acc, axis=0, keepdims=True))
    out = jnp.zeros((TILE, TILE * LANES), jnp.float32)
    for b in range(width // LANES):
        rows = slice(b * LANES, (b + 1) * LANES)
        acc = matrix_ref[rows, 0:LANES] * pieces[0]
        for t in range(1, width // LANES):
            acc = acc + matrix_ref[rows, t * LANES : (t + 1) * LANES] * pieces[t]
        column = jnp.sum(acc, axis=1, keepdims=True)
        for s in range(LANES // TILE):
            index = iota((TILE, TILE * LANES), 0) + (b * LANES + s * TILE)
            out = out + jnp.where(map_row == index, column[s * TILE : (s + 1) * TILE, :], 0.0)
    return jnp.sum(out, axis=0, keepdims=True)


def coarse_load(weighted, modes_ref, near_ref, rt_ref, l_ref, chunks):
    own = jnp.sum(modes_ref[...] * weighted, axis=1, keepdims=True)
    near = near_ref[...] * weighted
    loads = [own]
    for q in range(4):
        loads.append(-jnp.sum(near[:, SLOT * q : SLOT * (q + 1)], axis=1, keepdims=True))
    loads.append(jnp.zeros((LANES - 5 * CORNERS, 1), jnp.float32))
    column = jnp.concatenate(loads, axis=0)
    return jnp.dot(rt_ref[0:chunks, :], column * l_ref[...], precision=HIGHEST)


def plane_edges(tile, target, ncols):
    pair, col = target // ncols, target % ncols
    same = lax.axis_index("xl") == pair
    here = lax.axis_index("sy")
    first = jnp.where(
        same,
        jnp.where(here + 1 == col, tile[0:2], jnp.where(here - 1 == col, tile[4:6], 0.0)),
        jnp.where(here == col, tile[2:4], 0.0),
    )
    second = jnp.where(same, 0.0, jnp.where(here == col, tile[6:8], 0.0))
    return first, second


def plane_arrivals(arrived, row, ncols):
    pair, here = lax.axis_index("xl"), lax.axis_index("sy")
    base = pair * ncols
    east = arrived[base + jnp.minimum(here + 1, ncols - 1), row : row + 2, :]
    west = arrived[base + jnp.maximum(here - 1, 0), row : row + 2, :]
    other = (1 - pair) * ncols + here
    their_south = arrived[other, row : row + 2, :]
    their_north = arrived[other, row + 2 : row + 4, :]
    south = jnp.where(pair == 0, their_north, 0.0)
    north = jnp.where(pair == 0, 0.0, their_south)
    forward = jnp.where(pair == 0, their_south, their_north)
    return jnp.concatenate([east, south, west, north], axis=0), forward


def z_edge(forward, target):
    goal = jnp.where(lax.axis_index("xl") == 0, lax.axis_index("z") + 1, lax.axis_index("z") - 1)
    return jnp.where(goal == target, forward, 0.0)


def z_arrival(arrived, row, partner):
    levels = arrived.shape[0]
    pair, level = lax.axis_index("xl"), lax.axis_index("z")
    source = jnp.where(pair == 0, jnp.maximum(level - 1, 0), jnp.minimum(level + 1, levels - 1))
    edge = arrived[source, row : row + 2, :]
    south = jnp.where(pair == 0, partner[2:4], edge)
    north = jnp.where(pair == 0, edge, partner[6:8])
    return jnp.concatenate([partner[0:2], south, partner[4:6], north], axis=0)


def apply_schur(tile, map_tile, map_row, mask_row, schur_ref, modes_ref, near_ref, rt_ref, l_ref, out_ref):
    chunks = out_ref.shape[0]
    y_row = apply_matrix(tile, map_tile, map_row, schur_ref)
    load = coarse_load(0.25 * mask_row * y_row, modes_ref, near_ref, rt_ref, l_ref, chunks)
    y = as_tile(y_row)
    gamma = jnp.broadcast_to(0.25 * total(tile * y), (1, LANES))
    rest = jnp.zeros((2, LANES), jnp.float32)
    for p in range(chunks):
        first, second = plane_edges(y, p, chunks // 2)
        out_ref[p, 0:TILE, :] = jnp.concatenate([load[p : p + 1], gamma, first, second, rest], axis=0)
    return y


def pack_kernel(
    links_hbm, modes_hbm, map_hbm, gap_hbm, cmap_hbm, out_modes, to_east, to_south, to_west, to_north, out_row, out_tile,
    out_cmap, links_ref, modes_ref, map_ref, gap_ref, cmap_ref, sems,
):
    copies = [
        pltpu.make_async_copy(source, target, sems.at[k])
        for k, (source, target) in enumerate(
            (
                (modes_hbm, modes_ref), (map_hbm, map_ref), (gap_hbm, gap_ref), (cmap_hbm, cmap_ref),
                (links_hbm, links_ref),
            )
        )
    ]
    for copy in copies:
        copy.start()
    for copy in copies:
        copy.wait()
    nrows, ncols = lax.axis_size("z") * lax.axis_size("xl"), lax.axis_size("sy")
    row_here = lax.axis_index("z") * lax.axis_size("xl") + lax.axis_index("xl")
    map_row = jnp.concatenate(slots(map_ref[0], 4, -1), axis=1)
    out_row[...] = map_row
    out_tile[...] = as_tile(map_row)
    width = modes_ref.shape[3]
    modes = jnp.concatenate([modes_ref[0, 0], jnp.zeros((8, width), jnp.float32)], axis=0)
    first = modes.astype(jnp.bfloat16)
    left = modes - first.astype(jnp.float32)
    second = left.astype(jnp.bfloat16)
    third = (left - second.astype(jnp.float32)).astype(jnp.bfloat16)
    acc = jnp.zeros((CORNERS + 8, TILE * LANES), jnp.float32)
    for b in range(width // LANES):
        cols = slice(b * LANES, (b + 1) * LANES)
        index = iota((LANES, TILE * LANES), 0) + b * LANES
        hit = jnp.where(map_row == index, 1.0, 0.0).astype(jnp.bfloat16)
        for part in (first, second, third):
            acc = acc + jnp.dot(part[:, cols], hit, preferred_element_type=jnp.float32)
    acc = acc[0:CORNERS]
    out_modes[...] = acc
    links = jnp.where(links_ref[0] == 1, 1.0, 0.0)
    east = jnp.where(lax.axis_index("sy") < ncols - 1, links[:, 0:1], 0.0)
    south = jnp.where(row_here < nrows - 1, links[:, 1:2], 0.0)
    gaps = slots(gap_ref[0], 2, 0.0)
    out_cmap[...] = jnp.zeros(out_cmap.shape, jnp.float32)
    out_cmap[0:1, 0:CORNERS] = cmap_ref[0].astype(jnp.float32)
    cmap = out_cmap[...]
    rest = jnp.zeros((5, SLOT), jnp.float32)
    none = jnp.zeros((1, SLOT), jnp.float32)
    for q, ref in enumerate((to_east, to_south, to_west, to_north)):
        ref[0:CORNERS, :] = acc[:, SLOT * q : SLOT * (q + 1)]
        values, mask = none, none
        if q < 2:
            mask = none + (east, south)[q]
            values = gaps[q] * mask
        ref[CORNERS : CORNERS + 8, :] = jnp.concatenate([values, mask, cmap, rest], axis=0)


def load_kernel(schur_hbm, coarse_hbm, schur_out, blocks_out, coarse_ref, sems):
    matrix = pltpu.make_async_copy(schur_hbm.at[0, 0], schur_out, sems.at[0])
    coarse = pltpu.make_async_copy(coarse_hbm, coarse_ref, sems.at[1])
    coarse.start()
    matrix.start()
    coarse.wait()
    chunks = blocks_out.shape[0]
    ncoarse = coarse_ref.shape[1]
    block = ncoarse // chunks
    padded = -(-ncoarse // LANES) * LANES
    values = coarse_ref[...]
    if padded > ncoarse:
        values = jnp.pad(values, ((0, 0), (0, padded - ncoarse)))
    values = jnp.concatenate([values, jnp.zeros((TILE - NDOF, padded), jnp.float32)], axis=0)
    values = jnp.concatenate([values, jnp.zeros((TILE, LANES), jnp.float32)], axis=1)
    lanes = iota((TILE, LANES), 1)
    for p in range(chunks):
        start = block * p // LANES * LANES
        window = values[:, start : start + SLOT]
        shift = block * p - start
        if shift:
            window = pltpu.roll(window, SLOT - shift, 1)
        blocks_out[p] = jnp.where(lanes < block, window[:, 0:LANES], 0.0)
    matrix.wait()


def start_kernel(
    own_east, own_south, from_east, from_south, from_west, from_north, cmap_ref, map_ref, map_tile_ref, schur_ref, modes_ref,
    blocks_ref, out_ref, state, near, r_ref, rt_ref, l_ref, mask_row_ref,
):
    chunks = out_ref.shape[0]
    block = NDOF * chunks // 2
    row, cm = CORNERS, CORNERS + 2
    sources = (from_east, from_south, from_west, from_north)
    for q, ref in enumerate(sources):
        near[:, SLOT * q : SLOT * (q + 1)] = ref[0:CORNERS, :]
    values = [own_east[row : row + 1], own_south[row : row + 1], -from_west[row : row + 1], -from_north[row : row + 1]]
    masks = [ref[row + 1 : row + 2] for ref in (own_east, own_south, from_west, from_north)]
    residual = as_tile(jnp.concatenate(values, axis=1))
    mask_row = jnp.concatenate(masks, axis=1)
    mask_row_ref[...] = mask_row
    maps = [cmap_ref[:, 0:LANES]] + [ref[cm : cm + 1, 0:LANES] for ref in sources]
    columns = jnp.transpose(jnp.concatenate(maps + [jnp.zeros((3, LANES), jnp.float32)], axis=0))
    column = [columns[0:CORNERS, g : g + 1] for g in range(5)]
    column.append(jnp.full((LANES - 5 * CORNERS, 1), float(block * chunks), jnp.float32))
    column = jnp.concatenate(column, axis=0)
    group = jnp.floor((column + 0.5) * (1.0 / block))
    inside = column - group * block
    lanes = iota((LANES, LANES), 1).astype(jnp.float32)
    hit_row = jnp.where((group == lanes) & (lanes < chunks), 1.0, 0.0)
    r_ref[...] = hit_row
    rt_ref[...] = jnp.transpose(hit_row)
    l_ref[...] = jnp.where(inside == lanes, 1.0, 0.0)
    y = apply_schur(residual, map_tile_ref[...], map_ref[...], mask_row, schur_ref, modes_ref, near, rt_ref, l_ref, out_ref)
    for p in range(chunks):
        out_ref[p, TILE : 2 * TILE, :] = blocks_ref[p]
    state[...] = jnp.zeros(state.shape, jnp.float32)
    state[RES : RES + TILE, :] = residual
    state[IFACE : IFACE + TILE, :] = y
    state[MASK : MASK + TILE, :] = as_tile(mask_row)


def rows_kernel(arrived, state_in, out_ref, state):
    chunks, levels = arrived.shape[0], out_ref.shape[0]
    summed = arrived[0, 0:TILE, :]
    for p in range(1, chunks):
        summed = summed + arrived[p, 0:TILE, :]
    partner, forward = plane_arrivals(arrived, 2, chunks // 2)
    state[...] = state_in[...]
    state[PARTNER : PARTNER + TILE, :] = partner
    for level in range(levels):
        out_ref[level] = jnp.concatenate([summed[0:2], z_edge(forward, level)], axis=0)


def direction_kernel(step, arrived, state_in, map_ref, map_tile_ref, kinv_ref, blocks_ref, out_ref, state):
    chunks, levels = out_ref.shape[0], arrived.shape[0]
    half = chunks // 2
    summed = arrived[0]
    for level in range(1, levels):
        summed = summed + arrived[level]
    partner = z_arrival(arrived, 2, state_in[PARTNER : PARTNER + TILE, :])
    direction = 0.25 * state_in[MASK : MASK + TILE, :] * (state_in[IFACE : IFACE + TILE, :] - partner)
    load = summed[0:1]
    gamma = summed[1:2]
    if step:
        beta = gamma / state_in[GAMMA : GAMMA + 1, :]
        direction = direction + beta * state_in[DIR : DIR + TILE, :]
        load = load + beta * state_in[LOAD : LOAD + 1, :]
    inner = as_tile(apply_matrix(direction, map_tile_ref[...], map_ref[...], kinv_ref))
    energy = jnp.broadcast_to(total(direction * inner), (1, LANES))
    lanes = iota((TILE, LANES), 1)
    dof = iota((TILE, LANES), 0)
    solved = []
    for a in range(2):
        acc = jnp.zeros((TILE, LANES), jnp.float32)
        for p in range(half):
            column = jnp.sum(blocks_ref[a * half + p, TILE : 2 * TILE, :] * load, axis=1, keepdims=True)
            acc = acc + jnp.where((lanes == dof + p * NDOF) & (dof < NDOF), column, 0.0)
        solved.append(jnp.sum(acc, axis=0, keepdims=True))
    for p in range(chunks):
        first, second = plane_edges(inner, p, half)
        out_ref[p] = jnp.concatenate(solved + [load, energy, first, second], axis=0)
    state[...] = state_in[...]
    state[DIR : DIR + TILE, :] = direction
    state[IFACE : IFACE + TILE, :] = inner
    state[SCAL : SCAL + TILE, :] = jnp.concatenate([gamma, load, jnp.zeros((6, LANES), jnp.float32)], axis=0)


def solve_kernel(arrived, state_in, out_ref, state, whole_load):
    chunks, levels = arrived.shape[0], out_ref.shape[0]
    block = NDOF * chunks // 2
    summed = arrived[0]
    for p in range(1, chunks):
        summed = summed + arrived[p]
    whole_load[...] = jnp.concatenate([arrived[p, 2:3, :] for p in range(chunks)], axis=0)
    partner, forward = plane_arrivals(arrived, 4, chunks // 2)
    state[...] = state_in[...]
    state[PARTNER : PARTNER + TILE, :] = partner
    first = jnp.where(iota((1, LANES), 1) < block, summed[0:1], summed[3:4])
    for level in range(levels):
        out_ref[level] = jnp.concatenate([first, summed[1:2], z_edge(forward, level)], axis=0)


def advance(arrived, state_in, whole_load, modes_ref, near_ref, r_ref, l_ref):
    levels = arrived.shape[0]
    energy = arrived[0, 0:1, :]
    for level in range(1, levels):
        energy = energy + arrived[level, 0:1, :]
    partner = z_arrival(arrived, 2, state_in[PARTNER : PARTNER + TILE, :])
    solved = jnp.concatenate([arrived[level, 0:2, :] for level in range(levels)], axis=0)
    energy = energy[:, LANES - 1 : LANES] + total(whole_load[...] * solved)
    alpha = state_in[GAMMA : GAMMA + 1, :] / energy
    found = jnp.dot(r_ref[:, 0 : 2 * levels], solved, precision=HIGHEST)
    corners = jnp.sum(found * l_ref[...], axis=1, keepdims=True)
    coarse = jnp.sum(corners[0:CORNERS] * modes_ref[...], axis=0, keepdims=True)
    near = []
    for q in range(4):
        values = corners[CORNERS * (q + 1) : CORNERS * (q + 2)]
        near.append(jnp.sum(values * near_ref[:, SLOT * q : SLOT * (q + 1)], axis=0, keepdims=True))
    coarse = as_tile(coarse - jnp.concatenate(near, axis=1))
    image = state_in[MASK : MASK + TILE, :] * (state_in[IFACE : IFACE + TILE, :] - partner + coarse)
    multipliers = state_in[MUL : MUL + TILE, :] + alpha * state_in[DIR : DIR + TILE, :]
    residual = state_in[RES : RES + TILE, :] - alpha * image
    return multipliers, residual


def next_kernel(
    arrived, state_in, whole_load, modes_ref, near_ref, r_ref, l_ref, rt_ref, mask_row_ref, map_ref, map_tile_ref, schur_ref,
    out_ref, state,
):
    multipliers, residual = advance(arrived, state_in, whole_load, modes_ref, near_ref, r_ref, l_ref)
    y = apply_schur(
        residual, map_tile_ref[...], map_ref[...], mask_row_ref[...], schur_ref, modes_ref, near_ref, rt_ref, l_ref, out_ref
    )
    state[...] = state_in[...]
    state[RES : RES + TILE, :] = residual
    state[MUL : MUL + TILE, :] = multipliers
    state[IFACE : IFACE + TILE, :] = y


def last_kernel(
    arrived, state_in, whole_load, modes_ref, near_ref, r_ref, l_ref, out_multipliers, out_residual, scratch, sems
):
    results = advance(arrived, state_in, whole_load, modes_ref, near_ref, r_ref, l_ref)
    width = scratch.shape[3]
    none = jnp.zeros((1, width - SLOT), jnp.float32)
    lanes = iota((1, width), 1)
    copies = []
    for k, (tile, target) in enumerate(zip(results, (out_multipliers, out_residual))):
        east = jnp.concatenate([tile[0:1], tile[1:2], none], axis=1)
        south = jnp.concatenate([tile[2:3], tile[3:4], none], axis=1)
        south = pltpu.roll(jnp.broadcast_to(south, (TILE, width)), width // 2, 1)[0:1]
        scratch[k, 0] = jnp.where(lanes < width // 2, east, south)
        copies.append(pltpu.make_async_copy(scratch.at[k], target, sems.at[k]))
        copies[k].start()
    for copy in copies:
        copy.wait()


def shifted(block, axis, distance):
    devices = range(lax.axis_size(axis))
    route = [(i - distance, i) for i in devices if i - distance in devices]
    return lax.ppermute(block, axis, route)


def on_device(gap, kinv, schur, corner_modes, coarse_inverse, edge_map, corner_map, links):
    levels, chunks = lax.axis_size("z"), lax.axis_size("xl") * lax.axis_size("sy")
    width = kinv.shape[-1]
    kinv = kinv.reshape(width, width)
    ints = jnp.int32
    own_modes, east, south, west, north, map_row, map_tile, cmap = call(
        pack_kernel,
        (links, corner_modes, edge_map, gap, corner_map),
        [(CORNERS, TILE * LANES)]
        + [(CORNERS + 8, SLOT)] * 4
        + [jax.ShapeDtypeStruct((1, TILE * LANES), ints), jax.ShapeDtypeStruct((TILE, LANES), ints), (1, SLOT)],
        in_specs=[ANY] * 5,
        scratch=[
            pltpu.VMEM(links.shape, ints),
            pltpu.VMEM(corner_modes.shape, jnp.float32),
            pltpu.VMEM(edge_map.shape, ints),
            pltpu.VMEM(gap.shape, jnp.float32),
            pltpu.VMEM(corner_map.shape, ints),
            pltpu.SemaphoreType.DMA((5,)),
        ],
        name="pack",
    )
    from_west = shifted(east, "sy", 1)
    from_east = shifted(west, "sy", -1)
    from_north = shifted(south, ROWS_AXES, 1)
    from_south = shifted(north, ROWS_AXES, -1)
    schur, blocks = call(
        load_kernel,
        (schur, coarse_inverse),
        [(width, width), (chunks, TILE, LANES)],
        in_specs=[ANY] * 2,
        scratch=[pltpu.VMEM(coarse_inverse.shape, jnp.float32), pltpu.SemaphoreType.DMA((2,))],
        name="load",
    )
    square = (LANES, LANES)
    state_shape = (NSTATE, LANES)
    out, state, near, r, rt, l, mask_row = call(
        start_kernel,
        (
            east, south, from_east, from_south, from_west, from_north, cmap, map_row, map_tile, schur, own_modes, blocks,
        ),
        [(chunks, 2 * TILE, LANES), state_shape, (CORNERS, TILE * LANES), square, square, square, (1, TILE * LANES)],
        name="start",
    )
    to_plane, to_z = (chunks, TILE, LANES), (levels, 4, LANES)
    for step in range(ITERS):
        arrived = lax.all_to_all(out, PLANE, 0, 0, tiled=True)
        if step == 0:
            solver = arrived
        out, state = call(rows_kernel, (arrived, state), [to_z, state_shape], name="rows")
        arrived = lax.all_to_all(out, "z", 0, 0, tiled=True)

        def kernel(*refs, step=step):
            direction_kernel(step, *refs)

        out, state = call(
            kernel, (arrived, state, map_row, map_tile, kinv, solver), [to_plane, state_shape], name="direction"
        )
        arrived = lax.all_to_all(out, PLANE, 0, 0, tiled=True)
        out, state, load = call(solve_kernel, (arrived, state), [to_z, state_shape, (chunks, LANES)], name="solve")
        arrived = lax.all_to_all(out, "z", 0, 0, tiled=True)
        common = (arrived, state, load, own_modes, near, r, l)
        if step + 1 < ITERS:
            out, state = call(
                next_kernel, common + (rt, mask_row, map_row, map_tile, schur), [to_plane, state_shape], name="next"
            )
    return tuple(
        call(
            last_kernel,
            common,
            [gap.shape] * 2,
            out_specs=[ANY] * 2,
            scratch=[pltpu.VMEM((2,) + gap.shape[:2] + gap.shape[2:], jnp.float32), pltpu.SemaphoreType.DMA((2,))],
            name="last",
        )
    )


def solution(mesh):
    rows, cols = mesh.devices.shape
    split = Mesh(mesh.devices.reshape(rows // 2, 2, cols), ("z", "xl", "sy"))
    placed = (
        P(ROWS_AXES, "sy", None),
        P(ROWS_AXES, "sy", None, None),
        P(ROWS_AXES, "sy", None, None),
        P(ROWS_AXES, "sy", None, None),
        P(("z", "xl", "sy"), None),
        P(ROWS_AXES, "sy", None),
        P(ROWS_AXES, "sy", None),
        P(ROWS_AXES, "sy", None),
    )
    return jax.shard_map(
        on_device,
        mesh=split,
        in_specs=placed,
        out_specs=(P(ROWS_AXES, "sy", None), P(ROWS_AXES, "sy", None)),
        check_vma=False,
    )
```

```python
import jax
import jax.numpy as jnp
from jax import lax
from jax.experimental import pallas as pl
from jax.experimental.pallas import tpu as pltpu
from jax.sharding import Mesh
from jax.sharding import PartitionSpec as P

ITERS = 3
LANES = 128
SLOT = 256
TILE = 8
CORNERS = 24
NDOF = 6
HIGHEST = lax.Precision.HIGHEST
VMEM = pl.BlockSpec(memory_space=pltpu.VMEM)
HBM = pl.BlockSpec(memory_space=pl.ANY)
LIMIT = 40 * 1024 * 1024

ROWS_AXES = ("z", "xl")
PLANE = ("xl", "sy")

RES, MUL, DIR, IFACE, PARTNER, MASK, SCAL, NSTATE = 0, 8, 16, 24, 32, 40, 48, 56
GAMMA, LOAD = 48, 49


def call(kernel, inputs, outputs, in_specs=None, out_specs=None, scratch=(), name=None):
    shapes = [shape if hasattr(shape, "dtype") else jax.ShapeDtypeStruct(shape, jnp.float32) for shape in outputs]
    return pl.pallas_call(
        kernel,
        out_shape=shapes,
        in_specs=in_specs or [VMEM] * len(inputs),
        out_specs=out_specs or [VMEM] * len(outputs),
        scratch_shapes=list(scratch),
        compiler_params=pltpu.CompilerParams(vmem_limit_bytes=LIMIT),
        name=name,
    )(*inputs)


def in_hbm(*arrays):
    return tuple(pltpu.with_memory_space_constraint(array, pltpu.HBM) for array in arrays)


def iota(shape, dim):
    return lax.broadcasted_iota(jnp.int32, shape, dim)


def as_tile(row):
    return jnp.concatenate([row[:, LANES * c : LANES * (c + 1)] for c in range(TILE)], axis=0)


def total(value):
    return jnp.sum(jnp.sum(value, axis=1, keepdims=True), axis=0, keepdims=True)


def slots(row, count, fill):
    width = row.shape[1]
    wide = jnp.broadcast_to(row, (TILE, width))
    lanes = iota((1, SLOT), 1)
    edge = SLOT * 3 // 4
    pieces = []
    for q in range(count):
        moved = wide if q == 0 else pltpu.roll(wide, width - edge * q, 1)
        pieces.append(jnp.where(lanes < edge, moved[0:1, 0:SLOT], fill))
    return pieces


def apply_matrix(tile, map_tile, map_row, matrix_ref):
    width = matrix_ref.shape[0]
    values = jnp.transpose(tile)
    places = jnp.transpose(map_tile)
    lanes = iota((LANES, LANES), 1)
    pieces = []
    for t in range(width // LANES):
        acc = jnp.zeros((LANES, LANES), jnp.float32)
        for c in range(TILE):
            hit = places[:, c : c + 1] == lanes + t * LANES
            acc = acc + jnp.where(hit, values[:, c : c + 1], 0.0)
        pieces.append(jnp.sum(acc, axis=0, keepdims=True))
    out = jnp.zeros((TILE, TILE * LANES), jnp.float32)
    for b in range(width // LANES):
        rows = slice(b * LANES, (b + 1) * LANES)
        acc = matrix_ref[rows, 0:LANES] * pieces[0]
        for t in range(1, width // LANES):
            acc = acc + matrix_ref[rows, t * LANES : (t + 1) * LANES] * pieces[t]
        column = jnp.sum(acc, axis=1, keepdims=True)
        for s in range(LANES // TILE):
            index = iota((TILE, TILE * LANES), 0) + (b * LANES + s * TILE)
            out = out + jnp.where(map_row == index, column[s * TILE : (s + 1) * TILE, :], 0.0)
    return jnp.sum(out, axis=0, keepdims=True)


def coarse_load(weighted, modes_ref, near_ref, rt_ref, l_ref, chunks):
    own = jnp.sum(modes_ref[...] * weighted, axis=1, keepdims=True)
    near = near_ref[...] * weighted
    loads = [own]
    for q in range(4):
        loads.append(-jnp.sum(near[:, SLOT * q : SLOT * (q + 1)], axis=1, keepdims=True))
    loads.append(jnp.zeros((LANES - 5 * CORNERS, 1), jnp.float32))
    column = jnp.concatenate(loads, axis=0)
    return jnp.dot(rt_ref[0:chunks, :], column * l_ref[...], precision=HIGHEST)


def plane_edges(tile, target, ncols):
    pair, col = target // ncols, target % ncols
    same = lax.axis_index("xl") == pair
    here = lax.axis_index("sy")
    first = jnp.where(
        same,
        jnp.where(here + 1 == col, tile[0:2], jnp.where(here - 1 == col, tile[4:6], 0.0)),
        jnp.where(here == col, tile[2:4], 0.0),
    )
    second = jnp.where(same, 0.0, jnp.where(here == col, tile[6:8], 0.0))
    return first, second


def plane_arrivals(arrived, row, ncols):
    pair, here = lax.axis_index("xl"), lax.axis_index("sy")
    base = pair * ncols
    east = arrived[base + jnp.minimum(here + 1, ncols - 1), row : row + 2, :]
    west = arrived[base + jnp.maximum(here - 1, 0), row : row + 2, :]
    other = (1 - pair) * ncols + here
    their_south = arrived[other, row : row + 2, :]
    their_north = arrived[other, row + 2 : row + 4, :]
    south = jnp.where(pair == 0, their_north, 0.0)
    north = jnp.where(pair == 0, 0.0, their_south)
    forward = jnp.where(pair == 0, their_south, their_north)
    return jnp.concatenate([east, south, west, north], axis=0), forward


def z_edge(forward, target):
    goal = jnp.where(lax.axis_index("xl") == 0, lax.axis_index("z") + 1, lax.axis_index("z") - 1)
    return jnp.where(goal == target, forward, 0.0)


def z_arrival(arrived, row, partner):
    levels = arrived.shape[0]
    pair, level = lax.axis_index("xl"), lax.axis_index("z")
    source = jnp.where(pair == 0, jnp.maximum(level - 1, 0), jnp.minimum(level + 1, levels - 1))
    edge = arrived[source, row : row + 2, :]
    south = jnp.where(pair == 0, partner[2:4], edge)
    north = jnp.where(pair == 0, edge, partner[6:8])
    return jnp.concatenate([partner[0:2], south, partner[4:6], north], axis=0)


def apply_schur(tile, map_tile, map_row, mask_row, schur_ref, modes_ref, near_ref, rt_ref, l_ref, out_ref):
    chunks = out_ref.shape[0]
    y_row = apply_matrix(tile, map_tile, map_row, schur_ref)
    load = coarse_load(0.25 * mask_row * y_row, modes_ref, near_ref, rt_ref, l_ref, chunks)
    y = as_tile(y_row)
    gamma = jnp.broadcast_to(0.25 * total(tile * y), (1, LANES))
    rest = jnp.zeros((2, LANES), jnp.float32)
    for p in range(chunks):
        first, second = plane_edges(y, p, chunks // 2)
        out_ref[p, 0:TILE, :] = jnp.concatenate([load[p : p + 1], gamma, first, second, rest], axis=0)
    return y


def pack_kernel(
    links_hbm, modes_hbm, map_hbm, gap_hbm, cmap_hbm, out_modes, to_east, to_south, to_west, to_north, out_row, out_tile,
    out_cmap, links_ref, modes_ref, map_ref, gap_ref, cmap_ref, sems,
):
    copies = [
        pltpu.make_async_copy(source, target, sems.at[k])
        for k, (source, target) in enumerate(
            (
                (modes_hbm, modes_ref), (map_hbm, map_ref), (gap_hbm, gap_ref), (cmap_hbm, cmap_ref),
                (links_hbm, links_ref),
            )
        )
    ]
    for copy in copies:
        copy.start()
    for copy in copies:
        copy.wait()
    nrows, ncols = lax.axis_size("z") * lax.axis_size("xl"), lax.axis_size("sy")
    row_here = lax.axis_index("z") * lax.axis_size("xl") + lax.axis_index("xl")
    map_row = jnp.concatenate(slots(map_ref[0], 4, -1), axis=1)
    out_row[...] = map_row
    out_tile[...] = as_tile(map_row)
    width = modes_ref.shape[3]
    modes = jnp.concatenate([modes_ref[0, 0], jnp.zeros((8, width), jnp.float32)], axis=0)
    first = modes.astype(jnp.bfloat16)
    left = modes - first.astype(jnp.float32)
    second = left.astype(jnp.bfloat16)
    third = (left - second.astype(jnp.float32)).astype(jnp.bfloat16)
    acc = jnp.zeros((CORNERS + 8, TILE * LANES), jnp.float32)
    for b in range(width // LANES):
        cols = slice(b * LANES, (b + 1) * LANES)
        index = iota((LANES, TILE * LANES), 0) + b * LANES
        hit = jnp.where(map_row == index, 1.0, 0.0).astype(jnp.bfloat16)
        for part in (first, second, third):
            acc = acc + jnp.dot(part[:, cols], hit, preferred_element_type=jnp.float32)
    acc = acc[0:CORNERS]
    out_modes[...] = acc
    links = jnp.where(links_ref[0] == 1, 1.0, 0.0)
    east = jnp.where(lax.axis_index("sy") < ncols - 1, links[:, 0:1], 0.0)
    south = jnp.where(row_here < nrows - 1, links[:, 1:2], 0.0)
    gaps = slots(gap_ref[0], 2, 0.0)
    out_cmap[...] = jnp.zeros(out_cmap.shape, jnp.float32)
    out_cmap[0:1, 0:CORNERS] = cmap_ref[0].astype(jnp.float32)
    cmap = out_cmap[...]
    rest = jnp.zeros((5, SLOT), jnp.float32)
    none = jnp.zeros((1, SLOT), jnp.float32)
    for q, ref in enumerate((to_east, to_south, to_west, to_north)):
        ref[0:CORNERS, :] = acc[:, SLOT * q : SLOT * (q + 1)]
        values, mask = none, none
        if q < 2:
            mask = none + (east, south)[q]
            values = gaps[q] * mask
        ref[CORNERS : CORNERS + 8, :] = jnp.concatenate([values, mask, cmap, rest], axis=0)


def load_kernel(schur_hbm, coarse_hbm, schur_out, blocks_out, coarse_ref, sems):
    matrix = pltpu.make_async_copy(schur_hbm.at[0, 0], schur_out, sems.at[0])
    coarse = pltpu.make_async_copy(coarse_hbm, coarse_ref, sems.at[1])
    coarse.start()
    matrix.start()
    coarse.wait()
    chunks = blocks_out.shape[0]
    ncoarse = coarse_ref.shape[1]
    block = ncoarse // chunks
    padded = -(-ncoarse // LANES) * LANES
    values = coarse_ref[...]
    if padded > ncoarse:
        values = jnp.pad(values, ((0, 0), (0, padded - ncoarse)))
    values = jnp.concatenate([values, jnp.zeros((TILE - NDOF, padded), jnp.float32)], axis=0)
    values = jnp.concatenate([values, jnp.zeros((TILE, LANES), jnp.float32)], axis=1)
    lanes = iota((TILE, LANES), 1)
    for p in range(chunks):
        start = block * p // LANES * LANES
        window = values[:, start : start + SLOT]
        shift = block * p - start
        if shift:
            window = pltpu.roll(window, SLOT - shift, 1)
        blocks_out[p] = jnp.where(lanes < block, window[:, 0:LANES], 0.0)
    matrix.wait()


def start_kernel(
    own_east, own_south, from_east, from_south, from_west, from_north, cmap_ref, map_ref, map_tile_ref, schur_ref, modes_ref,
    blocks_ref, out_ref, state, near, r_ref, rt_ref, l_ref, mask_row_ref,
):
    chunks = out_ref.shape[0]
    block = NDOF * chunks // 2
    row, cm = CORNERS, CORNERS + 2
    sources = (from_east, from_south, from_west, from_north)
    for q, ref in enumerate(sources):
        near[:, SLOT * q : SLOT * (q + 1)] = ref[0:CORNERS, :]
    values = [own_east[row : row + 1], own_south[row : row + 1], -from_west[row : row + 1], -from_north[row : row + 1]]
    masks = [ref[row + 1 : row + 2] for ref in (own_east, own_south, from_west, from_north)]
    residual = as_tile(jnp.concatenate(values, axis=1))
    mask_row = jnp.concatenate(masks, axis=1)
    mask_row_ref[...] = mask_row
    maps = [cmap_ref[:, 0:LANES]] + [ref[cm : cm + 1, 0:LANES] for ref in sources]
    columns = jnp.transpose(jnp.concatenate(maps + [jnp.zeros((3, LANES), jnp.float32)], axis=0))
    column = [columns[0:CORNERS, g : g + 1] for g in range(5)]
    column.append(jnp.full((LANES - 5 * CORNERS, 1), float(block * chunks), jnp.float32))
    column = jnp.concatenate(column, axis=0)
    group = jnp.floor((column + 0.5) * (1.0 / block))
    inside = column - group * block
    lanes = iota((LANES, LANES), 1).astype(jnp.float32)
    hit_row = jnp.where((group == lanes) & (lanes < chunks), 1.0, 0.0)
    r_ref[...] = hit_row
    rt_ref[...] = jnp.transpose(hit_row)
    l_ref[...] = jnp.where(inside == lanes, 1.0, 0.0)
    y = apply_schur(residual, map_tile_ref[...], map_ref[...], mask_row, schur_ref, modes_ref, near, rt_ref, l_ref, out_ref)
    for p in range(chunks):
        out_ref[p, TILE : 2 * TILE, :] = blocks_ref[p]
    state[...] = jnp.zeros(state.shape, jnp.float32)
    state[RES : RES + TILE, :] = residual
    state[IFACE : IFACE + TILE, :] = y
    state[MASK : MASK + TILE, :] = as_tile(mask_row)


def rows_kernel(arrived, state_in, out_ref, state):
    chunks, levels = arrived.shape[0], out_ref.shape[0]
    summed = arrived[0, 0:TILE, :]
    for p in range(1, chunks):
        summed = summed + arrived[p, 0:TILE, :]
    partner, forward = plane_arrivals(arrived, 2, chunks // 2)
    state[...] = state_in[...]
    state[PARTNER : PARTNER + TILE, :] = partner
    for level in range(levels):
        out_ref[level] = jnp.concatenate([summed[0:2], z_edge(forward, level)], axis=0)


def direction_kernel(step, arrived, state_in, map_ref, map_tile_ref, kinv_ref, blocks_ref, out_ref, state):
    chunks, levels = out_ref.shape[0], arrived.shape[0]
    half = chunks // 2
    summed = arrived[0]
    for level in range(1, levels):
        summed = summed + arrived[level]
    partner = z_arrival(arrived, 2, state_in[PARTNER : PARTNER + TILE, :])
    direction = 0.25 * state_in[MASK : MASK + TILE, :] * (state_in[IFACE : IFACE + TILE, :] - partner)
    load = summed[0:1]
    gamma = summed[1:2]
    if step:
        beta = gamma / state_in[GAMMA : GAMMA + 1, :]
        direction = direction + beta * state_in[DIR : DIR + TILE, :]
        load = load + beta * state_in[LOAD : LOAD + 1, :]
    inner = as_tile(apply_matrix(direction, map_tile_ref[...], map_ref[...], kinv_ref))
    energy = jnp.broadcast_to(total(direction * inner), (1, LANES))
    lanes = iota((TILE, LANES), 1)
    dof = iota((TILE, LANES), 0)
    solved = []
    for a in range(2):
        acc = jnp.zeros((TILE, LANES), jnp.float32)
        for p in range(half):
            column = jnp.sum(blocks_ref[a * half + p, TILE : 2 * TILE, :] * load, axis=1, keepdims=True)
            acc = acc + jnp.where((lanes == dof + p * NDOF) & (dof < NDOF), column, 0.0)
        solved.append(jnp.sum(acc, axis=0, keepdims=True))
    for p in range(chunks):
        first, second = plane_edges(inner, p, half)
        out_ref[p] = jnp.concatenate(solved + [load, energy, first, second], axis=0)
    state[...] = state_in[...]
    state[DIR : DIR + TILE, :] = direction
    state[IFACE : IFACE + TILE, :] = inner
    state[SCAL : SCAL + TILE, :] = jnp.concatenate([gamma, load, jnp.zeros((6, LANES), jnp.float32)], axis=0)


def solve_kernel(arrived, state_in, out_ref, state, whole_load):
    chunks, levels = arrived.shape[0], out_ref.shape[0]
    block = NDOF * chunks // 2
    summed = arrived[0]
    for p in range(1, chunks):
        summed = summed + arrived[p]
    whole_load[...] = jnp.concatenate([arrived[p, 2:3, :] for p in range(chunks)], axis=0)
    partner, forward = plane_arrivals(arrived, 4, chunks // 2)
    state[...] = state_in[...]
    state[PARTNER : PARTNER + TILE, :] = partner
    first = jnp.where(iota((1, LANES), 1) < block, summed[0:1], summed[3:4])
    for level in range(levels):
        out_ref[level] = jnp.concatenate([first, summed[1:2], z_edge(forward, level)], axis=0)


def advance(arrived, state_in, whole_load, modes_ref, near_ref, r_ref, l_ref):
    levels = arrived.shape[0]
    energy = arrived[0, 0:1, :]
    for level in range(1, levels):
        energy = energy + arrived[level, 0:1, :]
    partner = z_arrival(arrived, 2, state_in[PARTNER : PARTNER + TILE, :])
    solved = jnp.concatenate([arrived[level, 0:2, :] for level in range(levels)], axis=0)
    energy = energy[:, LANES - 1 : LANES] + total(whole_load[...] * solved)
    alpha = state_in[GAMMA : GAMMA + 1, :] / energy
    found = jnp.dot(r_ref[:, 0 : 2 * levels], solved, precision=HIGHEST)
    corners = jnp.sum(found * l_ref[...], axis=1, keepdims=True)
    coarse = jnp.sum(corners[0:CORNERS] * modes_ref[...], axis=0, keepdims=True)
    near = []
    for q in range(4):
        values = corners[CORNERS * (q + 1) : CORNERS * (q + 2)]
        near.append(jnp.sum(values * near_ref[:, SLOT * q : SLOT * (q + 1)], axis=0, keepdims=True))
    coarse = as_tile(coarse - jnp.concatenate(near, axis=1))
    image = state_in[MASK : MASK + TILE, :] * (state_in[IFACE : IFACE + TILE, :] - partner + coarse)
    multipliers = state_in[MUL : MUL + TILE, :] + alpha * state_in[DIR : DIR + TILE, :]
    residual = state_in[RES : RES + TILE, :] - alpha * image
    return multipliers, residual


def next_kernel(
    arrived, state_in, whole_load, modes_ref, near_ref, r_ref, l_ref, rt_ref, mask_row_ref, map_ref, map_tile_ref, schur_ref,
    out_ref, state,
):
    multipliers, residual = advance(arrived, state_in, whole_load, modes_ref, near_ref, r_ref, l_ref)
    y = apply_schur(
        residual, map_tile_ref[...], map_ref[...], mask_row_ref[...], schur_ref, modes_ref, near_ref, rt_ref, l_ref, out_ref
    )
    state[...] = state_in[...]
    state[RES : RES + TILE, :] = residual
    state[MUL : MUL + TILE, :] = multipliers
    state[IFACE : IFACE + TILE, :] = y


def last_kernel(
    arrived, state_in, whole_load, modes_ref, near_ref, r_ref, l_ref, out_multipliers, out_residual, scratch, sems
):
    results = advance(arrived, state_in, whole_load, modes_ref, near_ref, r_ref, l_ref)
    width = scratch.shape[3]
    none = jnp.zeros((1, width - SLOT), jnp.float32)
    lanes = iota((1, width), 1)
    copies = []
    for k, (tile, target) in enumerate(zip(results, (out_multipliers, out_residual))):
        east = jnp.concatenate([tile[0:1], tile[1:2], none], axis=1)
        south = jnp.concatenate([tile[2:3], tile[3:4], none], axis=1)
        south = pltpu.roll(jnp.broadcast_to(south, (TILE, width)), width // 2, 1)[0:1]
        scratch[k, 0] = jnp.where(lanes < width // 2, east, south)
        copies.append(pltpu.make_async_copy(scratch.at[k], target, sems.at[k]))
        copies[k].start()
    for copy in copies:
        copy.wait()


def shifted(block, axis, distance):
    devices = range(lax.axis_size(axis))
    route = [(i - distance, i) for i in devices if i - distance in devices]
    return lax.ppermute(block, axis, route)


def on_device(gap, kinv, schur, corner_modes, coarse_inverse, edge_map, corner_map, links):
    levels, chunks = lax.axis_size("z"), lax.axis_size("xl") * lax.axis_size("sy")
    width = kinv.shape[-1]
    kinv = kinv.reshape(width, width)
    ints = jnp.int32
    own_modes, east, south, west, north, map_row, map_tile, cmap = call(
        pack_kernel,
        in_hbm(links, corner_modes, edge_map, gap, corner_map),
        [(CORNERS, TILE * LANES)]
        + [(CORNERS + 8, SLOT)] * 4
        + [jax.ShapeDtypeStruct((1, TILE * LANES), ints), jax.ShapeDtypeStruct((TILE, LANES), ints), (1, SLOT)],
        in_specs=[HBM] * 5,
        scratch=[
            pltpu.VMEM(links.shape, ints),
            pltpu.VMEM(corner_modes.shape, jnp.float32),
            pltpu.VMEM(edge_map.shape, ints),
            pltpu.VMEM(gap.shape, jnp.float32),
            pltpu.VMEM(corner_map.shape, ints),
            pltpu.SemaphoreType.DMA((5,)),
        ],
        name="pack",
    )
    from_west = shifted(east, "sy", 1)
    from_east = shifted(west, "sy", -1)
    from_north = shifted(south, ROWS_AXES, 1)
    from_south = shifted(north, ROWS_AXES, -1)
    schur, blocks = call(
        load_kernel,
        in_hbm(schur, coarse_inverse),
        [(width, width), (chunks, TILE, LANES)],
        in_specs=[HBM] * 2,
        scratch=[pltpu.VMEM(coarse_inverse.shape, jnp.float32), pltpu.SemaphoreType.DMA((2,))],
        name="load",
    )
    square = (LANES, LANES)
    state_shape = (NSTATE, LANES)
    out, state, near, r, rt, l, mask_row = call(
        start_kernel,
        (
            east, south, from_east, from_south, from_west, from_north, cmap, map_row, map_tile, schur, own_modes, blocks,
        ),
        [(chunks, 2 * TILE, LANES), state_shape, (CORNERS, TILE * LANES), square, square, square, (1, TILE * LANES)],
        name="start",
    )
    to_plane, to_z = (chunks, TILE, LANES), (levels, 4, LANES)
    for step in range(ITERS):
        arrived = lax.all_to_all(out, PLANE, 0, 0, tiled=True)
        if step == 0:
            solver = arrived
        out, state = call(rows_kernel, (arrived, state), [to_z, state_shape], name="rows")
        arrived = lax.all_to_all(out, "z", 0, 0, tiled=True)

        def kernel(*refs, step=step):
            direction_kernel(step, *refs)

        out, state = call(
            kernel, (arrived, state, map_row, map_tile, kinv, solver), [to_plane, state_shape], name="direction"
        )
        arrived = lax.all_to_all(out, PLANE, 0, 0, tiled=True)
        out, state, load = call(solve_kernel, (arrived, state), [to_z, state_shape, (chunks, LANES)], name="solve")
        arrived = lax.all_to_all(out, "z", 0, 0, tiled=True)
        common = (arrived, state, load, own_modes, near, r, l)
        if step + 1 < ITERS:
            out, state = call(
                next_kernel, common + (rt, mask_row, map_row, map_tile, schur), [to_plane, state_shape], name="next"
            )
    return tuple(
        call(
            last_kernel,
            common,
            [gap.shape] * 2,
            out_specs=[HBM] * 2,
            scratch=[pltpu.VMEM((2,) + gap.shape[:2] + gap.shape[2:], jnp.float32), pltpu.SemaphoreType.DMA((2,))],
            name="last",
        )
    )


def solution(mesh):
    rows, cols = mesh.devices.shape
    split = Mesh(mesh.devices.reshape(rows // 2, 2, cols), ("z", "xl", "sy"))
    placed = (
        P(ROWS_AXES, "sy", None),
        P(ROWS_AXES, "sy", None, None),
        P(ROWS_AXES, "sy", None, None),
        P(ROWS_AXES, "sy", None, None),
        P(("z", "xl", "sy"), None),
        P(ROWS_AXES, "sy", None),
        P(ROWS_AXES, "sy", None),
        P(ROWS_AXES, "sy", None),
    )
    return jax.shard_map(
        on_device,
        mesh=split,
        in_specs=placed,
        out_specs=(P(ROWS_AXES, "sy", None), P(ROWS_AXES, "sy", None)),
        check_vma=False,
    )
```

```python
import jax
import jax.numpy as jnp
from jax import lax
from jax.experimental import pallas as pl
from jax.experimental.pallas import tpu as pltpu
from jax.sharding import Mesh
from jax.sharding import PartitionSpec as P

ITERS = 3
LANES = 128
SLOT = 256
TILE = 8
CORNERS = 24
NDOF = 6
HIGHEST = lax.Precision.HIGHEST
VMEM = pl.BlockSpec(memory_space=pltpu.VMEM)
HBM = pl.BlockSpec(memory_space=pl.ANY)
LIMIT = 40 * 1024 * 1024

ROWS_AXES = ("z", "xl")
PLANE = ("xl", "sy")

RES, MUL, DIR, IFACE, PARTNER, MASK, SCAL, NSTATE = 0, 8, 16, 24, 32, 40, 48, 56
GAMMA, LOAD = 48, 49


def call(kernel, inputs, outputs, in_specs=None, out_specs=None, scratch=(), name=None):
    shapes = [shape if hasattr(shape, "dtype") else jax.ShapeDtypeStruct(shape, jnp.float32) for shape in outputs]
    return pl.pallas_call(
        kernel,
        out_shape=shapes,
        in_specs=in_specs or [VMEM] * len(inputs),
        out_specs=out_specs or [VMEM] * len(outputs),
        scratch_shapes=list(scratch),
        compiler_params=pltpu.CompilerParams(vmem_limit_bytes=LIMIT),
        name=name,
    )(*inputs)


def in_hbm(*arrays):
    return tuple(pltpu.with_memory_space_constraint(array, pltpu.HBM) for array in arrays)


def iota(shape, dim):
    return lax.broadcasted_iota(jnp.int32, shape, dim)


def as_tile(row):
    return jnp.concatenate([row[:, LANES * c : LANES * (c + 1)] for c in range(TILE)], axis=0)


def total(value):
    return jnp.sum(jnp.sum(value, axis=1, keepdims=True), axis=0, keepdims=True)


def slots(row, count, fill):
    width = row.shape[1]
    wide = jnp.broadcast_to(row, (TILE, width))
    lanes = iota((1, SLOT), 1)
    edge = SLOT * 3 // 4
    pieces = []
    for q in range(count):
        moved = wide if q == 0 else pltpu.roll(wide, width - edge * q, 1)
        pieces.append(jnp.where(lanes < edge, moved[0:1, 0:SLOT], fill))
    return pieces


def apply_matrix(tile, map_tile, map_row, matrix_ref):
    width = matrix_ref.shape[0]
    values = jnp.transpose(tile)
    places = jnp.transpose(map_tile)
    lanes = iota((LANES, LANES), 1)
    pieces = []
    for t in range(width // LANES):
        acc = jnp.zeros((LANES, LANES), jnp.float32)
        for c in range(TILE):
            hit = places[:, c : c + 1] == lanes + t * LANES
            acc = acc + jnp.where(hit, values[:, c : c + 1], 0.0)
        pieces.append(jnp.sum(acc, axis=0, keepdims=True))
    out = jnp.zeros((TILE, TILE * LANES), jnp.float32)
    for b in range(width // LANES):
        rows = slice(b * LANES, (b + 1) * LANES)
        acc = matrix_ref[rows, 0:LANES] * pieces[0]
        for t in range(1, width // LANES):
            acc = acc + matrix_ref[rows, t * LANES : (t + 1) * LANES] * pieces[t]
        column = jnp.sum(acc, axis=1, keepdims=True)
        for s in range(LANES // TILE):
            index = iota((TILE, TILE * LANES), 0) + (b * LANES + s * TILE)
            out = out + jnp.where(map_row == index, column[s * TILE : (s + 1) * TILE, :], 0.0)
    return jnp.sum(out, axis=0, keepdims=True)


def coarse_load(weighted, modes_ref, near_ref, rt_ref, l_ref, chunks):
    own = jnp.sum(modes_ref[...] * weighted, axis=1, keepdims=True)
    near = near_ref[...] * weighted
    loads = [own]
    for q in range(4):
        loads.append(-jnp.sum(near[:, SLOT * q : SLOT * (q + 1)], axis=1, keepdims=True))
    loads.append(jnp.zeros((LANES - 5 * CORNERS, 1), jnp.float32))
    column = jnp.concatenate(loads, axis=0)
    return jnp.dot(rt_ref[0:chunks, :], column * l_ref[...], precision=HIGHEST)


def plane_edges(tile, target, ncols):
    pair, col = target // ncols, target % ncols
    same = lax.axis_index("xl") == pair
    here = lax.axis_index("sy")
    first = jnp.where(
        same,
        jnp.where(here + 1 == col, tile[0:2], jnp.where(here - 1 == col, tile[4:6], 0.0)),
        jnp.where(here == col, tile[2:4], 0.0),
    )
    second = jnp.where(same, 0.0, jnp.where(here == col, tile[6:8], 0.0))
    return first, second


def plane_arrivals(arrived, row, ncols):
    pair, here = lax.axis_index("xl"), lax.axis_index("sy")
    base = pair * ncols
    east = arrived[base + jnp.minimum(here + 1, ncols - 1), row : row + 2, :]
    west = arrived[base + jnp.maximum(here - 1, 0), row : row + 2, :]
    other = (1 - pair) * ncols + here
    their_south = arrived[other, row : row + 2, :]
    their_north = arrived[other, row + 2 : row + 4, :]
    south = jnp.where(pair == 0, their_north, 0.0)
    north = jnp.where(pair == 0, 0.0, their_south)
    forward = jnp.where(pair == 0, their_south, their_north)
    return jnp.concatenate([east, south, west, north], axis=0), forward


def z_edge(forward, target):
    goal = jnp.where(lax.axis_index("xl") == 0, lax.axis_index("z") + 1, lax.axis_index("z") - 1)
    return jnp.where(goal == target, forward, 0.0)


def z_arrival(arrived, row, partner):
    levels = arrived.shape[0]
    pair, level = lax.axis_index("xl"), lax.axis_index("z")
    source = jnp.where(pair == 0, jnp.maximum(level - 1, 0), jnp.minimum(level + 1, levels - 1))
    edge = arrived[source, row : row + 2, :]
    south = jnp.where(pair == 0, partner[2:4], edge)
    north = jnp.where(pair == 0, edge, partner[6:8])
    return jnp.concatenate([partner[0:2], south, partner[4:6], north], axis=0)


def apply_schur(tile, map_tile, map_row, mask_row, schur_ref, modes_ref, near_ref, rt_ref, l_ref, out_ref):
    chunks = out_ref.shape[0]
    y_row = apply_matrix(tile, map_tile, map_row, schur_ref)
    load = coarse_load(0.25 * mask_row * y_row, modes_ref, near_ref, rt_ref, l_ref, chunks)
    y = as_tile(y_row)
    gamma = jnp.broadcast_to(0.25 * total(tile * y), (1, LANES))
    rest = jnp.zeros((2, LANES), jnp.float32)
    for p in range(chunks):
        first, second = plane_edges(y, p, chunks // 2)
        out_ref[p, 0:TILE, :] = jnp.concatenate([load[p : p + 1], gamma, first, second, rest], axis=0)
    return y


def pack_kernel(
    links_hbm, modes_hbm, map_hbm, gap_hbm, cmap_hbm, schur_hbm, out_modes, col_even, col_odd, row_pair, row_cross, out_own,
    out_row, out_tile, out_cmap, out_schur, links_ref, modes_ref, map_ref, gap_ref, cmap_ref, sems,
):
    copies = [
        pltpu.make_async_copy(source, target, sems.at[k])
        for k, (source, target) in enumerate(
            (
                (modes_hbm, modes_ref), (map_hbm, map_ref), (gap_hbm, gap_ref), (cmap_hbm, cmap_ref),
                (links_hbm, links_ref),
            )
        )
    ]
    matrix = pltpu.make_async_copy(schur_hbm.at[0, 0], out_schur, sems.at[len(copies)])
    for copy in copies:
        copy.start()
    matrix.start()
    for copy in copies:
        copy.wait()
    nrows, ncols = lax.axis_size("z") * lax.axis_size("xl"), lax.axis_size("sy")
    row_here = lax.axis_index("z") * lax.axis_size("xl") + lax.axis_index("xl")
    map_row = jnp.concatenate(slots(map_ref[0], 4, -1), axis=1)
    out_row[...] = map_row
    out_tile[...] = as_tile(map_row)
    width = modes_ref.shape[3]
    modes = jnp.concatenate([modes_ref[0, 0], jnp.zeros((8, width), jnp.float32)], axis=0)
    first = modes.astype(jnp.bfloat16)
    left = modes - first.astype(jnp.float32)
    second = left.astype(jnp.bfloat16)
    third = (left - second.astype(jnp.float32)).astype(jnp.bfloat16)
    acc = jnp.zeros((CORNERS + 8, TILE * LANES), jnp.float32)
    for b in range(width // LANES):
        cols = slice(b * LANES, (b + 1) * LANES)
        index = iota((LANES, TILE * LANES), 0) + b * LANES
        hit = jnp.where(map_row == index, 1.0, 0.0).astype(jnp.bfloat16)
        for part in (first, second, third):
            acc = acc + jnp.dot(part[:, cols], hit, preferred_element_type=jnp.float32)
    acc = acc[0:CORNERS]
    out_modes[...] = acc
    links = jnp.where(links_ref[0] == 1, 1.0, 0.0)
    east = jnp.where(lax.axis_index("sy") < ncols - 1, links[:, 0:1], 0.0)
    south = jnp.where(row_here < nrows - 1, links[:, 1:2], 0.0)
    gaps = slots(gap_ref[0], 2, 0.0)
    out_cmap[...] = jnp.zeros(out_cmap.shape, jnp.float32)
    out_cmap[0:1, 0:CORNERS] = cmap_ref[0].astype(jnp.float32)
    cmap = out_cmap[...]
    rest = jnp.zeros((5, SLOT), jnp.float32)
    none = jnp.zeros((1, SLOT), jnp.float32)
    parts = []
    own = []
    for q in range(4):
        values, mask = none, none
        if q < 2:
            mask = none + (east, south)[q]
            values = gaps[q] * mask
            own += [values, mask]
        parts.append(jnp.concatenate([acc[:, SLOT * q : SLOT * (q + 1)], values, mask, cmap, rest], axis=0))
    out_own[...] = jnp.concatenate(own + [jnp.zeros((4, SLOT), jnp.float32)], axis=0)
    even = lax.axis_index("sy") % 2 == 0
    first_row = lax.axis_index("xl") == 0
    col_even[...] = jnp.where(even, parts[0], parts[2])
    col_odd[...] = jnp.where(even, parts[2], parts[0])
    row_pair[...] = jnp.where(first_row, parts[1], parts[3])
    row_cross[...] = jnp.where(first_row, parts[3], parts[1])
    matrix.wait()


def load_kernel(coarse_hbm, blocks_out, coarse_ref, sem):
    coarse = pltpu.make_async_copy(coarse_hbm, coarse_ref, sem)
    coarse.start()
    coarse.wait()
    chunks = blocks_out.shape[0]
    ncoarse = coarse_ref.shape[1]
    block = ncoarse // chunks
    padded = -(-ncoarse // LANES) * LANES
    values = coarse_ref[...]
    if padded > ncoarse:
        values = jnp.pad(values, ((0, 0), (0, padded - ncoarse)))
    values = jnp.concatenate([values, jnp.zeros((TILE - NDOF, padded), jnp.float32)], axis=0)
    values = jnp.concatenate([values, jnp.zeros((TILE, LANES), jnp.float32)], axis=1)
    lanes = iota((TILE, LANES), 1)
    for p in range(chunks):
        start = block * p // LANES * LANES
        window = values[:, start : start + SLOT]
        shift = block * p - start
        if shift:
            window = pltpu.roll(window, SLOT - shift, 1)
        blocks_out[p] = jnp.where(lanes < block, window[:, 0:LANES], 0.0)


def start_kernel(
    own_ref, col_even, col_odd, row_pair, row_cross, cmap_ref, map_ref, map_tile_ref, schur_ref, modes_ref, blocks_ref, out_ref,
    state, near, r_ref, rt_ref, l_ref, mask_row_ref,
):
    chunks = out_ref.shape[0]
    block = NDOF * chunks // 2
    row, cm = CORNERS, CORNERS + 2
    even = lax.axis_index("sy") % 2 == 0
    first_row = lax.axis_index("xl") == 0
    from_east = jnp.where(even, col_even[...], col_odd[...])
    from_west = jnp.where(even, col_odd[...], col_even[...])
    from_south = jnp.where(first_row, row_pair[...], row_cross[...])
    from_north = jnp.where(first_row, row_cross[...], row_pair[...])
    sources = (from_east, from_south, from_west, from_north)
    for q, part in enumerate(sources):
        near[:, SLOT * q : SLOT * (q + 1)] = part[0:CORNERS]
    values = [own_ref[0:1], own_ref[2:3], -from_west[row : row + 1], -from_north[row : row + 1]]
    masks = [own_ref[1:2], own_ref[3:4], from_west[row + 1 : row + 2], from_north[row + 1 : row + 2]]
    residual = as_tile(jnp.concatenate(values, axis=1))
    mask_row = jnp.concatenate(masks, axis=1)
    mask_row_ref[...] = mask_row
    maps = [cmap_ref[:, 0:LANES]] + [part[cm : cm + 1, 0:LANES] for part in sources]
    columns = jnp.transpose(jnp.concatenate(maps + [jnp.zeros((3, LANES), jnp.float32)], axis=0))
    column = [columns[0:CORNERS, g : g + 1] for g in range(5)]
    column.append(jnp.full((LANES - 5 * CORNERS, 1), float(block * chunks), jnp.float32))
    column = jnp.concatenate(column, axis=0)
    group = jnp.floor((column + 0.5) * (1.0 / block))
    inside = column - group * block
    lanes = iota((LANES, LANES), 1).astype(jnp.float32)
    hit_row = jnp.where((group == lanes) & (lanes < chunks), 1.0, 0.0)
    r_ref[...] = hit_row
    rt_ref[...] = jnp.transpose(hit_row)
    l_ref[...] = jnp.where(inside == lanes, 1.0, 0.0)
    y = apply_schur(residual, map_tile_ref[...], map_ref[...], mask_row, schur_ref, modes_ref, near, rt_ref, l_ref, out_ref)
    for p in range(chunks):
        out_ref[p, TILE : 2 * TILE, :] = blocks_ref[p]
    state[...] = jnp.zeros(state.shape, jnp.float32)
    state[RES : RES + TILE, :] = residual
    state[IFACE : IFACE + TILE, :] = y
    state[MASK : MASK + TILE, :] = as_tile(mask_row)


def rows_kernel(arrived, state_in, out_ref, state):
    chunks, levels = arrived.shape[0], out_ref.shape[0]
    summed = arrived[0, 0:TILE, :]
    for p in range(1, chunks):
        summed = summed + arrived[p, 0:TILE, :]
    partner, forward = plane_arrivals(arrived, 2, chunks // 2)
    state[...] = state_in[...]
    state[PARTNER : PARTNER + TILE, :] = partner
    for level in range(levels):
        out_ref[level] = jnp.concatenate([summed[0:2], z_edge(forward, level)], axis=0)


def direction_kernel(step, arrived, state_in, map_ref, map_tile_ref, kinv_ref, blocks_ref, out_ref, state):
    chunks, levels = out_ref.shape[0], arrived.shape[0]
    half = chunks // 2
    summed = arrived[0]
    for level in range(1, levels):
        summed = summed + arrived[level]
    partner = z_arrival(arrived, 2, state_in[PARTNER : PARTNER + TILE, :])
    direction = 0.25 * state_in[MASK : MASK + TILE, :] * (state_in[IFACE : IFACE + TILE, :] - partner)
    load = summed[0:1]
    gamma = summed[1:2]
    if step:
        beta = gamma / state_in[GAMMA : GAMMA + 1, :]
        direction = direction + beta * state_in[DIR : DIR + TILE, :]
        load = load + beta * state_in[LOAD : LOAD + 1, :]
    inner = as_tile(apply_matrix(direction, map_tile_ref[...], map_ref[...], kinv_ref))
    energy = jnp.broadcast_to(total(direction * inner), (1, LANES))
    lanes = iota((TILE, LANES), 1)
    dof = iota((TILE, LANES), 0)
    solved = []
    for a in range(2):
        acc = jnp.zeros((TILE, LANES), jnp.float32)
        for p in range(half):
            column = jnp.sum(blocks_ref[a * half + p, TILE : 2 * TILE, :] * load, axis=1, keepdims=True)
            acc = acc + jnp.where((lanes == dof + p * NDOF) & (dof < NDOF), column, 0.0)
        solved.append(jnp.sum(acc, axis=0, keepdims=True))
    for p in range(chunks):
        first, second = plane_edges(inner, p, half)
        out_ref[p] = jnp.concatenate(solved + [load, energy, first, second], axis=0)
    state[...] = state_in[...]
    state[DIR : DIR + TILE, :] = direction
    state[IFACE : IFACE + TILE, :] = inner
    state[SCAL : SCAL + TILE, :] = jnp.concatenate([gamma, load, jnp.zeros((6, LANES), jnp.float32)], axis=0)


def solve_kernel(arrived, state_in, out_ref, state, whole_load):
    chunks, levels = arrived.shape[0], out_ref.shape[0]
    block = NDOF * chunks // 2
    summed = arrived[0]
    for p in range(1, chunks):
        summed = summed + arrived[p]
    whole_load[...] = jnp.concatenate([arrived[p, 2:3, :] for p in range(chunks)], axis=0)
    partner, forward = plane_arrivals(arrived, 4, chunks // 2)
    state[...] = state_in[...]
    state[PARTNER : PARTNER + TILE, :] = partner
    first = jnp.where(iota((1, LANES), 1) < block, summed[0:1], summed[3:4])
    for level in range(levels):
        out_ref[level] = jnp.concatenate([first, summed[1:2], z_edge(forward, level)], axis=0)


def advance(arrived, state_in, whole_load, modes_ref, near_ref, r_ref, l_ref):
    levels = arrived.shape[0]
    energy = arrived[0, 0:1, :]
    for level in range(1, levels):
        energy = energy + arrived[level, 0:1, :]
    partner = z_arrival(arrived, 2, state_in[PARTNER : PARTNER + TILE, :])
    solved = jnp.concatenate([arrived[level, 0:2, :] for level in range(levels)], axis=0)
    energy = energy[:, LANES - 1 : LANES] + total(whole_load[...] * solved)
    alpha = state_in[GAMMA : GAMMA + 1, :] / energy
    found = jnp.dot(r_ref[:, 0 : 2 * levels], solved, precision=HIGHEST)
    corners = jnp.sum(found * l_ref[...], axis=1, keepdims=True)
    coarse = jnp.sum(corners[0:CORNERS] * modes_ref[...], axis=0, keepdims=True)
    near = []
    for q in range(4):
        values = corners[CORNERS * (q + 1) : CORNERS * (q + 2)]
        near.append(jnp.sum(values * near_ref[:, SLOT * q : SLOT * (q + 1)], axis=0, keepdims=True))
    coarse = as_tile(coarse - jnp.concatenate(near, axis=1))
    image = state_in[MASK : MASK + TILE, :] * (state_in[IFACE : IFACE + TILE, :] - partner + coarse)
    multipliers = state_in[MUL : MUL + TILE, :] + alpha * state_in[DIR : DIR + TILE, :]
    residual = state_in[RES : RES + TILE, :] - alpha * image
    return multipliers, residual


def next_kernel(
    arrived, state_in, whole_load, modes_ref, near_ref, r_ref, l_ref, rt_ref, mask_row_ref, map_ref, map_tile_ref, schur_ref,
    out_ref, state,
):
    multipliers, residual = advance(arrived, state_in, whole_load, modes_ref, near_ref, r_ref, l_ref)
    y = apply_schur(
        residual, map_tile_ref[...], map_ref[...], mask_row_ref[...], schur_ref, modes_ref, near_ref, rt_ref, l_ref, out_ref
    )
    state[...] = state_in[...]
    state[RES : RES + TILE, :] = residual
    state[MUL : MUL + TILE, :] = multipliers
    state[IFACE : IFACE + TILE, :] = y


def last_kernel(
    arrived, state_in, whole_load, modes_ref, near_ref, r_ref, l_ref, out_multipliers, out_residual, scratch, sems
):
    results = advance(arrived, state_in, whole_load, modes_ref, near_ref, r_ref, l_ref)
    width = scratch.shape[3]
    none = jnp.zeros((1, width - SLOT), jnp.float32)
    lanes = iota((1, width), 1)
    copies = []
    for k, (tile, target) in enumerate(zip(results, (out_multipliers, out_residual))):
        east = jnp.concatenate([tile[0:1], tile[1:2], none], axis=1)
        south = jnp.concatenate([tile[2:3], tile[3:4], none], axis=1)
        south = pltpu.roll(jnp.broadcast_to(south, (TILE, width)), width // 2, 1)[0:1]
        scratch[k, 0] = jnp.where(lanes < width // 2, east, south)
        copies.append(pltpu.make_async_copy(scratch.at[k], target, sems.at[k]))
        copies[k].start()
    for copy in copies:
        copy.wait()


def swapped(block, axis, first):
    count = lax.axis_size(axis)
    route = []
    for i in range(first, count - 1, 2):
        route += [(i, i + 1), (i + 1, i)]
    return lax.ppermute(block, axis, route)


def on_device(gap, kinv, schur, corner_modes, coarse_inverse, edge_map, corner_map, links):
    levels, chunks = lax.axis_size("z"), lax.axis_size("xl") * lax.axis_size("sy")
    width = kinv.shape[-1]
    kinv = kinv.reshape(width, width)
    ints = jnp.int32
    own_modes, col_even, col_odd, row_pair, row_cross, own, map_row, map_tile, cmap, schur = call(
        pack_kernel,
        in_hbm(links, corner_modes, edge_map, gap, corner_map, schur),
        [(CORNERS, TILE * LANES)]
        + [(CORNERS + 8, SLOT)] * 4
        + [(TILE, SLOT), jax.ShapeDtypeStruct((1, TILE * LANES), ints), jax.ShapeDtypeStruct((TILE, LANES), ints)]
        + [(1, SLOT), (width, width)],
        in_specs=[HBM] * 6,
        scratch=[
            pltpu.VMEM(links.shape, ints),
            pltpu.VMEM(corner_modes.shape, jnp.float32),
            pltpu.VMEM(edge_map.shape, ints),
            pltpu.VMEM(gap.shape, jnp.float32),
            pltpu.VMEM(corner_map.shape, ints),
            pltpu.SemaphoreType.DMA((6,)),
        ],
        name="pack",
    )
    col_even = swapped(col_even, "sy", 0)
    col_odd = swapped(col_odd, "sy", 1)
    row_pair = swapped(row_pair, ROWS_AXES, 0)
    row_cross = swapped(row_cross, ROWS_AXES, 1)
    (blocks,) = call(
        load_kernel,
        in_hbm(coarse_inverse),
        [(chunks, TILE, LANES)],
        in_specs=[HBM],
        scratch=[pltpu.VMEM(coarse_inverse.shape, jnp.float32), pltpu.SemaphoreType.DMA(())],
        name="load",
    )
    square = (LANES, LANES)
    state_shape = (NSTATE, LANES)
    out, state, near, r, rt, l, mask_row = call(
        start_kernel,
        (
            own, col_even, col_odd, row_pair, row_cross, cmap, map_row, map_tile, schur, own_modes, blocks,
        ),
        [(chunks, 2 * TILE, LANES), state_shape, (CORNERS, TILE * LANES), square, square, square, (1, TILE * LANES)],
        name="start",
    )
    to_plane, to_z = (chunks, TILE, LANES), (levels, 4, LANES)
    for step in range(ITERS):
        arrived = lax.all_to_all(out, PLANE, 0, 0, tiled=True)
        if step == 0:
            solver = arrived
        out, state = call(rows_kernel, (arrived, state), [to_z, state_shape], name="rows")
        arrived = lax.all_to_all(out, "z", 0, 0, tiled=True)

        def kernel(*refs, step=step):
            direction_kernel(step, *refs)

        out, state = call(
            kernel, (arrived, state, map_row, map_tile, kinv, solver), [to_plane, state_shape], name="direction"
        )
        arrived = lax.all_to_all(out, PLANE, 0, 0, tiled=True)
        out, state, load = call(solve_kernel, (arrived, state), [to_z, state_shape, (chunks, LANES)], name="solve")
        arrived = lax.all_to_all(out, "z", 0, 0, tiled=True)
        common = (arrived, state, load, own_modes, near, r, l)
        if step + 1 < ITERS:
            out, state = call(
                next_kernel, common + (rt, mask_row, map_row, map_tile, schur), [to_plane, state_shape], name="next"
            )
    return tuple(
        call(
            last_kernel,
            common,
            [gap.shape] * 2,
            out_specs=[HBM] * 2,
            scratch=[pltpu.VMEM((2,) + gap.shape[:2] + gap.shape[2:], jnp.float32), pltpu.SemaphoreType.DMA((2,))],
            name="last",
        )
    )


def solution(mesh):
    rows, cols = mesh.devices.shape
    split = Mesh(mesh.devices.reshape(rows // 2, 2, cols), ("z", "xl", "sy"))
    placed = (
        P(ROWS_AXES, "sy", None),
        P(ROWS_AXES, "sy", None, None),
        P(ROWS_AXES, "sy", None, None),
        P(ROWS_AXES, "sy", None, None),
        P(("z", "xl", "sy"), None),
        P(ROWS_AXES, "sy", None),
        P(ROWS_AXES, "sy", None),
        P(ROWS_AXES, "sy", None),
    )
    return jax.shard_map(
        on_device,
        mesh=split,
        in_specs=placed,
        out_specs=(P(ROWS_AXES, "sy", None), P(ROWS_AXES, "sy", None)),
        check_vma=False,
    )
```

```python
import functools

import jax
import jax.numpy as jnp
from jax import lax
from jax.experimental import pallas as pl
from jax.experimental.pallas import tpu as pltpu
from jax.sharding import Mesh
from jax.sharding import PartitionSpec as P

ITERS = 3
LANES = 128
SLOT = 256
TILE = 8
CORNERS = 24
NDOF = 6
HIGHEST = lax.Precision.HIGHEST
VMEM = pl.BlockSpec(memory_space=pltpu.VMEM)
HBM = pl.BlockSpec(memory_space=pl.ANY)
LIMIT = 40 * 1024 * 1024

ROWS_AXES = ("z", "xl")
PLANE = ("xl", "sy")

RES, MUL, DIR, IFACE, PARTNER, MASK, SCAL, INNER, NSTATE = 0, 8, 16, 24, 32, 40, 48, 56, 64
GAMMA, LOAD, CARRY, ENERGY = 48, 49, 50, 51


def call(kernel, inputs, outputs, in_specs=None, out_specs=None, scratch=(), name=None):
    shapes = [shape if hasattr(shape, "dtype") else jax.ShapeDtypeStruct(shape, jnp.float32) for shape in outputs]
    return pl.pallas_call(
        kernel,
        out_shape=shapes,
        in_specs=in_specs or [VMEM] * len(inputs),
        out_specs=out_specs or [VMEM] * len(outputs),
        scratch_shapes=list(scratch),
        compiler_params=pltpu.CompilerParams(vmem_limit_bytes=LIMIT),
        name=name,
    )(*inputs)


def in_hbm(*arrays):
    return tuple(pltpu.with_memory_space_constraint(array, pltpu.HBM) for array in arrays)


def iota(shape, dim):
    return lax.broadcasted_iota(jnp.int32, shape, dim)


def as_tile(row):
    return jnp.concatenate([row[:, LANES * c : LANES * (c + 1)] for c in range(TILE)], axis=0)


def total(value):
    return jnp.sum(jnp.sum(value, axis=1, keepdims=True), axis=0, keepdims=True)


def slots(row, count, fill):
    width = row.shape[1]
    wide = jnp.broadcast_to(row, (TILE, width))
    lanes = iota((1, SLOT), 1)
    edge = SLOT * 3 // 4
    pieces = []
    for q in range(count):
        moved = wide if q == 0 else pltpu.roll(wide, width - edge * q, 1)
        pieces.append(jnp.where(lanes < edge, moved[0:1, 0:SLOT], fill))
    return pieces


def apply_matrix(tile, map_tile, map_row, matrix_ref):
    width = matrix_ref.shape[0]
    values = jnp.transpose(tile)
    places = jnp.transpose(map_tile)
    lanes = iota((LANES, LANES), 1)
    pieces = []
    for t in range(width // LANES):
        acc = jnp.zeros((LANES, LANES), jnp.float32)
        for c in range(TILE):
            hit = places[:, c : c + 1] == lanes + t * LANES
            acc = acc + jnp.where(hit, values[:, c : c + 1], 0.0)
        pieces.append(jnp.sum(acc, axis=0, keepdims=True))
    out = jnp.zeros((TILE, TILE * LANES), jnp.float32)
    for b in range(width // LANES):
        rows = slice(b * LANES, (b + 1) * LANES)
        acc = matrix_ref[rows, 0:LANES] * pieces[0]
        for t in range(1, width // LANES):
            acc = acc + matrix_ref[rows, t * LANES : (t + 1) * LANES] * pieces[t]
        column = jnp.sum(acc, axis=1, keepdims=True)
        for s in range(LANES // TILE):
            index = iota((TILE, TILE * LANES), 0) + (b * LANES + s * TILE)
            out = out + jnp.where(map_row == index, column[s * TILE : (s + 1) * TILE, :], 0.0)
    return jnp.sum(out, axis=0, keepdims=True)


def coarse_load(weighted, modes_ref, near_ref, rt_ref, l_ref, chunks):
    own = jnp.sum(modes_ref[...] * weighted, axis=1, keepdims=True)
    near = near_ref[...] * weighted
    loads = [own]
    for q in range(4):
        loads.append(-jnp.sum(near[:, SLOT * q : SLOT * (q + 1)], axis=1, keepdims=True))
    loads.append(jnp.zeros((LANES - 5 * CORNERS, 1), jnp.float32))
    column = jnp.concatenate(loads, axis=0)
    return jnp.dot(rt_ref[0:chunks, :], column * l_ref[...], precision=HIGHEST)


def plane_edges(tile, target, ncols):
    pair, col = target // ncols, target % ncols
    same = lax.axis_index("xl") == pair
    here = lax.axis_index("sy")
    first = jnp.where(
        same,
        jnp.where(here + 1 == col, tile[0:2], jnp.where(here - 1 == col, tile[4:6], 0.0)),
        jnp.where(here == col, tile[2:4], 0.0),
    )
    second = jnp.where(same, 0.0, jnp.where(here == col, tile[6:8], 0.0))
    return first, second


def plane_arrivals(arrived, row, ncols):
    pair, here = lax.axis_index("xl"), lax.axis_index("sy")
    base = pair * ncols
    east = arrived[base + jnp.minimum(here + 1, ncols - 1), row : row + 2, :]
    west = arrived[base + jnp.maximum(here - 1, 0), row : row + 2, :]
    other = (1 - pair) * ncols + here
    their_south = arrived[other, row : row + 2, :]
    their_north = arrived[other, row + 2 : row + 4, :]
    south = jnp.where(pair == 0, their_north, 0.0)
    north = jnp.where(pair == 0, 0.0, their_south)
    forward = jnp.where(pair == 0, their_south, their_north)
    return jnp.concatenate([east, south, west, north], axis=0), forward


def z_edge(forward, target):
    goal = jnp.where(lax.axis_index("xl") == 0, lax.axis_index("z") + 1, lax.axis_index("z") - 1)
    return jnp.where(goal == target, forward, 0.0)


def z_arrival(arrived, row, partner):
    levels = arrived.shape[0]
    pair, level = lax.axis_index("xl"), lax.axis_index("z")
    source = jnp.where(pair == 0, jnp.maximum(level - 1, 0), jnp.minimum(level + 1, levels - 1))
    edge = arrived[source, row : row + 2, :]
    south = jnp.where(pair == 0, partner[2:4], edge)
    north = jnp.where(pair == 0, edge, partner[6:8])
    return jnp.concatenate([partner[0:2], south, partner[4:6], north], axis=0)


def apply_schur(tile, map_tile, map_row, mask_row, schur_ref, modes_ref, near_ref, rt_ref, l_ref, out_ref, nrows):
    chunks = out_ref.shape[0]
    y_row = apply_matrix(tile, map_tile, map_row, schur_ref)
    load = coarse_load(0.25 * mask_row * y_row, modes_ref, near_ref, rt_ref, l_ref, nrows)
    y = as_tile(y_row)
    gamma = jnp.broadcast_to(0.25 * total(tile * y), (1, LANES))
    rest = jnp.zeros((2, LANES), jnp.float32)
    for p in range(chunks):
        first, second = plane_edges(y, p, chunks // 2)
        chunk = load[p : p + 1] if p < nrows else jnp.zeros((1, LANES), jnp.float32)
        out_ref[p, 0:TILE, :] = jnp.concatenate([chunk, gamma, first, second, rest], axis=0)
    return y


def pack_kernel(
    links_hbm, modes_hbm, map_hbm, gap_hbm, cmap_hbm, schur_hbm, out_modes, col_even, col_odd, row_pair, row_cross, out_own,
    out_row, out_tile, out_cmap, out_schur, links_ref, modes_ref, map_ref, gap_ref, cmap_ref, sems,
):
    copies = [
        pltpu.make_async_copy(source, target, sems.at[k])
        for k, (source, target) in enumerate(
            (
                (modes_hbm, modes_ref), (map_hbm, map_ref), (gap_hbm, gap_ref), (cmap_hbm, cmap_ref),
                (links_hbm, links_ref),
            )
        )
    ]
    matrix = pltpu.make_async_copy(schur_hbm.at[0, 0], out_schur, sems.at[len(copies)])
    for copy in copies:
        copy.start()
    matrix.start()
    for copy in copies:
        copy.wait()
    nrows, ncols = lax.axis_size("z") * lax.axis_size("xl"), lax.axis_size("sy")
    row_here = lax.axis_index("z") * lax.axis_size("xl") + lax.axis_index("xl")
    map_row = jnp.concatenate(slots(map_ref[0], 4, -1), axis=1)
    out_row[...] = map_row
    out_tile[...] = as_tile(map_row)
    width = modes_ref.shape[3]
    modes = jnp.concatenate([modes_ref[0, 0], jnp.zeros((8, width), jnp.float32)], axis=0)
    first = modes.astype(jnp.bfloat16)
    left = modes - first.astype(jnp.float32)
    second = left.astype(jnp.bfloat16)
    third = (left - second.astype(jnp.float32)).astype(jnp.bfloat16)
    acc = jnp.zeros((CORNERS + 8, TILE * LANES), jnp.float32)
    for b in range(width // LANES):
        cols = slice(b * LANES, (b + 1) * LANES)
        index = iota((LANES, TILE * LANES), 0) + b * LANES
        hit = jnp.where(map_row == index, 1.0, 0.0).astype(jnp.bfloat16)
        for part in (first, second, third):
            acc = acc + jnp.dot(part[:, cols], hit, preferred_element_type=jnp.float32)
    acc = acc[0:CORNERS]
    out_modes[...] = acc
    links = jnp.where(links_ref[0] == 1, 1.0, 0.0)
    east = jnp.where(lax.axis_index("sy") < ncols - 1, links[:, 0:1], 0.0)
    south = jnp.where(row_here < nrows - 1, links[:, 1:2], 0.0)
    gaps = slots(gap_ref[0], 2, 0.0)
    out_cmap[...] = jnp.zeros(out_cmap.shape, jnp.float32)
    out_cmap[0:1, 0:CORNERS] = cmap_ref[0].astype(jnp.float32)
    cmap = out_cmap[...]
    rest = jnp.zeros((5, SLOT), jnp.float32)
    none = jnp.zeros((1, SLOT), jnp.float32)
    parts = []
    own = []
    for q in range(4):
        values, mask = none, none
        if q < 2:
            mask = none + (east, south)[q]
            values = gaps[q] * mask
            own += [values, mask]
        parts.append(jnp.concatenate([acc[:, SLOT * q : SLOT * (q + 1)], values, mask, cmap, rest], axis=0))
    out_own[...] = jnp.concatenate(own + [jnp.zeros((4, SLOT), jnp.float32)], axis=0)
    even = lax.axis_index("sy") % 2 == 0
    first_row = lax.axis_index("xl") == 0
    col_even[...] = jnp.where(even, parts[0], parts[2])
    col_odd[...] = jnp.where(even, parts[2], parts[0])
    row_pair[...] = jnp.where(first_row, parts[1], parts[3])
    row_cross[...] = jnp.where(first_row, parts[3], parts[1])
    matrix.wait()


def load_kernel(coarse_hbm, blocks_out, coarse_ref, sem):
    coarse = pltpu.make_async_copy(coarse_hbm, coarse_ref, sem)
    coarse.start()
    coarse.wait()
    ncoarse = coarse_ref.shape[1]
    blocks_out[...] = jnp.zeros(blocks_out.shape, jnp.float32)
    for p in range(-(-ncoarse // LANES)):
        width = min(LANES, ncoarse - p * LANES)
        blocks_out[p, 0:NDOF, 0:width] = coarse_ref[:, p * LANES : p * LANES + width]


def start_kernel(
    nrows, own_ref, col_even, col_odd, row_pair, row_cross, cmap_ref, map_ref, map_tile_ref, schur_ref, modes_ref, blocks_ref, out_ref,
    state, near, r_ref, rt_ref, l_ref, mask_row_ref,
):
    chunks = out_ref.shape[0]
    row, cm = CORNERS, CORNERS + 2
    even = lax.axis_index("sy") % 2 == 0
    first_row = lax.axis_index("xl") == 0
    from_east = jnp.where(even, col_even[...], col_odd[...])
    from_west = jnp.where(even, col_odd[...], col_even[...])
    from_south = jnp.where(first_row, row_pair[...], row_cross[...])
    from_north = jnp.where(first_row, row_cross[...], row_pair[...])
    sources = (from_east, from_south, from_west, from_north)
    for q, part in enumerate(sources):
        near[:, SLOT * q : SLOT * (q + 1)] = part[0:CORNERS]
    values = [own_ref[0:1], own_ref[2:3], -from_west[row : row + 1], -from_north[row : row + 1]]
    masks = [own_ref[1:2], own_ref[3:4], from_west[row + 1 : row + 2], from_north[row + 1 : row + 2]]
    residual = as_tile(jnp.concatenate(values, axis=1))
    mask_row = jnp.concatenate(masks, axis=1)
    mask_row_ref[...] = mask_row
    maps = [cmap_ref[:, 0:LANES]] + [part[cm : cm + 1, 0:LANES] for part in sources]
    columns = jnp.transpose(jnp.concatenate(maps + [jnp.zeros((3, LANES), jnp.float32)], axis=0))
    column = [columns[0:CORNERS, g : g + 1] for g in range(5)]
    column.append(jnp.full((LANES - 5 * CORNERS, 1), float(nrows * LANES), jnp.float32))
    column = jnp.concatenate(column, axis=0)
    group = jnp.floor((column + 0.5) * (1.0 / LANES))
    inside = column - group * LANES
    lanes = iota((LANES, LANES), 1).astype(jnp.float32)
    hit_row = jnp.where((group == lanes) & (lanes < nrows), 1.0, 0.0)
    r_ref[...] = hit_row
    rt_ref[...] = jnp.transpose(hit_row)
    l_ref[...] = jnp.where(inside == lanes, 1.0, 0.0)
    y = apply_schur(
        residual, map_tile_ref[...], map_ref[...], mask_row, schur_ref, modes_ref, near, rt_ref, l_ref, out_ref, nrows
    )
    for p in range(chunks):
        out_ref[p, TILE : 2 * TILE, :] = blocks_ref[p]
    state[...] = jnp.zeros(state.shape, jnp.float32)
    state[RES : RES + TILE, :] = residual
    state[IFACE : IFACE + TILE, :] = y
    state[MASK : MASK + TILE, :] = as_tile(mask_row)


def rows_kernel(arrived, state_in, out_ref, state, own_block):
    chunks, levels = arrived.shape[0], out_ref.shape[0]
    summed = arrived[0, 0:TILE, :]
    for p in range(1, chunks):
        summed = summed + arrived[p, 0:TILE, :]
    partner, forward = plane_arrivals(arrived, 2, chunks // 2)
    state[...] = state_in[...]
    state[PARTNER : PARTNER + TILE, :] = partner
    for level in range(levels):
        out_ref[level] = jnp.concatenate([summed[0:2], z_edge(forward, level)], axis=0)
    block = jnp.concatenate([arrived[p, TILE : TILE + NDOF, :] for p in range(chunks)], axis=0)
    for k in range(own_block.shape[0]):
        own_block[k] = block[k * TILE : (k + 1) * TILE]


def first_direction_kernel(arrived, state_in, map_ref, map_tile_ref, kinv_ref, block_ref, out_ref, state):
    chunks, levels = out_ref.shape[0], arrived.shape[0]
    summed = arrived[0]
    for level in range(1, levels):
        summed = summed + arrived[level]
    partner = z_arrival(arrived, 2, state_in[PARTNER : PARTNER + TILE, :])
    direction = 0.25 * state_in[MASK : MASK + TILE, :] * (state_in[IFACE : IFACE + TILE, :] - partner)
    load = summed[0:1]
    gamma = summed[1:2]
    inner = as_tile(apply_matrix(direction, map_tile_ref[...], map_ref[...], kinv_ref))
    energy = jnp.broadcast_to(total(direction * inner), (1, LANES))
    place = iota((TILE, LANES), 1) - iota((TILE, LANES), 0) - lax.rem(lax.axis_index("z") * (NDOF * chunks), LANES)
    window = [jnp.zeros((TILE, LANES), jnp.float32)] * 2
    for k in range(block_ref.shape[0]):
        column = jnp.sum(block_ref[k] * load, axis=1, keepdims=True)
        window = [window[a] + jnp.where(place + a * LANES == k * TILE, column, 0.0) for a in range(2)]
    window = [jnp.sum(half, axis=0, keepdims=True) for half in window]
    for p in range(chunks):
        first, second = plane_edges(inner, p, chunks // 2)
        out_ref[p] = jnp.concatenate(window + [load, energy, first, second], axis=0)
    state[...] = state_in[...]
    state[DIR : DIR + TILE, :] = direction
    state[INNER : INNER + TILE, :] = inner
    state[SCAL : SCAL + TILE, :] = jnp.concatenate([gamma, load, jnp.zeros((6, LANES), jnp.float32)], axis=0)


def first_solve_kernel(arrived, state_in, out_ref, state, whole_load):
    chunks, levels = arrived.shape[0], out_ref.shape[0]
    size = NDOF * chunks
    summed = arrived[0]
    for p in range(1, chunks):
        summed = summed + arrived[p]
    for p in range(whole_load.shape[0]):
        whole_load[p : p + 1, :] = arrived[p, 2:3, :]
    partner, forward = plane_arrivals(arrived, 4, chunks // 2)
    state[...] = state_in[...]
    state[PARTNER : PARTNER + TILE, :] = partner
    begin = lax.rem(lax.axis_index("z") * size, LANES)
    places = iota((2, LANES), 1) + LANES * iota((2, LANES), 0) - begin
    window = jnp.where((places >= 0) & (places < size), summed[0:2], summed[3:4])
    for level in range(levels):
        out_ref[level] = jnp.concatenate([window, z_edge(forward, level)], axis=0)


def first_image_parts(arrived, state_in, whole_load):
    levels, nrows = arrived.shape[0], whole_load.shape[0]
    size = NDOF * 2 * lax.axis_size("sy")
    energy = jnp.zeros((1, 1), jnp.float32)
    rows = [jnp.zeros((1, LANES), jnp.float32)] * (nrows + 2)
    lanes = iota((1, LANES), 1)
    for level in range(levels):
        base, begin = divmod(level * size, LANES)
        for a in range(2):
            places = lanes + (a * LANES - begin)
            values = arrived[level, a : a + 1, :]
            rows[base + a] = rows[base + a] + jnp.where((places >= 0) & (places < size), values, 0.0)
        if begin + size < 2 * LANES:
            energy = energy + arrived[level, 1:2, LANES - 1 : LANES]
        else:
            energy = energy + arrived[level, 0:1, 0:1]
    partner = z_arrival(arrived, 2, state_in[PARTNER : PARTNER + TILE, :])
    return energy, partner, whole_load[...], jnp.concatenate(rows[0:nrows], axis=0)


def with_crossing(partner, crossed):
    pair = lax.axis_index("xl")
    south = jnp.where(pair == 0, partner[2:4], crossed[6:8])
    north = jnp.where(pair == 0, crossed[2:4], partner[6:8])
    return jnp.concatenate([partner[0:2], south, partner[4:6], north], axis=0)


def inner_kernel(arrived, crossed, state_in, map_ref, map_tile_ref, kinv_ref, out_ref, state):
    chunks, levels = arrived.shape[0], out_ref.shape[0]
    summed = arrived[0]
    for p in range(1, chunks):
        summed = summed + arrived[p]
    partner, _ = plane_arrivals(arrived, 2, chunks // 2)
    partner = with_crossing(partner, crossed[...])
    z = 0.25 * state_in[MASK : MASK + TILE, :] * (state_in[IFACE : IFACE + TILE, :] - partner)
    inner = as_tile(apply_matrix(z, map_tile_ref[...], map_ref[...], kinv_ref))
    own = jnp.broadcast_to(total(z * inner), (1, LANES))
    mixed = z * state_in[INNER : INNER + TILE, :] + state_in[DIR : DIR + TILE, :] * inner
    mixed = jnp.broadcast_to(total(mixed), (1, LANES))
    message = jnp.concatenate([summed[0:2], own, mixed], axis=0)
    for level in range(levels):
        out_ref[level] = message
    state[...] = state_in[...]
    state[IFACE : IFACE + TILE, :] = inner
    state[PARTNER : PARTNER + TILE, :] = z


def direction_kernel(arrived, state_in, columns_ref, out_ref, state, crossing):
    chunks, levels = out_ref.shape[0], arrived.shape[0]
    summed = arrived[0]
    for level in range(1, levels):
        summed = summed + arrived[level]
    gamma = summed[1:2]
    beta = gamma / state_in[GAMMA : GAMMA + 1, :]
    direction = state_in[PARTNER : PARTNER + TILE, :] + beta * state_in[DIR : DIR + TILE, :]
    inner = state_in[IFACE : IFACE + TILE, :] + beta * state_in[INNER : INNER + TILE, :]
    load = summed[0:1] + beta * state_in[LOAD : LOAD + 1, :]
    energy = summed[2:3] + beta * summed[3:4]
    carry = beta * beta * state_in[ENERGY : ENERGY + 1, :]
    place = iota((TILE, LANES), 1) - iota((TILE, LANES), 0)
    groups = columns_ref.shape[0]
    per_row = LANES // TILE
    message = []
    for r in range(-(-groups // per_row)):
        acc = jnp.zeros((TILE, LANES), jnp.float32)
        for k in range(min(per_row, groups - r * per_row)):
            column = jnp.sum(columns_ref[r * per_row + k] * load, axis=1, keepdims=True)
            acc = acc + jnp.where(place == k * TILE, column, 0.0)
        message.append(jnp.sum(acc, axis=0, keepdims=True))
    message += [load, energy]
    rest = out_ref.shape[1] - len(message) - 4
    for p in range(chunks):
        first, second = plane_edges(inner, p, chunks // 2)
        tail = [jnp.zeros((rest, LANES), jnp.float32)] if rest else []
        out_ref[p] = jnp.concatenate(message + [first, second] + tail, axis=0)
    crossing[...] = inner
    state[...] = state_in[...]
    state[DIR : DIR + TILE, :] = direction
    state[INNER : INNER + TILE, :] = inner
    state[SCAL : SCAL + TILE, :] = jnp.concatenate([gamma, load, carry, jnp.zeros((5, LANES), jnp.float32)], axis=0)


def image_parts(arrived, state_in, crossed, nrows):
    chunks = arrived.shape[0]
    summed = arrived[0]
    for p in range(1, chunks):
        summed = summed + arrived[p]
    energy = summed[nrows + 1 : nrows + 2, 0:1] + state_in[CARRY : CARRY + 1, 0:1]
    partner, _ = plane_arrivals(arrived, nrows + 2, chunks // 2)
    partner = with_crossing(partner, crossed[...])
    load = jnp.concatenate([arrived[p, nrows : nrows + 1, :] for p in range(nrows)], axis=0)
    return energy, partner, load, summed[0:nrows]


def advance(parts, state_in, modes_ref, near_ref, r_ref, l_ref):
    inner_energy, partner, load, solved = parts
    energy = inner_energy + total(load * solved)
    alpha = state_in[GAMMA : GAMMA + 1, :] / energy
    found = jnp.dot(r_ref[:, 0 : solved.shape[0]], solved, precision=HIGHEST)
    corners = jnp.sum(found * l_ref[...], axis=1, keepdims=True)
    coarse = jnp.sum(corners[0:CORNERS] * modes_ref[...], axis=0, keepdims=True)
    near = []
    for q in range(4):
        values = corners[CORNERS * (q + 1) : CORNERS * (q + 2)]
        near.append(jnp.sum(values * near_ref[:, SLOT * q : SLOT * (q + 1)], axis=0, keepdims=True))
    coarse = as_tile(coarse - jnp.concatenate(near, axis=1))
    image = state_in[MASK : MASK + TILE, :] * (state_in[INNER : INNER + TILE, :] - partner + coarse)
    multipliers = state_in[MUL : MUL + TILE, :] + alpha * state_in[DIR : DIR + TILE, :]
    residual = state_in[RES : RES + TILE, :] - alpha * image
    return multipliers, residual


def next_kernel(
    step, nrows, arrived, extra, state_in, modes_ref, near_ref, r_ref, l_ref, rt_ref, mask_row_ref, map_ref, map_tile_ref,
    schur_ref, out_ref, state, crossing,
):
    parts = image_parts(arrived, state_in, extra, nrows) if step else first_image_parts(arrived, state_in, extra)
    multipliers, residual = advance(parts, state_in, modes_ref, near_ref, r_ref, l_ref)
    y = apply_schur(
        residual, map_tile_ref[...], map_ref[...], mask_row_ref[...], schur_ref, modes_ref, near_ref, rt_ref, l_ref, out_ref,
        nrows,
    )
    crossing[...] = y
    state[...] = state_in[...]
    state[RES : RES + TILE, :] = residual
    state[MUL : MUL + TILE, :] = multipliers
    state[IFACE : IFACE + TILE, :] = y
    state[ENERGY : ENERGY + 1, :] = jnp.broadcast_to(parts[0], (1, LANES))


def last_kernel(
    nrows, arrived, crossed, state_in, modes_ref, near_ref, r_ref, l_ref, out_multipliers, out_residual, scratch, sems
):
    parts = image_parts(arrived, state_in, crossed, nrows)
    results = advance(parts, state_in, modes_ref, near_ref, r_ref, l_ref)
    width = scratch.shape[3]
    none = jnp.zeros((1, width - SLOT), jnp.float32)
    lanes = iota((1, width), 1)
    copies = []
    for k, (tile, target) in enumerate(zip(results, (out_multipliers, out_residual))):
        east = jnp.concatenate([tile[0:1], tile[1:2], none], axis=1)
        south = jnp.concatenate([tile[2:3], tile[3:4], none], axis=1)
        south = pltpu.roll(jnp.broadcast_to(south, (TILE, width)), width // 2, 1)[0:1]
        scratch[k, 0] = jnp.where(lanes < width // 2, east, south)
        copies.append(pltpu.make_async_copy(scratch.at[k], target, sems.at[k]))
        copies[k].start()
    for copy in copies:
        copy.wait()


def swapped(block, axis, first):
    count = lax.axis_size(axis)
    route = []
    for i in range(first, count - 1, 2):
        route += [(i, i + 1), (i + 1, i)]
    return lax.ppermute(block, axis, route)


def on_device(gap, kinv, schur, corner_modes, coarse_inverse, edge_map, corner_map, links):
    levels, chunks = lax.axis_size("z"), lax.axis_size("xl") * lax.axis_size("sy")
    width = kinv.shape[-1]
    kinv = kinv.reshape(width, width)
    ints = jnp.int32
    own_modes, col_even, col_odd, row_pair, row_cross, own, map_row, map_tile, cmap, schur = call(
        pack_kernel,
        in_hbm(links, corner_modes, edge_map, gap, corner_map, schur),
        [(CORNERS, TILE * LANES)]
        + [(CORNERS + 8, SLOT)] * 4
        + [(TILE, SLOT), jax.ShapeDtypeStruct((1, TILE * LANES), ints), jax.ShapeDtypeStruct((TILE, LANES), ints)]
        + [(1, SLOT), (width, width)],
        in_specs=[HBM] * 6,
        scratch=[
            pltpu.VMEM(links.shape, ints),
            pltpu.VMEM(corner_modes.shape, jnp.float32),
            pltpu.VMEM(edge_map.shape, ints),
            pltpu.VMEM(gap.shape, jnp.float32),
            pltpu.VMEM(corner_map.shape, ints),
            pltpu.SemaphoreType.DMA((6,)),
        ],
        name="pack",
    )
    col_even = swapped(col_even, "sy", 0)
    col_odd = swapped(col_odd, "sy", 1)
    row_pair = swapped(row_pair, ROWS_AXES, 0)
    row_cross = swapped(row_cross, ROWS_AXES, 1)
    (blocks,) = call(
        load_kernel,
        in_hbm(coarse_inverse),
        [(chunks, TILE, LANES)],
        in_specs=[HBM],
        scratch=[pltpu.VMEM(coarse_inverse.shape, jnp.float32), pltpu.SemaphoreType.DMA(())],
        name="load",
    )
    square = (LANES, LANES)
    state_shape = (NSTATE, LANES)
    ncoarse = coarse_inverse.shape[1]
    nrows = -(-ncoarse // LANES)
    to_plane, to_z = (chunks, TILE, LANES), (levels, 4, LANES)
    to_plane_whole = (chunks, -(-(nrows + 6) // TILE) * TILE, LANES)
    tile_shape = (TILE, LANES)
    out, state, near, r, rt, l, mask_row = call(
        functools.partial(start_kernel, nrows),
        (
            own, col_even, col_odd, row_pair, row_cross, cmap, map_row, map_tile, schur, own_modes, blocks,
        ),
        [(chunks, 2 * TILE, LANES), state_shape, (CORNERS, TILE * LANES), square, square, square, (1, TILE * LANES)],
        name="start",
    )
    for step in range(ITERS):
        arrived = lax.all_to_all(out, PLANE, 0, 0, tiled=True)
        if step == 0:
            out, state, block = call(
                rows_kernel,
                (arrived, state),
                [to_z, state_shape, (ncoarse // levels // TILE, TILE, LANES)],
                name="rows",
            )
            columns = lax.all_gather(block, "z", axis=0, tiled=True)
            arrived = lax.all_to_all(out, "z", 0, 0, tiled=True)
            out, state = call(
                first_direction_kernel,
                (arrived, state, map_row, map_tile, kinv, block),
                [to_plane, state_shape],
                name="first_direction",
            )
            arrived = lax.all_to_all(out, PLANE, 0, 0, tiled=True)
            out, state, extra = call(
                first_solve_kernel, (arrived, state), [to_z, state_shape, (nrows, LANES)], name="first_solve"
            )
            arrived = lax.all_to_all(out, "z", 0, 0, tiled=True)
        else:
            crossed = swapped(crossing, ROWS_AXES, 1)
            out, state = call(
                inner_kernel, (arrived, crossed, state, map_row, map_tile, kinv), [to_z, state_shape], name="inner"
            )
            arrived = lax.all_to_all(out, "z", 0, 0, tiled=True)
            out, state, crossing = call(
                direction_kernel, (arrived, state, columns), [to_plane_whole, state_shape, tile_shape], name="direction"
            )
            extra = swapped(crossing, ROWS_AXES, 1)
            arrived = lax.all_to_all(out, PLANE, 0, 0, tiled=True)
        common = (arrived, extra, state, own_modes, near, r, l)
        if step + 1 < ITERS:
            out, state, crossing = call(
                functools.partial(next_kernel, step, nrows),
                common + (rt, mask_row, map_row, map_tile, schur),
                [to_plane, state_shape, tile_shape],
                name="next",
            )
    return tuple(
        call(
            functools.partial(last_kernel, nrows),
            common,
            [gap.shape] * 2,
            out_specs=[HBM] * 2,
            scratch=[pltpu.VMEM((2,) + gap.shape, jnp.float32), pltpu.SemaphoreType.DMA((2,))],
            name="last",
        )
    )


def solution(mesh):
    rows, cols = mesh.devices.shape
    split = Mesh(mesh.devices.reshape(rows // 2, 2, cols), ("z", "xl", "sy"))
    placed = (
        P(ROWS_AXES, "sy", None),
        P(ROWS_AXES, "sy", None, None),
        P(ROWS_AXES, "sy", None, None),
        P(ROWS_AXES, "sy", None, None),
        P(("z", "xl", "sy"), None),
        P(ROWS_AXES, "sy", None),
        P(ROWS_AXES, "sy", None),
        P(ROWS_AXES, "sy", None),
    )
    return jax.shard_map(
        on_device,
        mesh=split,
        in_specs=placed,
        out_specs=(P(ROWS_AXES, "sy", None), P(ROWS_AXES, "sy", None)),
        check_vma=False,
    )
```

```python
import jax
import jax.numpy as jnp
from jax import lax
from jax.experimental import pallas as pl
from jax.experimental.pallas import tpu as pltpu
from jax.sharding import Mesh
from jax.sharding import PartitionSpec as P

ITERS = 3
LANES = 128
SLOT = 256
TILE = 8
CORNERS = 24
NDOF = 6
HIGHEST = lax.Precision.HIGHEST
VMEM = pl.BlockSpec(memory_space=pltpu.VMEM)
HBM = pl.BlockSpec(memory_space=pl.ANY)
LIMIT = 40 * 1024 * 1024

ROWS_AXES = ("z", "xl")
PLANE = ("xl", "sy")

RES, MUL, DIR, IFACE, PARTNER, MASK, SCAL, NSTATE = 0, 8, 16, 24, 32, 40, 48, 56
GAMMA, LOAD = 48, 49


def call(kernel, inputs, outputs, in_specs=None, out_specs=None, scratch=(), name=None):
    shapes = [shape if hasattr(shape, "dtype") else jax.ShapeDtypeStruct(shape, jnp.float32) for shape in outputs]
    return pl.pallas_call(
        kernel,
        out_shape=shapes,
        in_specs=in_specs or [VMEM] * len(inputs),
        out_specs=out_specs or [VMEM] * len(outputs),
        scratch_shapes=list(scratch),
        compiler_params=pltpu.CompilerParams(vmem_limit_bytes=LIMIT),
        name=name,
    )(*inputs)


def in_hbm(*arrays):
    return tuple(pltpu.with_memory_space_constraint(array, pltpu.HBM) for array in arrays)


def iota(shape, dim):
    return lax.broadcasted_iota(jnp.int32, shape, dim)


def as_row(tile):
    return jnp.concatenate([tile[c : c + 1, :] for c in range(TILE)], axis=1)


def as_tile(row):
    return jnp.concatenate([row[:, LANES * c : LANES * (c + 1)] for c in range(TILE)], axis=0)


def total(value):
    return jnp.sum(jnp.sum(value, axis=1, keepdims=True), axis=0, keepdims=True)


def slots(row, count, fill):
    width = row.shape[1]
    wide = jnp.broadcast_to(row, (TILE, width))
    lanes = iota((1, SLOT), 1)
    edge = SLOT * 3 // 4
    pieces = []
    for q in range(count):
        moved = wide if q == 0 else pltpu.roll(wide, width - edge * q, 1)
        pieces.append(jnp.where(lanes < edge, moved[0:1, 0:SLOT], fill))
    return pieces


def bf16_parts(value):
    first = value.astype(jnp.bfloat16).astype(jnp.float32)
    left = value - first
    second = left.astype(jnp.bfloat16).astype(jnp.float32)
    return jnp.concatenate([first, second, left - second], axis=0)


def apply_matrix(tile, group_row, hits, matrix_ref):
    width = matrix_ref.shape[0]
    ours = group_row == iota((TILE, TILE * LANES), 0)
    none = jnp.zeros((TILE, TILE * LANES), jnp.float32)
    parts = bf16_parts(jnp.where(ours, as_row(tile), 0.0))
    parts = jnp.concatenate([parts, none], axis=0).astype(jnp.bfloat16)
    local = lax.dot_general(parts, hits, (((1,), (1,)), ((), ())), preferred_element_type=jnp.float32)
    local = local[0:TILE] + local[TILE : 2 * TILE] + local[2 * TILE : 3 * TILE]
    place = iota((TILE, LANES), 1) - iota((TILE, LANES), 0)
    rows = []
    for b in range(width // LANES):
        block = slice(b * LANES, (b + 1) * LANES)
        acc = matrix_ref[block, 0:LANES] * local[0:1]
        for t in range(1, width // LANES):
            acc = acc + matrix_ref[block, t * LANES : (t + 1) * LANES] * local[t : t + 1]
        column = jnp.sum(acc, axis=1, keepdims=True)
        row = jnp.zeros((TILE, LANES), jnp.float32)
        for k in range(LANES // TILE):
            row = row + jnp.where(place == k * TILE, column[k * TILE : (k + 1) * TILE], 0.0)
        rows.append(jnp.sum(row, axis=0, keepdims=True))
    rows.append(jnp.zeros((TILE - len(rows), LANES), jnp.float32))
    parts = bf16_parts(jnp.concatenate(rows, axis=0))
    parts = jnp.concatenate([parts, jnp.zeros((TILE, LANES), jnp.float32)], axis=0).astype(jnp.bfloat16)
    found = jnp.dot(parts, hits, preferred_element_type=jnp.float32)
    found = found[0:TILE] + found[TILE : 2 * TILE] + found[2 * TILE : 3 * TILE]
    return jnp.sum(jnp.where(ours, found, 0.0), axis=0, keepdims=True)


def coarse_load(weighted, modes_ref, near_ref, rt_ref, l_ref, chunks):
    own = jnp.sum(modes_ref[...] * weighted, axis=1, keepdims=True)
    near = near_ref[...] * weighted
    loads = [own]
    for q in range(4):
        loads.append(-jnp.sum(near[:, SLOT * q : SLOT * (q + 1)], axis=1, keepdims=True))
    loads.append(jnp.zeros((LANES - 5 * CORNERS, 1), jnp.float32))
    column = jnp.concatenate(loads, axis=0)
    return jnp.dot(rt_ref[0:chunks, :], column * l_ref[...], precision=HIGHEST)


def plane_edges(tile, target, ncols):
    pair, col = target // ncols, target % ncols
    same = lax.axis_index("xl") == pair
    here = lax.axis_index("sy")
    first = jnp.where(
        same,
        jnp.where(here + 1 == col, tile[0:2], jnp.where(here - 1 == col, tile[4:6], 0.0)),
        jnp.where(here == col, tile[2:4], 0.0),
    )
    second = jnp.where(same, 0.0, jnp.where(here == col, tile[6:8], 0.0))
    return first, second


def plane_arrivals(arrived, row, ncols):
    pair, here = lax.axis_index("xl"), lax.axis_index("sy")
    base = pair * ncols
    east = arrived[base + jnp.minimum(here + 1, ncols - 1), row : row + 2, :]
    west = arrived[base + jnp.maximum(here - 1, 0), row : row + 2, :]
    other = (1 - pair) * ncols + here
    their_south = arrived[other, row : row + 2, :]
    their_north = arrived[other, row + 2 : row + 4, :]
    south = jnp.where(pair == 0, their_north, 0.0)
    north = jnp.where(pair == 0, 0.0, their_south)
    forward = jnp.where(pair == 0, their_south, their_north)
    return jnp.concatenate([east, south, west, north], axis=0), forward


def z_edge(forward, target):
    goal = jnp.where(lax.axis_index("xl") == 0, lax.axis_index("z") + 1, lax.axis_index("z") - 1)
    return jnp.where(goal == target, forward, 0.0)


def z_arrival(arrived, row, partner):
    levels = arrived.shape[0]
    pair, level = lax.axis_index("xl"), lax.axis_index("z")
    source = jnp.where(pair == 0, jnp.maximum(level - 1, 0), jnp.minimum(level + 1, levels - 1))
    edge = arrived[source, row : row + 2, :]
    south = jnp.where(pair == 0, partner[2:4], edge)
    north = jnp.where(pair == 0, edge, partner[6:8])
    return jnp.concatenate([partner[0:2], south, partner[4:6], north], axis=0)


def apply_schur(tile, group_row, hits, mask_row, schur_ref, modes_ref, near_ref, rt_ref, l_ref, out_ref):
    chunks = out_ref.shape[0]
    y_row = apply_matrix(tile, group_row, hits, schur_ref)
    load = coarse_load(0.25 * mask_row * y_row, modes_ref, near_ref, rt_ref, l_ref, chunks)
    y = as_tile(y_row)
    gamma = jnp.broadcast_to(0.25 * total(tile * y), (1, LANES))
    rest = jnp.zeros((2, LANES), jnp.float32)
    for p in range(chunks):
        first, second = plane_edges(y, p, chunks // 2)
        out_ref[p, 0:TILE, :] = jnp.concatenate([load[p : p + 1], gamma, first, second, rest], axis=0)
    return y


def pack_kernel(
    links_hbm, modes_hbm, map_hbm, gap_hbm, cmap_hbm, schur_hbm, out_modes, col_even, col_odd, row_pair, row_cross, out_own,
    out_group, out_hits, out_cmap, out_schur, links_ref, modes_ref, map_ref, gap_ref, cmap_ref, sems,
):
    copies = [
        pltpu.make_async_copy(source, target, sems.at[k])
        for k, (source, target) in enumerate(
            (
                (modes_hbm, modes_ref), (map_hbm, map_ref), (gap_hbm, gap_ref), (cmap_hbm, cmap_ref),
                (links_hbm, links_ref),
            )
        )
    ]
    matrix = pltpu.make_async_copy(schur_hbm.at[0, 0], out_schur, sems.at[len(copies)])
    for copy in copies:
        copy.start()
    matrix.start()
    for copy in copies:
        copy.wait()
    nrows, ncols = lax.axis_size("z") * lax.axis_size("xl"), lax.axis_size("sy")
    row_here = lax.axis_index("z") * lax.axis_size("xl") + lax.axis_index("xl")
    map_row = jnp.concatenate(slots(map_ref[0], 4, -1), axis=1)
    group = lax.shift_right_arithmetic(map_row, 7)
    out_group[...] = group
    hits = jnp.where(map_row - LANES * group == iota((LANES, TILE * LANES), 0), 1.0, 0.0)
    hits = jnp.where(group >= 0, hits, 0.0).astype(jnp.bfloat16)
    out_hits[...] = hits
    count = modes_ref.shape[3] // LANES
    parts = [modes_ref[0, 0, :, t * LANES : (t + 1) * LANES] for t in range(count)]
    parts = bf16_parts(jnp.concatenate(parts, axis=0)).astype(jnp.bfloat16)
    found = jnp.dot(parts, hits, preferred_element_type=jnp.float32)
    acc = jnp.zeros((CORNERS, TILE * LANES), jnp.float32)
    for t in range(count):
        pieces = [found[(count * k + t) * CORNERS : (count * k + t + 1) * CORNERS] for k in range(3)]
        acc = acc + jnp.where(group == t, pieces[0] + pieces[1] + pieces[2], 0.0)
    out_modes[...] = acc
    links = jnp.where(links_ref[0] == 1, 1.0, 0.0)
    east = jnp.where(lax.axis_index("sy") < ncols - 1, links[:, 0:1], 0.0)
    south = jnp.where(row_here < nrows - 1, links[:, 1:2], 0.0)
    gaps = slots(gap_ref[0], 2, 0.0)
    out_cmap[...] = jnp.zeros(out_cmap.shape, jnp.float32)
    out_cmap[0:1, 0:CORNERS] = cmap_ref[0].astype(jnp.float32)
    cmap = out_cmap[...]
    rest = jnp.zeros((5, SLOT), jnp.float32)
    none = jnp.zeros((1, SLOT), jnp.float32)
    parts = []
    own = []
    for q in range(4):
        values, mask = none, none
        if q < 2:
            mask = none + (east, south)[q]
            values = gaps[q] * mask
            own += [values, mask]
        parts.append(jnp.concatenate([acc[:, SLOT * q : SLOT * (q + 1)], values, mask, cmap, rest], axis=0))
    out_own[...] = jnp.concatenate(own + [jnp.zeros((4, SLOT), jnp.float32)], axis=0)
    even = lax.axis_index("sy") % 2 == 0
    first_row = lax.axis_index("xl") == 0
    col_even[...] = jnp.where(even, parts[0], parts[2])
    col_odd[...] = jnp.where(even, parts[2], parts[0])
    row_pair[...] = jnp.where(first_row, parts[1], parts[3])
    row_cross[...] = jnp.where(first_row, parts[3], parts[1])
    matrix.wait()


def column_chunk(coarse, p, block):
    start = block * p // LANES * LANES
    window = coarse[:, start : start + SLOT]
    shift = block * p - start
    if shift:
        window = pltpu.roll(window, SLOT - shift, 1)
    return jnp.where(iota((TILE, LANES), 1) < block, window[:, 0:LANES], 0.0)


def start_kernel(
    own_ref, row_cross, col_odd, row_pair, col_even, cmap_ref, group_ref, hits_ref, schur_ref, modes_ref, coarse_hbm, out_ref,
    state, near, r_ref, rt_ref, l_ref, mask_row_ref, coarse_ref, sem,
):
    copy = pltpu.make_async_copy(coarse_hbm, coarse_ref, sem)
    copy.start()
    chunks = out_ref.shape[0]
    block = NDOF * chunks // 2
    row, cm = CORNERS, CORNERS + 2
    even = lax.axis_index("sy") % 2 == 0
    first_row = lax.axis_index("xl") == 0
    from_east = jnp.where(even, col_even[...], col_odd[...])
    from_west = jnp.where(even, col_odd[...], col_even[...])
    from_south = jnp.where(first_row, row_pair[...], row_cross[...])
    from_north = jnp.where(first_row, row_cross[...], row_pair[...])
    sources = (from_east, from_south, from_west, from_north)
    for q, part in enumerate(sources):
        near[:, SLOT * q : SLOT * (q + 1)] = part[0:CORNERS]
    values = [own_ref[0:1], own_ref[2:3], -from_west[row : row + 1], -from_north[row : row + 1]]
    masks = [own_ref[1:2], own_ref[3:4], from_west[row + 1 : row + 2], from_north[row + 1 : row + 2]]
    residual = as_tile(jnp.concatenate(values, axis=1))
    mask_row = jnp.concatenate(masks, axis=1)
    mask_row_ref[...] = mask_row
    maps = [cmap_ref[:, 0:LANES]] + [part[cm : cm + 1, 0:LANES] for part in sources]
    columns = jnp.transpose(jnp.concatenate(maps + [jnp.zeros((3, LANES), jnp.float32)], axis=0))
    column = [columns[0:CORNERS, g : g + 1] for g in range(5)]
    column.append(jnp.full((LANES - 5 * CORNERS, 1), float(block * chunks), jnp.float32))
    column = jnp.concatenate(column, axis=0)
    group = jnp.floor((column + 0.5) * (1.0 / block))
    inside = column - group * block
    lanes = iota((LANES, LANES), 1).astype(jnp.float32)
    hit_row = jnp.where((group == lanes) & (lanes < chunks), 1.0, 0.0)
    r_ref[...] = hit_row
    rt_ref[...] = jnp.transpose(hit_row)
    l_ref[...] = jnp.where(inside == lanes, 1.0, 0.0)
    y = apply_schur(residual, group_ref[...], hits_ref[...], mask_row, schur_ref, modes_ref, near, rt_ref, l_ref, out_ref)
    copy.wait()
    ncoarse = coarse_ref.shape[1]
    wide = (-(-ncoarse // LANES) + 1) * LANES
    coarse = jnp.concatenate([coarse_ref[...], jnp.zeros((TILE - NDOF, ncoarse), jnp.float32)], axis=0)
    coarse = jnp.pad(coarse, ((0, 0), (0, wide - ncoarse)))
    for p in range(chunks):
        out_ref[p, TILE : 2 * TILE, :] = column_chunk(coarse, p, block)
    state[...] = jnp.zeros(state.shape, jnp.float32)
    state[RES : RES + TILE, :] = residual
    state[IFACE : IFACE + TILE, :] = y
    state[MASK : MASK + TILE, :] = as_tile(mask_row)


def rows_kernel(arrived, state_in, out_ref, state):
    chunks, levels = arrived.shape[0], out_ref.shape[0]
    summed = arrived[0, 0:TILE, :]
    for p in range(1, chunks):
        summed = summed + arrived[p, 0:TILE, :]
    partner, forward = plane_arrivals(arrived, 2, chunks // 2)
    state[...] = state_in[...]
    state[PARTNER : PARTNER + TILE, :] = partner
    for level in range(levels):
        out_ref[level] = jnp.concatenate([summed[0:2], z_edge(forward, level)], axis=0)


def direction_kernel(step, arrived, state_in, group_ref, hits_ref, kinv_ref, blocks_ref, out_ref, state):
    chunks, levels = out_ref.shape[0], arrived.shape[0]
    half = chunks // 2
    summed = arrived[0]
    for level in range(1, levels):
        summed = summed + arrived[level]
    partner = z_arrival(arrived, 2, state_in[PARTNER : PARTNER + TILE, :])
    direction = 0.25 * state_in[MASK : MASK + TILE, :] * (state_in[IFACE : IFACE + TILE, :] - partner)
    load = summed[0:1]
    gamma = summed[1:2]
    if step:
        beta = gamma / state_in[GAMMA : GAMMA + 1, :]
        direction = direction + beta * state_in[DIR : DIR + TILE, :]
        load = load + beta * state_in[LOAD : LOAD + 1, :]
    inner = as_tile(apply_matrix(direction, group_ref[...], hits_ref[...], kinv_ref))
    energy = jnp.broadcast_to(total(direction * inner), (1, LANES))
    lanes = iota((TILE, LANES), 1)
    dof = iota((TILE, LANES), 0)
    solved = []
    for a in range(2):
        acc = jnp.zeros((TILE, LANES), jnp.float32)
        for p in range(half):
            column = jnp.sum(blocks_ref[a * half + p, TILE : 2 * TILE, :] * load, axis=1, keepdims=True)
            acc = acc + jnp.where((lanes == dof + p * NDOF) & (dof < NDOF), column, 0.0)
        solved.append(jnp.sum(acc, axis=0, keepdims=True))
    for p in range(chunks):
        first, second = plane_edges(inner, p, half)
        out_ref[p] = jnp.concatenate(solved + [load, energy, first, second], axis=0)
    state[...] = state_in[...]
    state[DIR : DIR + TILE, :] = direction
    state[IFACE : IFACE + TILE, :] = inner
    state[SCAL : SCAL + TILE, :] = jnp.concatenate([gamma, load, jnp.zeros((6, LANES), jnp.float32)], axis=0)


def solve_kernel(arrived, state_in, out_ref, state, whole_load):
    chunks, levels = arrived.shape[0], out_ref.shape[0]
    block = NDOF * chunks // 2
    summed = arrived[0]
    for p in range(1, chunks):
        summed = summed + arrived[p]
    whole_load[...] = jnp.concatenate([arrived[p, 2:3, :] for p in range(chunks)], axis=0)
    partner, forward = plane_arrivals(arrived, 4, chunks // 2)
    state[...] = state_in[...]
    state[PARTNER : PARTNER + TILE, :] = partner
    first = jnp.where(iota((1, LANES), 1) < block, summed[0:1], summed[3:4])
    for level in range(levels):
        out_ref[level] = jnp.concatenate([first, summed[1:2], z_edge(forward, level)], axis=0)


def advance(arrived, state_in, whole_load, modes_ref, near_ref, r_ref, l_ref):
    levels = arrived.shape[0]
    energy = arrived[0, 0:1, :]
    for level in range(1, levels):
        energy = energy + arrived[level, 0:1, :]
    partner = z_arrival(arrived, 2, state_in[PARTNER : PARTNER + TILE, :])
    solved = jnp.concatenate([arrived[level, 0:2, :] for level in range(levels)], axis=0)
    energy = energy[:, LANES - 1 : LANES] + total(whole_load[...] * solved)
    alpha = state_in[GAMMA : GAMMA + 1, :] / energy
    found = jnp.dot(r_ref[:, 0 : 2 * levels], solved, precision=HIGHEST)
    corners = jnp.sum(found * l_ref[...], axis=1, keepdims=True)
    coarse = jnp.sum(corners[0:CORNERS] * modes_ref[...], axis=0, keepdims=True)
    near = []
    for q in range(4):
        values = corners[CORNERS * (q + 1) : CORNERS * (q + 2)]
        near.append(jnp.sum(values * near_ref[:, SLOT * q : SLOT * (q + 1)], axis=0, keepdims=True))
    coarse = as_tile(coarse - jnp.concatenate(near, axis=1))
    image = state_in[MASK : MASK + TILE, :] * (state_in[IFACE : IFACE + TILE, :] - partner + coarse)
    multipliers = state_in[MUL : MUL + TILE, :] + alpha * state_in[DIR : DIR + TILE, :]
    residual = state_in[RES : RES + TILE, :] - alpha * image
    return multipliers, residual


def next_kernel(
    arrived, state_in, whole_load, modes_ref, near_ref, r_ref, l_ref, rt_ref, mask_row_ref, group_ref, hits_ref, schur_ref,
    out_ref, state,
):
    multipliers, residual = advance(arrived, state_in, whole_load, modes_ref, near_ref, r_ref, l_ref)
    y = apply_schur(
        residual, group_ref[...], hits_ref[...], mask_row_ref[...], schur_ref, modes_ref, near_ref, rt_ref, l_ref, out_ref
    )
    state[...] = state_in[...]
    state[RES : RES + TILE, :] = residual
    state[MUL : MUL + TILE, :] = multipliers
    state[IFACE : IFACE + TILE, :] = y


def last_kernel(
    arrived, state_in, whole_load, modes_ref, near_ref, r_ref, l_ref, out_multipliers, out_residual, scratch, sems
):
    results = advance(arrived, state_in, whole_load, modes_ref, near_ref, r_ref, l_ref)
    width = scratch.shape[3]
    none = jnp.zeros((1, width - SLOT), jnp.float32)
    lanes = iota((1, width), 1)
    copies = []
    for k, (tile, target) in enumerate(zip(results, (out_multipliers, out_residual))):
        east = jnp.concatenate([tile[0:1], tile[1:2], none], axis=1)
        south = jnp.concatenate([tile[2:3], tile[3:4], none], axis=1)
        south = pltpu.roll(jnp.broadcast_to(south, (TILE, width)), width // 2, 1)[0:1]
        scratch[k, 0] = jnp.where(lanes < width // 2, east, south)
        copies.append(pltpu.make_async_copy(scratch.at[k], target, sems.at[k]))
        copies[k].start()
    for copy in copies:
        copy.wait()


def swapped(block, axis, first):
    count = lax.axis_size(axis)
    route = []
    for i in range(first, count - 1, 2):
        route += [(i, i + 1), (i + 1, i)]
    return lax.ppermute(block, axis, route)


def on_device(gap, kinv, schur, corner_modes, coarse_inverse, edge_map, corner_map, links):
    levels, chunks = lax.axis_size("z"), lax.axis_size("xl") * lax.axis_size("sy")
    width = kinv.shape[-1]
    kinv = kinv.reshape(width, width)
    ints = jnp.int32
    own_modes, col_even, col_odd, row_pair, row_cross, own, group, hits, cmap, schur = call(
        pack_kernel,
        in_hbm(links, corner_modes, edge_map, gap, corner_map, schur),
        [(CORNERS, TILE * LANES)]
        + [(CORNERS + 8, SLOT)] * 4
        + [(TILE, SLOT), jax.ShapeDtypeStruct((1, TILE * LANES), ints)]
        + [jax.ShapeDtypeStruct((LANES, TILE * LANES), jnp.bfloat16)]
        + [(1, SLOT), (width, width)],
        in_specs=[HBM] * 6,
        scratch=[
            pltpu.VMEM(links.shape, ints),
            pltpu.VMEM(corner_modes.shape, jnp.float32),
            pltpu.VMEM(edge_map.shape, ints),
            pltpu.VMEM(gap.shape, jnp.float32),
            pltpu.VMEM(corner_map.shape, ints),
            pltpu.SemaphoreType.DMA((6,)),
        ],
        name="pack",
    )
    row_cross = swapped(row_cross, ROWS_AXES, 1)
    col_odd = swapped(col_odd, "sy", 1)
    row_pair = swapped(row_pair, ROWS_AXES, 0)
    col_even = swapped(col_even, "sy", 0)
    square = (LANES, LANES)
    state_shape = (NSTATE, LANES)
    out, state, near, r, rt, l, mask_row = call(
        start_kernel,
        (
            own, row_cross, col_odd, row_pair, col_even, cmap, group, hits, schur, own_modes,
            *in_hbm(coarse_inverse),
        ),
        [(chunks, 2 * TILE, LANES), state_shape, (CORNERS, TILE * LANES), square, square, square, (1, TILE * LANES)],
        in_specs=[VMEM] * 10 + [HBM],
        scratch=[pltpu.VMEM(coarse_inverse.shape, jnp.float32), pltpu.SemaphoreType.DMA(())],
        name="start",
    )
    to_plane, to_z = (chunks, TILE, LANES), (levels, 4, LANES)
    for step in range(ITERS):
        arrived = lax.all_to_all(out, PLANE, 0, 0, tiled=True)
        if step == 0:
            solver = arrived
        out, state = call(rows_kernel, (arrived, state), [to_z, state_shape], name="rows")
        arrived = lax.all_to_all(out, "z", 0, 0, tiled=True)

        def kernel(*refs, step=step):
            direction_kernel(step, *refs)

        out, state = call(
            kernel, (arrived, state, group, hits, kinv, solver), [to_plane, state_shape], name="direction"
        )
        arrived = lax.all_to_all(out, PLANE, 0, 0, tiled=True)
        out, state, load = call(solve_kernel, (arrived, state), [to_z, state_shape, (chunks, LANES)], name="solve")
        arrived = lax.all_to_all(out, "z", 0, 0, tiled=True)
        common = (arrived, state, load, own_modes, near, r, l)
        if step + 1 < ITERS:
            out, state = call(
                next_kernel, common + (rt, mask_row, group, hits, schur), [to_plane, state_shape], name="next"
            )
    return tuple(
        call(
            last_kernel,
            common,
            [gap.shape] * 2,
            out_specs=[HBM] * 2,
            scratch=[pltpu.VMEM((2,) + gap.shape[:2] + gap.shape[2:], jnp.float32), pltpu.SemaphoreType.DMA((2,))],
            name="last",
        )
    )


def solution(mesh):
    rows, cols = mesh.devices.shape
    split = Mesh(mesh.devices.reshape(rows // 2, 2, cols), ("z", "xl", "sy"))
    placed = (
        P(ROWS_AXES, "sy", None),
        P(ROWS_AXES, "sy", None, None),
        P(ROWS_AXES, "sy", None, None),
        P(ROWS_AXES, "sy", None, None),
        P(("z", "xl", "sy"), None),
        P(ROWS_AXES, "sy", None),
        P(ROWS_AXES, "sy", None),
        P(ROWS_AXES, "sy", None),
    )
    return jax.shard_map(
        on_device,
        mesh=split,
        in_specs=placed,
        out_specs=(P(ROWS_AXES, "sy", None), P(ROWS_AXES, "sy", None)),
        check_vma=False,
    )
```

```python
import jax
import jax.numpy as jnp
from jax import lax
from jax.experimental import pallas as pl
from jax.experimental.pallas import tpu as pltpu
from jax.sharding import Mesh
from jax.sharding import PartitionSpec as P

ITERS = 3
LANES = 128
SLOT = 256
TILE = 8
CORNERS = 24
NDOF = 6
VMEM = pl.BlockSpec(memory_space=pltpu.VMEM)
HBM = pl.BlockSpec(memory_space=pl.ANY)
LIMIT = 40 * 1024 * 1024

ROWS_AXES = ("z", "xl")
PLANE = ("xl", "sy")

RES, MUL, DIR, IFACE, PARTNER, MASK, SCAL, NSTATE = 0, 8, 16, 24, 32, 40, 48, 56
GAMMA, LOAD = 48, 49


def call(kernel, inputs, outputs, in_specs=None, out_specs=None, scratch=(), name=None):
    shapes = [shape if hasattr(shape, "dtype") else jax.ShapeDtypeStruct(shape, jnp.float32) for shape in outputs]
    return pl.pallas_call(
        kernel,
        out_shape=shapes,
        in_specs=in_specs or [VMEM] * len(inputs),
        out_specs=out_specs or [VMEM] * len(outputs),
        scratch_shapes=list(scratch),
        compiler_params=pltpu.CompilerParams(vmem_limit_bytes=LIMIT),
        name=name,
    )(*inputs)


def in_hbm(*arrays):
    return tuple(pltpu.with_memory_space_constraint(array, pltpu.HBM) for array in arrays)


def iota(shape, dim):
    return lax.broadcasted_iota(jnp.int32, shape, dim)


def as_row(tile):
    return jnp.concatenate([tile[c : c + 1, :] for c in range(TILE)], axis=1)


def as_tile(row):
    return jnp.concatenate([row[:, LANES * c : LANES * (c + 1)] for c in range(TILE)], axis=0)


def total(value):
    return jnp.sum(jnp.sum(value, axis=1, keepdims=True), axis=0, keepdims=True)


def slots(row, count, fill):
    width = row.shape[1]
    wide = jnp.broadcast_to(row, (TILE, width))
    lanes = iota((1, SLOT), 1)
    edge = SLOT * 3 // 4
    pieces = []
    for q in range(count):
        moved = wide if q == 0 else pltpu.roll(wide, width - edge * q, 1)
        pieces.append(jnp.where(lanes < edge, moved[0:1, 0:SLOT], fill))
    return pieces


def bf16_parts(value, axis=0):
    first = value.astype(jnp.bfloat16).astype(jnp.float32)
    left = value - first
    second = left.astype(jnp.bfloat16).astype(jnp.float32)
    return jnp.concatenate([first, second, left - second], axis=axis)


def one_hot_product(hits, values):
    parts = bf16_parts(values, axis=1).astype(jnp.bfloat16)
    found = jnp.dot(hits, parts, preferred_element_type=jnp.float32)
    return found[:, 0:LANES] + found[:, LANES : 2 * LANES] + found[:, 2 * LANES : 3 * LANES]


def apply_matrix(tile, group_row, hits, matrix_ref):
    width = matrix_ref.shape[0]
    ours = group_row == iota((TILE, TILE * LANES), 0)
    none = jnp.zeros((TILE, TILE * LANES), jnp.float32)
    parts = bf16_parts(jnp.where(ours, as_row(tile), 0.0))
    parts = jnp.concatenate([parts, none], axis=0).astype(jnp.bfloat16)
    local = lax.dot_general(parts, hits, (((1,), (1,)), ((), ())), preferred_element_type=jnp.float32)
    local = local[0:TILE] + local[TILE : 2 * TILE] + local[2 * TILE : 3 * TILE]
    place = iota((TILE, LANES), 1) - iota((TILE, LANES), 0)
    rows = []
    for b in range(width // LANES):
        block = slice(b * LANES, (b + 1) * LANES)
        acc = matrix_ref[block, 0:LANES] * local[0:1]
        for t in range(1, width // LANES):
            acc = acc + matrix_ref[block, t * LANES : (t + 1) * LANES] * local[t : t + 1]
        column = jnp.sum(acc, axis=1, keepdims=True)
        row = jnp.zeros((TILE, LANES), jnp.float32)
        for k in range(LANES // TILE):
            row = row + jnp.where(place == k * TILE, column[k * TILE : (k + 1) * TILE], 0.0)
        rows.append(jnp.sum(row, axis=0, keepdims=True))
    rows.append(jnp.zeros((TILE - len(rows), LANES), jnp.float32))
    parts = bf16_parts(jnp.concatenate(rows, axis=0))
    parts = jnp.concatenate([parts, jnp.zeros((TILE, LANES), jnp.float32)], axis=0).astype(jnp.bfloat16)
    found = jnp.dot(parts, hits, preferred_element_type=jnp.float32)
    found = found[0:TILE] + found[TILE : 2 * TILE] + found[2 * TILE : 3 * TILE]
    return jnp.sum(jnp.where(ours, found, 0.0), axis=0, keepdims=True)


def coarse_load(weighted, modes_ref, near_ref, rt_ref, l_ref, chunks):
    own = jnp.sum(modes_ref[...] * weighted, axis=1, keepdims=True)
    near = near_ref[...] * weighted
    loads = [own]
    for q in range(4):
        loads.append(-jnp.sum(near[:, SLOT * q : SLOT * (q + 1)], axis=1, keepdims=True))
    loads.append(jnp.zeros((LANES - 5 * CORNERS, 1), jnp.float32))
    column = jnp.concatenate(loads, axis=0)
    return one_hot_product(rt_ref[0:chunks, :], column * l_ref[...])


def plane_edges(tile, target, ncols):
    pair, col = target // ncols, target % ncols
    same = lax.axis_index("xl") == pair
    here = lax.axis_index("sy")
    first = jnp.where(
        same,
        jnp.where(here + 1 == col, tile[0:2], jnp.where(here - 1 == col, tile[4:6], 0.0)),
        jnp.where(here == col, tile[2:4], 0.0),
    )
    second = jnp.where(same, 0.0, jnp.where(here == col, tile[6:8], 0.0))
    return first, second


def plane_arrivals(arrived, row, ncols, dense=False):
    pair, here = lax.axis_index("xl"), lax.axis_index("sy")
    base = pair * ncols
    east = arrived[base + jnp.minimum(here + 1, ncols - 1), row : row + 2, :]
    west = arrived[base + jnp.maximum(here - 1, 0), row : row + 2, :]
    other = (1 - pair) * ncols + here
    if dense:
        both = arrived[other, row : row + 3, :]
        moved = pltpu.roll(jnp.concatenate([both, jnp.zeros((TILE - 3, LANES), jnp.float32)], axis=0), LANES // 2, 1)
        low = iota((1, LANES), 1) < LANES // 2
        their_south = jnp.concatenate([both[0:1], jnp.where(low, both[1:2], 0.0)], axis=0)
        first = jnp.where(low, moved[1:2], moved[2:3])
        their_north = jnp.concatenate([first, jnp.where(low, moved[2:3], 0.0)], axis=0)
    else:
        their_south = arrived[other, row : row + 2, :]
        their_north = arrived[other, row + 2 : row + 4, :]
    south = jnp.where(pair == 0, their_north, 0.0)
    north = jnp.where(pair == 0, 0.0, their_south)
    forward = jnp.where(pair == 0, their_south, their_north)
    return jnp.concatenate([east, south, west, north], axis=0), forward


def z_edge(forward, target):
    goal = jnp.where(lax.axis_index("xl") == 0, lax.axis_index("z") + 1, lax.axis_index("z") - 1)
    return jnp.where(goal == target, forward, 0.0)


def z_arrival(arrived, row, partner):
    levels = arrived.shape[0]
    pair, level = lax.axis_index("xl"), lax.axis_index("z")
    source = jnp.where(pair == 0, jnp.maximum(level - 1, 0), jnp.minimum(level + 1, levels - 1))
    edge = arrived[source, row : row + 2, :]
    south = jnp.where(pair == 0, partner[2:4], edge)
    north = jnp.where(pair == 0, edge, partner[6:8])
    return jnp.concatenate([partner[0:2], south, partner[4:6], north], axis=0)


def apply_schur(tile, group_row, hits, mask_row, schur_ref, modes_ref, near_ref, rt_ref, l_ref, out_ref):
    chunks = out_ref.shape[0]
    y_row = apply_matrix(tile, group_row, hits, schur_ref)
    load = coarse_load(0.25 * mask_row * y_row, modes_ref, near_ref, rt_ref, l_ref, chunks)
    y = as_tile(y_row)
    gamma = jnp.broadcast_to(0.25 * total(tile * y), (1, LANES))
    if out_ref.shape[1] > TILE:
        rest = jnp.zeros((2, LANES), jnp.float32)
        for p in range(chunks):
            first, second = plane_edges(y, p, chunks // 2)
            out_ref[p, 0:TILE, :] = jnp.concatenate([load[p : p + 1], gamma, first, second, rest], axis=0)
        return y
    heads = jnp.where(iota((chunks, LANES), 1) < NDOF * chunks // 2, load, gamma)
    pair, here, ncols = lax.axis_index("xl"), lax.axis_index("sy"), chunks // 2
    none = jnp.zeros((1, LANES), jnp.float32)
    east = jnp.concatenate([y[0:2], none], axis=0)
    west = jnp.concatenate([y[4:6], none], axis=0)
    moved = pltpu.roll(y, LANES // 2, 1)
    low = iota((1, LANES), 1) < LANES // 2
    middle = jnp.where(low, y[3:4], moved[6:7])
    both = jnp.concatenate([y[2:3], middle, jnp.where(low, moved[6:7], moved[7:8])], axis=0)
    to_east = jnp.where(here + 1 < ncols, pair * ncols + here + 1, -1)
    to_west = jnp.where(here > 0, pair * ncols + here - 1, -1)
    to_pair = (1 - pair) * ncols + here
    for p in range(chunks):
        edges = jnp.where(to_east == p, east, jnp.where(to_west == p, west, jnp.where(to_pair == p, both, 0.0)))
        out_ref[p] = jnp.concatenate([heads[p : p + 1], edges], axis=0)
    return y


def pack_kernel(
    links_hbm, modes_hbm, map_hbm, gap_hbm, cmap_hbm, schur_hbm, out_modes, col_even, col_odd, row_pair, row_cross, out_own,
    out_group, out_hits, out_cmap, out_schur, links_ref, modes_ref, map_ref, gap_ref, cmap_ref, sems,
):
    copies = [
        pltpu.make_async_copy(source, target, sems.at[k])
        for k, (source, target) in enumerate(
            (
                (modes_hbm, modes_ref), (map_hbm, map_ref), (gap_hbm, gap_ref), (cmap_hbm, cmap_ref),
                (links_hbm, links_ref),
            )
        )
    ]
    matrix = pltpu.make_async_copy(schur_hbm.at[0, 0], out_schur, sems.at[len(copies)])
    for copy in copies:
        copy.start()
    matrix.start()
    for copy in copies:
        copy.wait()
    nrows, ncols = lax.axis_size("z") * lax.axis_size("xl"), lax.axis_size("sy")
    row_here = lax.axis_index("z") * lax.axis_size("xl") + lax.axis_index("xl")
    map_row = jnp.concatenate(slots(map_ref[0], 4, -1), axis=1)
    group = lax.shift_right_arithmetic(map_row, 7)
    out_group[...] = group
    hits = jnp.where(map_row - LANES * group == iota((LANES, TILE * LANES), 0), 1.0, 0.0)
    hits = jnp.where(group >= 0, hits, 0.0).astype(jnp.bfloat16)
    out_hits[...] = hits
    count = modes_ref.shape[3] // LANES
    parts = [modes_ref[0, 0, :, t * LANES : (t + 1) * LANES] for t in range(count)]
    parts = bf16_parts(jnp.concatenate(parts, axis=0)).astype(jnp.bfloat16)
    found = jnp.dot(parts, hits, preferred_element_type=jnp.float32)
    acc = jnp.zeros((CORNERS, TILE * LANES), jnp.float32)
    for t in range(count):
        pieces = [found[(count * k + t) * CORNERS : (count * k + t + 1) * CORNERS] for k in range(3)]
        acc = acc + jnp.where(group == t, pieces[0] + pieces[1] + pieces[2], 0.0)
    out_modes[...] = acc
    links = jnp.where(links_ref[0] == 1, 1.0, 0.0)
    east = jnp.where(lax.axis_index("sy") < ncols - 1, links[:, 0:1], 0.0)
    south = jnp.where(row_here < nrows - 1, links[:, 1:2], 0.0)
    gaps = slots(gap_ref[0], 2, 0.0)
    out_cmap[...] = jnp.zeros(out_cmap.shape, jnp.float32)
    out_cmap[0:1, 0:CORNERS] = cmap_ref[0].astype(jnp.float32)
    cmap = out_cmap[...]
    rest = jnp.zeros((5, SLOT), jnp.float32)
    none = jnp.zeros((1, SLOT), jnp.float32)
    parts = []
    own = []
    for q in range(4):
        values, mask = none, none
        if q < 2:
            mask = none + (east, south)[q]
            values = gaps[q] * mask
            own += [values, mask]
        parts.append(jnp.concatenate([acc[:, SLOT * q : SLOT * (q + 1)], values, mask, cmap, rest], axis=0))
    out_own[...] = jnp.concatenate(own + [jnp.zeros((4, SLOT), jnp.float32)], axis=0)
    even = lax.axis_index("sy") % 2 == 0
    first_row = lax.axis_index("xl") == 0
    col_even[...] = jnp.where(even, parts[0], parts[2])
    col_odd[...] = jnp.where(even, parts[2], parts[0])
    row_pair[...] = jnp.where(first_row, parts[1], parts[3])
    row_cross[...] = jnp.where(first_row, parts[3], parts[1])
    matrix.wait()


def column_chunk(coarse, p, block):
    start = block * p // LANES * LANES
    window = coarse[:, start : start + SLOT]
    shift = block * p - start
    if shift:
        window = pltpu.roll(window, SLOT - shift, 1)
    return jnp.where(iota((TILE, LANES), 1) < block, window[:, 0:LANES], 0.0)


def start_kernel(
    own_ref, row_cross, col_odd, row_pair, col_even, cmap_ref, group_ref, hits_ref, schur_ref, modes_ref, coarse_hbm, out_ref,
    state, near, r_ref, rt_ref, l_ref, mask_row_ref, coarse_ref, sem,
):
    copy = pltpu.make_async_copy(coarse_hbm, coarse_ref, sem)
    copy.start()
    chunks = out_ref.shape[0]
    block = NDOF * chunks // 2
    row, cm = CORNERS, CORNERS + 2
    even = lax.axis_index("sy") % 2 == 0
    first_row = lax.axis_index("xl") == 0
    from_east = jnp.where(even, col_even[...], col_odd[...])
    from_west = jnp.where(even, col_odd[...], col_even[...])
    from_south = jnp.where(first_row, row_pair[...], row_cross[...])
    from_north = jnp.where(first_row, row_cross[...], row_pair[...])
    sources = (from_east, from_south, from_west, from_north)
    for q, part in enumerate(sources):
        near[:, SLOT * q : SLOT * (q + 1)] = part[0:CORNERS]
    values = [own_ref[0:1], own_ref[2:3], -from_west[row : row + 1], -from_north[row : row + 1]]
    masks = [own_ref[1:2], own_ref[3:4], from_west[row + 1 : row + 2], from_north[row + 1 : row + 2]]
    residual = as_tile(jnp.concatenate(values, axis=1))
    mask_row = jnp.concatenate(masks, axis=1)
    mask_row_ref[...] = mask_row
    maps = [cmap_ref[:, 0:LANES]] + [part[cm : cm + 1, 0:LANES] for part in sources]
    columns = jnp.transpose(jnp.concatenate(maps + [jnp.zeros((3, LANES), jnp.float32)], axis=0))
    column = [columns[0:CORNERS, g : g + 1] for g in range(5)]
    column.append(jnp.full((LANES - 5 * CORNERS, 1), float(block * chunks), jnp.float32))
    column = jnp.concatenate(column, axis=0)
    group = jnp.floor((column + 0.5) * (1.0 / block))
    inside = column - group * block
    lanes = iota((LANES, LANES), 1).astype(jnp.float32)
    hit_row = jnp.where((group == lanes) & (lanes < chunks), 1.0, 0.0)
    r_ref[...] = hit_row.astype(jnp.bfloat16)
    rt_ref[...] = jnp.transpose(hit_row).astype(jnp.bfloat16)
    l_ref[...] = jnp.where(inside == lanes, 1.0, 0.0)
    y = apply_schur(residual, group_ref[...], hits_ref[...], mask_row, schur_ref, modes_ref, near, rt_ref, l_ref, out_ref)
    copy.wait()
    ncoarse = coarse_ref.shape[1]
    wide = (-(-ncoarse // LANES) + 1) * LANES
    coarse = jnp.concatenate([coarse_ref[...], jnp.zeros((TILE - NDOF, ncoarse), jnp.float32)], axis=0)
    coarse = jnp.pad(coarse, ((0, 0), (0, wide - ncoarse)))
    for p in range(chunks):
        out_ref[p, TILE : 2 * TILE, :] = column_chunk(coarse, p, block)
    state[...] = jnp.zeros(state.shape, jnp.float32)
    state[RES : RES + TILE, :] = residual
    state[IFACE : IFACE + TILE, :] = y
    state[MASK : MASK + TILE, :] = as_tile(mask_row)


def rows_kernel(arrived, state_in, out_ref, state):
    chunks, levels = arrived.shape[0], out_ref.shape[0]
    dense = arrived.shape[1] < TILE
    summed = arrived[0, 0:4, :]
    for p in range(1, chunks):
        summed = summed + arrived[p, 0:4, :]
    load, gamma = summed[0:1], summed[1:2]
    if dense:
        gamma = jnp.broadcast_to(load[:, LANES - 1 : LANES], (1, LANES))
        load = jnp.where(iota((1, LANES), 1) < NDOF * chunks // 2, load, 0.0)
    partner, forward = plane_arrivals(arrived, 1 if dense else 2, chunks // 2, dense)
    state[...] = state_in[...]
    state[PARTNER : PARTNER + TILE, :] = partner
    for level in range(levels):
        out_ref[level] = jnp.concatenate([load, gamma, z_edge(forward, level)], axis=0)


def direction_kernel(step, arrived, state_in, group_ref, hits_ref, kinv_ref, blocks_ref, out_ref, state):
    chunks, levels = out_ref.shape[0], arrived.shape[0]
    half = chunks // 2
    summed = arrived[0]
    for level in range(1, levels):
        summed = summed + arrived[level]
    partner = z_arrival(arrived, 2, state_in[PARTNER : PARTNER + TILE, :])
    direction = 0.25 * state_in[MASK : MASK + TILE, :] * (state_in[IFACE : IFACE + TILE, :] - partner)
    load = summed[0:1]
    gamma = summed[1:2]
    if step:
        beta = gamma / state_in[GAMMA : GAMMA + 1, :]
        direction = direction + beta * state_in[DIR : DIR + TILE, :]
        load = load + beta * state_in[LOAD : LOAD + 1, :]
    inner = as_tile(apply_matrix(direction, group_ref[...], hits_ref[...], kinv_ref))
    energy = jnp.broadcast_to(total(direction * inner), (1, LANES))
    lanes = iota((TILE, LANES), 1)
    dof = iota((TILE, LANES), 0)
    solved = []
    for a in range(2):
        acc = jnp.zeros((TILE, LANES), jnp.float32)
        for p in range(half):
            column = jnp.sum(blocks_ref[a * half + p, TILE : 2 * TILE, :] * load, axis=1, keepdims=True)
            acc = acc + jnp.where((lanes == dof + p * NDOF) & (dof < NDOF), column, 0.0)
        solved.append(jnp.sum(acc, axis=0, keepdims=True))
    for p in range(chunks):
        first, second = plane_edges(inner, p, half)
        out_ref[p] = jnp.concatenate(solved + [load, energy, first, second], axis=0)
    state[...] = state_in[...]
    state[DIR : DIR + TILE, :] = direction
    state[IFACE : IFACE + TILE, :] = inner
    state[SCAL : SCAL + TILE, :] = jnp.concatenate([gamma, load, jnp.zeros((6, LANES), jnp.float32)], axis=0)


def solve_kernel(arrived, state_in, out_ref, state, whole_load):
    chunks, levels = arrived.shape[0], out_ref.shape[0]
    block = NDOF * chunks // 2
    summed = arrived[0]
    for p in range(1, chunks):
        summed = summed + arrived[p]
    whole_load[...] = jnp.concatenate([arrived[p, 2:3, :] for p in range(chunks)], axis=0)
    partner, forward = plane_arrivals(arrived, 4, chunks // 2)
    state[...] = state_in[...]
    state[PARTNER : PARTNER + TILE, :] = partner
    first = jnp.where(iota((1, LANES), 1) < block, summed[0:1], summed[3:4])
    for level in range(levels):
        out_ref[level] = jnp.concatenate([first, summed[1:2], z_edge(forward, level)], axis=0)


def advance(arrived, state_in, whole_load, modes_ref, near_ref, r_ref, l_ref):
    levels = arrived.shape[0]
    energy = arrived[0, 0:1, :]
    for level in range(1, levels):
        energy = energy + arrived[level, 0:1, :]
    partner = z_arrival(arrived, 2, state_in[PARTNER : PARTNER + TILE, :])
    solved = jnp.concatenate([arrived[level, 0:2, :] for level in range(levels)], axis=0)
    energy = energy[:, LANES - 1 : LANES] + total(whole_load[...] * solved)
    alpha = state_in[GAMMA : GAMMA + 1, :] / energy
    found = one_hot_product(r_ref[:, 0 : 2 * levels], solved)
    corners = jnp.sum(found * l_ref[...], axis=1, keepdims=True)
    coarse = jnp.sum(corners[0:CORNERS] * modes_ref[...], axis=0, keepdims=True)
    near = []
    for q in range(4):
        values = corners[CORNERS * (q + 1) : CORNERS * (q + 2)]
        near.append(jnp.sum(values * near_ref[:, SLOT * q : SLOT * (q + 1)], axis=0, keepdims=True))
    coarse = as_tile(coarse - jnp.concatenate(near, axis=1))
    image = state_in[MASK : MASK + TILE, :] * (state_in[IFACE : IFACE + TILE, :] - partner + coarse)
    multipliers = state_in[MUL : MUL + TILE, :] + alpha * state_in[DIR : DIR + TILE, :]
    residual = state_in[RES : RES + TILE, :] - alpha * image
    return multipliers, residual


def next_kernel(
    arrived, state_in, whole_load, modes_ref, near_ref, r_ref, l_ref, rt_ref, mask_row_ref, group_ref, hits_ref, schur_ref,
    out_ref, state,
):
    multipliers, residual = advance(arrived, state_in, whole_load, modes_ref, near_ref, r_ref, l_ref)
    y = apply_schur(
        residual, group_ref[...], hits_ref[...], mask_row_ref[...], schur_ref, modes_ref, near_ref, rt_ref, l_ref, out_ref
    )
    state[...] = state_in[...]
    state[RES : RES + TILE, :] = residual
    state[MUL : MUL + TILE, :] = multipliers
    state[IFACE : IFACE + TILE, :] = y


def last_kernel(
    arrived, state_in, whole_load, modes_ref, near_ref, r_ref, l_ref, out_multipliers, out_residual, scratch, sems
):
    results = advance(arrived, state_in, whole_load, modes_ref, near_ref, r_ref, l_ref)
    width = scratch.shape[3]
    none = jnp.zeros((1, width - SLOT), jnp.float32)
    lanes = iota((1, width), 1)
    copies = []
    for k, (tile, target) in enumerate(zip(results, (out_multipliers, out_residual))):
        east = jnp.concatenate([tile[0:1], tile[1:2], none], axis=1)
        south = jnp.concatenate([tile[2:3], tile[3:4], none], axis=1)
        south = pltpu.roll(jnp.broadcast_to(south, (TILE, width)), width // 2, 1)[0:1]
        scratch[k, 0] = jnp.where(lanes < width // 2, east, south)
        copies.append(pltpu.make_async_copy(scratch.at[k], target, sems.at[k]))
        copies[k].start()
    for copy in copies:
        copy.wait()


def swapped(block, axis, first):
    count = lax.axis_size(axis)
    route = []
    for i in range(first, count - 1, 2):
        route += [(i, i + 1), (i + 1, i)]
    return lax.ppermute(block, axis, route)


def on_device(gap, kinv, schur, corner_modes, coarse_inverse, edge_map, corner_map, links):
    levels, chunks = lax.axis_size("z"), lax.axis_size("xl") * lax.axis_size("sy")
    width = kinv.shape[-1]
    kinv = kinv.reshape(width, width)
    ints = jnp.int32
    own_modes, col_even, col_odd, row_pair, row_cross, own, group, hits, cmap, schur = call(
        pack_kernel,
        in_hbm(links, corner_modes, edge_map, gap, corner_map, schur),
        [(CORNERS, TILE * LANES)]
        + [(CORNERS + 8, SLOT)] * 4
        + [(TILE, SLOT), jax.ShapeDtypeStruct((1, TILE * LANES), ints)]
        + [jax.ShapeDtypeStruct((LANES, TILE * LANES), jnp.bfloat16)]
        + [(1, SLOT), (width, width)],
        in_specs=[HBM] * 6,
        scratch=[
            pltpu.VMEM(links.shape, ints),
            pltpu.VMEM(corner_modes.shape, jnp.float32),
            pltpu.VMEM(edge_map.shape, ints),
            pltpu.VMEM(gap.shape, jnp.float32),
            pltpu.VMEM(corner_map.shape, ints),
            pltpu.SemaphoreType.DMA((6,)),
        ],
        name="pack",
    )
    row_cross = swapped(row_cross, ROWS_AXES, 1)
    col_odd = swapped(col_odd, "sy", 1)
    row_pair = swapped(row_pair, ROWS_AXES, 0)
    col_even = swapped(col_even, "sy", 0)
    hits_shape = jax.ShapeDtypeStruct((LANES, LANES), jnp.bfloat16)
    state_shape = (NSTATE, LANES)
    out, state, near, r, rt, l, mask_row = call(
        start_kernel,
        (
            own, row_cross, col_odd, row_pair, col_even, cmap, group, hits, schur, own_modes,
            *in_hbm(coarse_inverse),
        ),
        [(chunks, 2 * TILE, LANES), state_shape, (CORNERS, TILE * LANES), hits_shape, hits_shape]
        + [(LANES, LANES), (1, TILE * LANES)],
        in_specs=[VMEM] * 10 + [HBM],
        scratch=[pltpu.VMEM(coarse_inverse.shape, jnp.float32), pltpu.SemaphoreType.DMA(())],
        name="start",
    )
    to_plane, to_plane_short, to_z = (chunks, TILE, LANES), (chunks, 4, LANES), (levels, 4, LANES)
    for step in range(ITERS):
        arrived = lax.all_to_all(out, PLANE, 0, 0, tiled=True)
        if step == 0:
            solver = arrived
        out, state = call(rows_kernel, (arrived, state), [to_z, state_shape], name="rows")
        arrived = lax.all_to_all(out, "z", 0, 0, tiled=True)

        def kernel(*refs, step=step):
            direction_kernel(step, *refs)

        out, state = call(
            kernel, (arrived, state, group, hits, kinv, solver), [to_plane, state_shape], name="direction"
        )
        arrived = lax.all_to_all(out, PLANE, 0, 0, tiled=True)
        out, state, load = call(solve_kernel, (arrived, state), [to_z, state_shape, (chunks, LANES)], name="solve")
        arrived = lax.all_to_all(out, "z", 0, 0, tiled=True)
        common = (arrived, state, load, own_modes, near, r, l)
        if step + 1 < ITERS:
            out, state = call(
                next_kernel, common + (rt, mask_row, group, hits, schur), [to_plane_short, state_shape], name="next"
            )
    return tuple(
        call(
            last_kernel,
            common,
            [gap.shape] * 2,
            out_specs=[HBM] * 2,
            scratch=[pltpu.VMEM((2,) + gap.shape[:2] + gap.shape[2:], jnp.float32), pltpu.SemaphoreType.DMA((2,))],
            name="last",
        )
    )


def solution(mesh):
    rows, cols = mesh.devices.shape
    split = Mesh(mesh.devices.reshape(rows // 2, 2, cols), ("z", "xl", "sy"))
    placed = (
        P(ROWS_AXES, "sy", None),
        P(ROWS_AXES, "sy", None, None),
        P(ROWS_AXES, "sy", None, None),
        P(ROWS_AXES, "sy", None, None),
        P(("z", "xl", "sy"), None),
        P(ROWS_AXES, "sy", None),
        P(ROWS_AXES, "sy", None),
        P(ROWS_AXES, "sy", None),
    )
    return jax.shard_map(
        on_device,
        mesh=split,
        in_specs=placed,
        out_specs=(P(ROWS_AXES, "sy", None), P(ROWS_AXES, "sy", None)),
        check_vma=False,
    )
```

```python
import jax
import jax.numpy as jnp
from jax import lax
from jax.experimental import pallas as pl
from jax.experimental.pallas import tpu as pltpu
from jax.sharding import Mesh
from jax.sharding import PartitionSpec as P

ITERS = 3
LANES = 128
SLOT = 256
TILE = 8
CORNERS = 24
NDOF = 6
VMEM = pl.BlockSpec(memory_space=pltpu.VMEM)
HBM = pl.BlockSpec(memory_space=pl.ANY)
LIMIT = 40 * 1024 * 1024

ROWS_AXES = ("z", "xl")
PLANE = ("xl", "sy")

RES, MUL, DIR, IFACE, PARTNER, MASK, SCAL, NSTATE = 0, 8, 16, 24, 32, 40, 48, 56
GAMMA, LOAD = 48, 49


def call(kernel, inputs, outputs, in_specs=None, out_specs=None, scratch=(), name=None):
    shapes = [shape if hasattr(shape, "dtype") else jax.ShapeDtypeStruct(shape, jnp.float32) for shape in outputs]
    return pl.pallas_call(
        kernel,
        out_shape=shapes,
        in_specs=in_specs or [VMEM] * len(inputs),
        out_specs=out_specs or [VMEM] * len(outputs),
        scratch_shapes=list(scratch),
        compiler_params=pltpu.CompilerParams(vmem_limit_bytes=LIMIT),
        name=name,
    )(*inputs)


def in_hbm(*arrays):
    return tuple(pltpu.with_memory_space_constraint(array, pltpu.HBM) for array in arrays)


def iota(shape, dim):
    return lax.broadcasted_iota(jnp.int32, shape, dim)


def as_row(tile):
    return jnp.concatenate([tile[c : c + 1, :] for c in range(TILE)], axis=1)


def as_tile(row):
    return jnp.concatenate([row[:, LANES * c : LANES * (c + 1)] for c in range(TILE)], axis=0)


def total(value):
    return jnp.sum(jnp.sum(value, axis=1, keepdims=True), axis=0, keepdims=True)


def slots(row, count, fill):
    width = row.shape[1]
    wide = jnp.broadcast_to(row, (TILE, width))
    lanes = iota((1, SLOT), 1)
    edge = SLOT * 3 // 4
    pieces = []
    for q in range(count):
        moved = wide if q == 0 else pltpu.roll(wide, width - edge * q, 1)
        pieces.append(jnp.where(lanes < edge, moved[0:1, 0:SLOT], fill))
    return pieces


def bf16_parts(value, axis=0):
    first = value.astype(jnp.bfloat16).astype(jnp.float32)
    left = value - first
    second = left.astype(jnp.bfloat16).astype(jnp.float32)
    return jnp.concatenate([first, second, left - second], axis=axis)


def one_hot_product(hits, values):
    parts = bf16_parts(values, axis=1).astype(jnp.bfloat16)
    found = jnp.dot(hits, parts, preferred_element_type=jnp.float32)
    return found[:, 0:LANES] + found[:, LANES : 2 * LANES] + found[:, 2 * LANES : 3 * LANES]


def apply_matrix(tile, group_row, hits, *matrix_refs):
    width = matrix_refs[0].shape[1]
    held = matrix_refs[0].shape[0] // LANES
    ours = group_row == iota((TILE, TILE * LANES), 0)
    none = jnp.zeros((TILE, TILE * LANES), jnp.float32)
    parts = bf16_parts(jnp.where(ours, as_row(tile), 0.0))
    parts = jnp.concatenate([parts, none], axis=0).astype(jnp.bfloat16)
    local = lax.dot_general(parts, hits, (((1,), (1,)), ((), ())), preferred_element_type=jnp.float32)
    local = local[0:TILE] + local[TILE : 2 * TILE] + local[2 * TILE : 3 * TILE]
    place = iota((TILE, LANES), 1) - iota((TILE, LANES), 0)
    rows = []
    for b in range(width // LANES):
        matrix_ref, first = matrix_refs[b // held], b % held * LANES
        block = slice(first, first + LANES)
        acc = matrix_ref[block, 0:LANES] * local[0:1]
        for t in range(1, width // LANES):
            acc = acc + matrix_ref[block, t * LANES : (t + 1) * LANES] * local[t : t + 1]
        column = jnp.sum(acc, axis=1, keepdims=True)
        row = jnp.zeros((TILE, LANES), jnp.float32)
        for k in range(LANES // TILE):
            row = row + jnp.where(place == k * TILE, column[k * TILE : (k + 1) * TILE], 0.0)
        rows.append(jnp.sum(row, axis=0, keepdims=True))
    rows.append(jnp.zeros((TILE - len(rows), LANES), jnp.float32))
    parts = bf16_parts(jnp.concatenate(rows, axis=0))
    parts = jnp.concatenate([parts, jnp.zeros((TILE, LANES), jnp.float32)], axis=0).astype(jnp.bfloat16)
    found = jnp.dot(parts, hits, preferred_element_type=jnp.float32)
    found = found[0:TILE] + found[TILE : 2 * TILE] + found[2 * TILE : 3 * TILE]
    return jnp.sum(jnp.where(ours, found, 0.0), axis=0, keepdims=True)


def coarse_load(weighted, modes_ref, near_ref, rt_ref, l_ref, chunks):
    own = jnp.sum(modes_ref[...] * weighted, axis=1, keepdims=True)
    near = near_ref[...] * weighted
    loads = [own]
    for q in range(4):
        loads.append(-jnp.sum(near[:, SLOT * q : SLOT * (q + 1)], axis=1, keepdims=True))
    loads.append(jnp.zeros((LANES - 5 * CORNERS, 1), jnp.float32))
    column = jnp.concatenate(loads, axis=0)
    return one_hot_product(rt_ref[0:chunks, :], column * l_ref[...])


def plane_edges(tile, target, ncols):
    pair, col = target // ncols, target % ncols
    same = lax.axis_index("xl") == pair
    here = lax.axis_index("sy")
    first = jnp.where(
        same,
        jnp.where(here + 1 == col, tile[0:2], jnp.where(here - 1 == col, tile[4:6], 0.0)),
        jnp.where(here == col, tile[2:4], 0.0),
    )
    second = jnp.where(same, 0.0, jnp.where(here == col, tile[6:8], 0.0))
    return first, second


def plane_arrivals(arrived, row, ncols, dense=False):
    pair, here = lax.axis_index("xl"), lax.axis_index("sy")
    base = pair * ncols
    east = arrived[base + jnp.minimum(here + 1, ncols - 1), row : row + 2, :]
    west = arrived[base + jnp.maximum(here - 1, 0), row : row + 2, :]
    other = (1 - pair) * ncols + here
    if dense:
        both = arrived[other, row : row + 3, :]
        moved = pltpu.roll(jnp.concatenate([both, jnp.zeros((TILE - 3, LANES), jnp.float32)], axis=0), LANES // 2, 1)
        low = iota((1, LANES), 1) < LANES // 2
        their_south = jnp.concatenate([both[0:1], jnp.where(low, both[1:2], 0.0)], axis=0)
        first = jnp.where(low, moved[1:2], moved[2:3])
        their_north = jnp.concatenate([first, jnp.where(low, moved[2:3], 0.0)], axis=0)
    else:
        their_south = arrived[other, row : row + 2, :]
        their_north = arrived[other, row + 2 : row + 4, :]
    south = jnp.where(pair == 0, their_north, 0.0)
    north = jnp.where(pair == 0, 0.0, their_south)
    forward = jnp.where(pair == 0, their_south, their_north)
    return jnp.concatenate([east, south, west, north], axis=0), forward


def z_edge(forward, target):
    goal = jnp.where(lax.axis_index("xl") == 0, lax.axis_index("z") + 1, lax.axis_index("z") - 1)
    return jnp.where(goal == target, forward, 0.0)


def z_arrival(arrived, row, partner):
    levels = arrived.shape[0]
    pair, level = lax.axis_index("xl"), lax.axis_index("z")
    source = jnp.where(pair == 0, jnp.maximum(level - 1, 0), jnp.minimum(level + 1, levels - 1))
    edge = arrived[source, row : row + 2, :]
    south = jnp.where(pair == 0, partner[2:4], edge)
    north = jnp.where(pair == 0, edge, partner[6:8])
    return jnp.concatenate([partner[0:2], south, partner[4:6], north], axis=0)


def apply_schur(tile, group_row, hits, mask_row, schur_refs, modes_ref, near_ref, rt_ref, l_ref, out_ref):
    chunks = out_ref.shape[0]
    y_row = apply_matrix(tile, group_row, hits, *schur_refs)
    load = coarse_load(0.25 * mask_row * y_row, modes_ref, near_ref, rt_ref, l_ref, chunks)
    y = as_tile(y_row)
    gamma = jnp.broadcast_to(0.25 * total(tile * y), (1, LANES))
    if out_ref.shape[1] > TILE:
        rest = jnp.zeros((2, LANES), jnp.float32)
        for p in range(chunks):
            first, second = plane_edges(y, p, chunks // 2)
            out_ref[p, 0:TILE, :] = jnp.concatenate([load[p : p + 1], gamma, first, second, rest], axis=0)
        return y
    heads = jnp.where(iota((chunks, LANES), 1) < NDOF * chunks // 2, load, gamma)
    pair, here, ncols = lax.axis_index("xl"), lax.axis_index("sy"), chunks // 2
    none = jnp.zeros((1, LANES), jnp.float32)
    east = jnp.concatenate([y[0:2], none], axis=0)
    west = jnp.concatenate([y[4:6], none], axis=0)
    moved = pltpu.roll(y, LANES // 2, 1)
    low = iota((1, LANES), 1) < LANES // 2
    middle = jnp.where(low, y[3:4], moved[6:7])
    both = jnp.concatenate([y[2:3], middle, jnp.where(low, moved[6:7], moved[7:8])], axis=0)
    to_east = jnp.where(here + 1 < ncols, pair * ncols + here + 1, -1)
    to_west = jnp.where(here > 0, pair * ncols + here - 1, -1)
    to_pair = (1 - pair) * ncols + here
    for p in range(chunks):
        edges = jnp.where(to_east == p, east, jnp.where(to_west == p, west, jnp.where(to_pair == p, both, 0.0)))
        out_ref[p] = jnp.concatenate([heads[p : p + 1], edges], axis=0)
    return y


def pack_kernel(
    links_hbm, modes_hbm, map_hbm, gap_hbm, cmap_hbm, schur_hbm, out_modes, col_even, col_odd, row_pair, row_cross, out_own,
    out_group, out_hits, out_cmap, out_schur, links_ref, modes_ref, map_ref, gap_ref, cmap_ref, sems,
):
    copies = [
        pltpu.make_async_copy(source, target, sems.at[k])
        for k, (source, target) in enumerate(
            (
                (modes_hbm, modes_ref), (map_hbm, map_ref), (gap_hbm, gap_ref), (cmap_hbm, cmap_ref),
                (links_hbm, links_ref),
            )
        )
    ]
    matrix = pltpu.make_async_copy(schur_hbm.at[0, 0, pl.ds(0, out_schur.shape[0])], out_schur, sems.at[len(copies)])
    for copy in copies:
        copy.start()
    matrix.start()
    for copy in copies:
        copy.wait()
    nrows, ncols = lax.axis_size("z") * lax.axis_size("xl"), lax.axis_size("sy")
    row_here = lax.axis_index("z") * lax.axis_size("xl") + lax.axis_index("xl")
    map_row = jnp.concatenate(slots(map_ref[0], 4, -1), axis=1)
    group = lax.shift_right_arithmetic(map_row, 7)
    out_group[...] = group
    hits = jnp.where(map_row - LANES * group == iota((LANES, TILE * LANES), 0), 1.0, 0.0)
    hits = jnp.where(group >= 0, hits, 0.0).astype(jnp.bfloat16)
    out_hits[...] = hits
    count = modes_ref.shape[3] // LANES
    parts = [modes_ref[0, 0, :, t * LANES : (t + 1) * LANES] for t in range(count)]
    parts = bf16_parts(jnp.concatenate(parts, axis=0)).astype(jnp.bfloat16)
    found = jnp.dot(parts, hits, preferred_element_type=jnp.float32)
    acc = jnp.zeros((CORNERS, TILE * LANES), jnp.float32)
    for t in range(count):
        pieces = [found[(count * k + t) * CORNERS : (count * k + t + 1) * CORNERS] for k in range(3)]
        acc = acc + jnp.where(group == t, pieces[0] + pieces[1] + pieces[2], 0.0)
    out_modes[...] = acc
    links = jnp.where(links_ref[0] == 1, 1.0, 0.0)
    east = jnp.where(lax.axis_index("sy") < ncols - 1, links[:, 0:1], 0.0)
    south = jnp.where(row_here < nrows - 1, links[:, 1:2], 0.0)
    gaps = slots(gap_ref[0], 2, 0.0)
    out_cmap[...] = jnp.zeros(out_cmap.shape, jnp.float32)
    out_cmap[0:1, 0:CORNERS] = cmap_ref[0].astype(jnp.float32)
    cmap = out_cmap[...]
    rest = jnp.zeros((5, SLOT), jnp.float32)
    none = jnp.zeros((1, SLOT), jnp.float32)
    parts = []
    own = []
    for q in range(4):
        values, mask = none, none
        if q < 2:
            mask = none + (east, south)[q]
            values = gaps[q] * mask
            own += [values, mask]
        parts.append(jnp.concatenate([acc[:, SLOT * q : SLOT * (q + 1)], values, mask, cmap, rest], axis=0))
    out_own[...] = jnp.concatenate(own + [jnp.zeros((4, SLOT), jnp.float32)], axis=0)
    even = lax.axis_index("sy") % 2 == 0
    first_row = lax.axis_index("xl") == 0
    col_even[...] = jnp.where(even, parts[0], parts[2])
    col_odd[...] = jnp.where(even, parts[2], parts[0])
    row_pair[...] = jnp.where(first_row, parts[1], parts[3])
    row_cross[...] = jnp.where(first_row, parts[3], parts[1])
    matrix.wait()


def column_chunk(coarse, p, block):
    start = block * p // LANES * LANES
    window = coarse[:, start : start + SLOT]
    shift = block * p - start
    if shift:
        window = pltpu.roll(window, SLOT - shift, 1)
    return jnp.where(iota((TILE, LANES), 1) < block, window[:, 0:LANES], 0.0)


def load_kernel(schur_hbm, coarse_hbm, lower_out, blocks_out, coarse_ref, sems):
    half = lower_out.shape[0]
    matrix = pltpu.make_async_copy(schur_hbm.at[0, 0, pl.ds(half, half)], lower_out, sems.at[0])
    copy = pltpu.make_async_copy(coarse_hbm, coarse_ref, sems.at[1])
    copy.start()
    matrix.start()
    copy.wait()
    chunks, ncoarse = blocks_out.shape[0], coarse_ref.shape[1]
    block = ncoarse // chunks
    wide = (-(-ncoarse // LANES) + 1) * LANES
    coarse = jnp.concatenate([coarse_ref[...], jnp.zeros((TILE - NDOF, ncoarse), jnp.float32)], axis=0)
    coarse = jnp.pad(coarse, ((0, 0), (0, wide - ncoarse)))
    for p in range(chunks):
        blocks_out[p] = column_chunk(coarse, p, block)
    matrix.wait()


def start_kernel(
    own_ref, row_cross, col_odd, row_pair, col_even, cmap_ref, group_ref, hits_ref, upper_ref, lower_ref, modes_ref, blocks_ref,
    out_ref,
    state, near, r_ref, rt_ref, l_ref, mask_row_ref,
):
    schur_refs = (upper_ref, lower_ref)
    chunks = out_ref.shape[0]
    block = NDOF * chunks // 2
    row, cm = CORNERS, CORNERS + 2
    even = lax.axis_index("sy") % 2 == 0
    first_row = lax.axis_index("xl") == 0
    from_east = jnp.where(even, col_even[...], col_odd[...])
    from_west = jnp.where(even, col_odd[...], col_even[...])
    from_south = jnp.where(first_row, row_pair[...], row_cross[...])
    from_north = jnp.where(first_row, row_cross[...], row_pair[...])
    sources = (from_east, from_south, from_west, from_north)
    for q, part in enumerate(sources):
        near[:, SLOT * q : SLOT * (q + 1)] = part[0:CORNERS]
    values = [own_ref[0:1], own_ref[2:3], -from_west[row : row + 1], -from_north[row : row + 1]]
    masks = [own_ref[1:2], own_ref[3:4], from_west[row + 1 : row + 2], from_north[row + 1 : row + 2]]
    residual = as_tile(jnp.concatenate(values, axis=1))
    mask_row = jnp.concatenate(masks, axis=1)
    mask_row_ref[...] = mask_row
    maps = [cmap_ref[:, 0:LANES]] + [part[cm : cm + 1, 0:LANES] for part in sources]
    columns = jnp.transpose(jnp.concatenate(maps + [jnp.zeros((3, LANES), jnp.float32)], axis=0))
    column = [columns[0:CORNERS, g : g + 1] for g in range(5)]
    column.append(jnp.full((LANES - 5 * CORNERS, 1), float(block * chunks), jnp.float32))
    column = jnp.concatenate(column, axis=0)
    group = jnp.floor((column + 0.5) * (1.0 / block))
    inside = column - group * block
    lanes = iota((LANES, LANES), 1).astype(jnp.float32)
    hit_row = jnp.where((group == lanes) & (lanes < chunks), 1.0, 0.0)
    r_ref[...] = hit_row.astype(jnp.bfloat16)
    rt_ref[...] = jnp.transpose(hit_row).astype(jnp.bfloat16)
    l_ref[...] = jnp.where(inside == lanes, 1.0, 0.0)
    y = apply_schur(residual, group_ref[...], hits_ref[...], mask_row, schur_refs, modes_ref, near, rt_ref, l_ref, out_ref)
    for p in range(chunks):
        out_ref[p, TILE : 2 * TILE, :] = blocks_ref[p]
    state[...] = jnp.zeros(state.shape, jnp.float32)
    state[RES : RES + TILE, :] = residual
    state[IFACE : IFACE + TILE, :] = y
    state[MASK : MASK + TILE, :] = as_tile(mask_row)


def rows_kernel(arrived, state_in, out_ref, state):
    chunks, levels = arrived.shape[0], out_ref.shape[0]
    dense = arrived.shape[1] < TILE
    summed = arrived[0, 0:4, :]
    for p in range(1, chunks):
        summed = summed + arrived[p, 0:4, :]
    load, gamma = summed[0:1], summed[1:2]
    if dense:
        gamma = jnp.broadcast_to(load[:, LANES - 1 : LANES], (1, LANES))
        load = jnp.where(iota((1, LANES), 1) < NDOF * chunks // 2, load, 0.0)
    partner, forward = plane_arrivals(arrived, 1 if dense else 2, chunks // 2, dense)
    state[...] = state_in[...]
    state[PARTNER : PARTNER + TILE, :] = partner
    for level in range(levels):
        out_ref[level] = jnp.concatenate([load, gamma, z_edge(forward, level)], axis=0)


def direction_kernel(step, arrived, state_in, group_ref, hits_ref, kinv_ref, blocks_ref, out_ref, state):
    chunks, levels = out_ref.shape[0], arrived.shape[0]
    half = chunks // 2
    summed = arrived[0]
    for level in range(1, levels):
        summed = summed + arrived[level]
    partner = z_arrival(arrived, 2, state_in[PARTNER : PARTNER + TILE, :])
    direction = 0.25 * state_in[MASK : MASK + TILE, :] * (state_in[IFACE : IFACE + TILE, :] - partner)
    load = summed[0:1]
    gamma = summed[1:2]
    if step:
        beta = gamma / state_in[GAMMA : GAMMA + 1, :]
        direction = direction + beta * state_in[DIR : DIR + TILE, :]
        load = load + beta * state_in[LOAD : LOAD + 1, :]
    inner = as_tile(apply_matrix(direction, group_ref[...], hits_ref[...], kinv_ref))
    energy = jnp.broadcast_to(total(direction * inner), (1, LANES))
    lanes = iota((TILE, LANES), 1)
    dof = iota((TILE, LANES), 0)
    solved = []
    for a in range(2):
        acc = jnp.zeros((TILE, LANES), jnp.float32)
        for p in range(half):
            column = jnp.sum(blocks_ref[a * half + p, TILE : 2 * TILE, :] * load, axis=1, keepdims=True)
            acc = acc + jnp.where((lanes == dof + p * NDOF) & (dof < NDOF), column, 0.0)
        solved.append(jnp.sum(acc, axis=0, keepdims=True))
    for p in range(chunks):
        first, second = plane_edges(inner, p, half)
        out_ref[p] = jnp.concatenate(solved + [load, energy, first, second], axis=0)
    state[...] = state_in[...]
    state[DIR : DIR + TILE, :] = direction
    state[IFACE : IFACE + TILE, :] = inner
    state[SCAL : SCAL + TILE, :] = jnp.concatenate([gamma, load, jnp.zeros((6, LANES), jnp.float32)], axis=0)


def solve_kernel(arrived, state_in, out_ref, state, whole_load):
    chunks, levels = arrived.shape[0], out_ref.shape[0]
    block = NDOF * chunks // 2
    summed = arrived[0]
    for p in range(1, chunks):
        summed = summed + arrived[p]
    whole_load[...] = jnp.concatenate([arrived[p, 2:3, :] for p in range(chunks)], axis=0)
    partner, forward = plane_arrivals(arrived, 4, chunks // 2)
    state[...] = state_in[...]
    state[PARTNER : PARTNER + TILE, :] = partner
    first = jnp.where(iota((1, LANES), 1) < block, summed[0:1], summed[3:4])
    for level in range(levels):
        out_ref[level] = jnp.concatenate([first, summed[1:2], z_edge(forward, level)], axis=0)


def advance(arrived, state_in, whole_load, modes_ref, near_ref, r_ref, l_ref):
    levels = arrived.shape[0]
    energy = arrived[0, 0:1, :]
    for level in range(1, levels):
        energy = energy + arrived[level, 0:1, :]
    partner = z_arrival(arrived, 2, state_in[PARTNER : PARTNER + TILE, :])
    solved = jnp.concatenate([arrived[level, 0:2, :] for level in range(levels)], axis=0)
    energy = energy[:, LANES - 1 : LANES] + total(whole_load[...] * solved)
    alpha = state_in[GAMMA : GAMMA + 1, :] / energy
    found = one_hot_product(r_ref[:, 0 : 2 * levels], solved)
    corners = jnp.sum(found * l_ref[...], axis=1, keepdims=True)
    coarse = jnp.sum(corners[0:CORNERS] * modes_ref[...], axis=0, keepdims=True)
    near = []
    for q in range(4):
        values = corners[CORNERS * (q + 1) : CORNERS * (q + 2)]
        near.append(jnp.sum(values * near_ref[:, SLOT * q : SLOT * (q + 1)], axis=0, keepdims=True))
    coarse = as_tile(coarse - jnp.concatenate(near, axis=1))
    image = state_in[MASK : MASK + TILE, :] * (state_in[IFACE : IFACE + TILE, :] - partner + coarse)
    multipliers = state_in[MUL : MUL + TILE, :] + alpha * state_in[DIR : DIR + TILE, :]
    residual = state_in[RES : RES + TILE, :] - alpha * image
    return multipliers, residual


def next_kernel(
    arrived, state_in, whole_load, modes_ref, near_ref, r_ref, l_ref, rt_ref, mask_row_ref, group_ref, hits_ref, upper_ref, lower_ref,
    out_ref, state,
):
    multipliers, residual = advance(arrived, state_in, whole_load, modes_ref, near_ref, r_ref, l_ref)
    y = apply_schur(
        residual, group_ref[...], hits_ref[...], mask_row_ref[...], (upper_ref, lower_ref), modes_ref, near_ref, rt_ref, l_ref, out_ref
    )
    state[...] = state_in[...]
    state[RES : RES + TILE, :] = residual
    state[MUL : MUL + TILE, :] = multipliers
    state[IFACE : IFACE + TILE, :] = y


def last_kernel(
    arrived, state_in, whole_load, modes_ref, near_ref, r_ref, l_ref, out_multipliers, out_residual, scratch, sems
):
    results = advance(arrived, state_in, whole_load, modes_ref, near_ref, r_ref, l_ref)
    width = scratch.shape[3]
    none = jnp.zeros((1, width - SLOT), jnp.float32)
    lanes = iota((1, width), 1)
    copies = []
    for k, (tile, target) in enumerate(zip(results, (out_multipliers, out_residual))):
        east = jnp.concatenate([tile[0:1], tile[1:2], none], axis=1)
        south = jnp.concatenate([tile[2:3], tile[3:4], none], axis=1)
        south = pltpu.roll(jnp.broadcast_to(south, (TILE, width)), width // 2, 1)[0:1]
        scratch[k, 0] = jnp.where(lanes < width // 2, east, south)
        copies.append(pltpu.make_async_copy(scratch.at[k], target, sems.at[k]))
        copies[k].start()
    for copy in copies:
        copy.wait()


def swapped(block, axis, first):
    count = lax.axis_size(axis)
    route = []
    for i in range(first, count - 1, 2):
        route += [(i, i + 1), (i + 1, i)]
    return lax.ppermute(block, axis, route)


def on_device(gap, kinv, schur, corner_modes, coarse_inverse, edge_map, corner_map, links):
    levels, chunks = lax.axis_size("z"), lax.axis_size("xl") * lax.axis_size("sy")
    width = kinv.shape[-1]
    kinv = kinv.reshape(width, width)
    ints = jnp.int32
    own_modes, col_even, col_odd, row_pair, row_cross, own, group, hits, cmap, upper = call(
        pack_kernel,
        in_hbm(links, corner_modes, edge_map, gap, corner_map, schur),
        [(CORNERS, TILE * LANES)]
        + [(CORNERS + 8, SLOT)] * 4
        + [(TILE, SLOT), jax.ShapeDtypeStruct((1, TILE * LANES), ints)]
        + [jax.ShapeDtypeStruct((LANES, TILE * LANES), jnp.bfloat16)]
        + [(1, SLOT), (width // 2, width)],
        in_specs=[HBM] * 6,
        scratch=[
            pltpu.VMEM(links.shape, ints),
            pltpu.VMEM(corner_modes.shape, jnp.float32),
            pltpu.VMEM(edge_map.shape, ints),
            pltpu.VMEM(gap.shape, jnp.float32),
            pltpu.VMEM(corner_map.shape, ints),
            pltpu.SemaphoreType.DMA((6,)),
        ],
        name="pack",
    )
    row_cross = swapped(row_cross, ROWS_AXES, 1)
    col_odd = swapped(col_odd, "sy", 1)
    row_pair = swapped(row_pair, ROWS_AXES, 0)
    col_even = swapped(col_even, "sy", 0)
    lower, blocks = call(
        load_kernel,
        in_hbm(schur, coarse_inverse),
        [(width // 2, width), (chunks, TILE, LANES)],
        in_specs=[HBM] * 2,
        scratch=[pltpu.VMEM(coarse_inverse.shape, jnp.float32), pltpu.SemaphoreType.DMA((2,))],
        name="load",
    )
    hits_shape = jax.ShapeDtypeStruct((LANES, LANES), jnp.bfloat16)
    state_shape = (NSTATE, LANES)
    out, state, near, r, rt, l, mask_row = call(
        start_kernel,
        (
            own, row_cross, col_odd, row_pair, col_even, cmap, group, hits, upper, lower, own_modes, blocks,
        ),
        [(chunks, 2 * TILE, LANES), state_shape, (CORNERS, TILE * LANES), hits_shape, hits_shape]
        + [(LANES, LANES), (1, TILE * LANES)],
        name="start",
    )
    to_plane, to_plane_short, to_z = (chunks, TILE, LANES), (chunks, 4, LANES), (levels, 4, LANES)
    for step in range(ITERS):
        arrived = lax.all_to_all(out, PLANE, 0, 0, tiled=True)
        if step == 0:
            solver = arrived
        out, state = call(rows_kernel, (arrived, state), [to_z, state_shape], name="rows")
        arrived = lax.all_to_all(out, "z", 0, 0, tiled=True)

        def kernel(*refs, step=step):
            direction_kernel(step, *refs)

        out, state = call(
            kernel, (arrived, state, group, hits, kinv, solver), [to_plane, state_shape], name="direction"
        )
        arrived = lax.all_to_all(out, PLANE, 0, 0, tiled=True)
        out, state, load = call(solve_kernel, (arrived, state), [to_z, state_shape, (chunks, LANES)], name="solve")
        arrived = lax.all_to_all(out, "z", 0, 0, tiled=True)
        common = (arrived, state, load, own_modes, near, r, l)
        if step + 1 < ITERS:
            out, state = call(
                next_kernel, common + (rt, mask_row, group, hits, upper, lower), [to_plane_short, state_shape], name="next"
            )
    return tuple(
        call(
            last_kernel,
            common,
            [gap.shape] * 2,
            out_specs=[HBM] * 2,
            scratch=[pltpu.VMEM((2,) + gap.shape[:2] + gap.shape[2:], jnp.float32), pltpu.SemaphoreType.DMA((2,))],
            name="last",
        )
    )


def solution(mesh):
    rows, cols = mesh.devices.shape
    split = Mesh(mesh.devices.reshape(rows // 2, 2, cols), ("z", "xl", "sy"))
    placed = (
        P(ROWS_AXES, "sy", None),
        P(ROWS_AXES, "sy", None, None),
        P(ROWS_AXES, "sy", None, None),
        P(ROWS_AXES, "sy", None, None),
        P(("z", "xl", "sy"), None),
        P(ROWS_AXES, "sy", None),
        P(ROWS_AXES, "sy", None),
        P(ROWS_AXES, "sy", None),
    )
    return jax.shard_map(
        on_device,
        mesh=split,
        in_specs=placed,
        out_specs=(P(ROWS_AXES, "sy", None), P(ROWS_AXES, "sy", None)),
        check_vma=False,
    )
```

```python
import jax
import jax.numpy as jnp
from jax import lax
from jax.experimental import pallas as pl
from jax.experimental.pallas import tpu as pltpu
from jax.sharding import Mesh
from jax.sharding import PartitionSpec as P

ITERS = 3
LANES = 128
SLOT = 256
TILE = 8
CORNERS = 24
NDOF = 6
VMEM = pl.BlockSpec(memory_space=pltpu.VMEM)
HBM = pl.BlockSpec(memory_space=pl.ANY)
LIMIT = 40 * 1024 * 1024

ROWS_AXES = ("z", "xl")
PLANE = ("xl", "sy")

RES, MUL, DIR, IFACE, PARTNER, MASK, SCAL, NSTATE = 0, 8, 16, 24, 32, 40, 48, 56
GAMMA, LOAD = 48, 49


def call(kernel, inputs, outputs, in_specs=None, out_specs=None, scratch=(), name=None):
    shapes = [shape if hasattr(shape, "dtype") else jax.ShapeDtypeStruct(shape, jnp.float32) for shape in outputs]
    return pl.pallas_call(
        kernel,
        out_shape=shapes,
        in_specs=in_specs or [VMEM] * len(inputs),
        out_specs=out_specs or [VMEM] * len(outputs),
        scratch_shapes=list(scratch),
        compiler_params=pltpu.CompilerParams(vmem_limit_bytes=LIMIT),
        name=name,
    )(*inputs)


def in_hbm(*arrays):
    return tuple(pltpu.with_memory_space_constraint(array, pltpu.HBM) for array in arrays)


def iota(shape, dim):
    return lax.broadcasted_iota(jnp.int32, shape, dim)


def as_row(tile):
    return jnp.concatenate([tile[c : c + 1, :] for c in range(TILE)], axis=1)


def as_tile(row):
    return jnp.concatenate([row[:, LANES * c : LANES * (c + 1)] for c in range(TILE)], axis=0)


def total(value):
    return jnp.sum(jnp.sum(value, axis=1, keepdims=True), axis=0, keepdims=True)


def slots(row, count, fill):
    width = row.shape[1]
    wide = jnp.broadcast_to(row, (TILE, width))
    lanes = iota((1, SLOT), 1)
    edge = SLOT * 3 // 4
    pieces = []
    for q in range(count):
        moved = wide if q == 0 else pltpu.roll(wide, width - edge * q, 1)
        pieces.append(jnp.where(lanes < edge, moved[0:1, 0:SLOT], fill))
    return pieces


def bf16_parts(value, axis=0):
    first = value.astype(jnp.bfloat16).astype(jnp.float32)
    left = value - first
    second = left.astype(jnp.bfloat16).astype(jnp.float32)
    return jnp.concatenate([first, second, left - second], axis=axis)


def one_hot_product(hits, values):
    parts = bf16_parts(values, axis=1).astype(jnp.bfloat16)
    found = jnp.dot(hits, parts, preferred_element_type=jnp.float32)
    return found[:, 0:LANES] + found[:, LANES : 2 * LANES] + found[:, 2 * LANES : 3 * LANES]


def apply_matrix(tile, group_row, hits, *matrix_refs):
    width = matrix_refs[0].shape[1]
    held = matrix_refs[0].shape[0] // LANES
    ours = group_row == iota((TILE, TILE * LANES), 0)
    none = jnp.zeros((TILE, TILE * LANES), jnp.float32)
    parts = bf16_parts(jnp.where(ours, as_row(tile), 0.0))
    parts = jnp.concatenate([parts, none], axis=0).astype(jnp.bfloat16)
    local = lax.dot_general(parts, hits, (((1,), (1,)), ((), ())), preferred_element_type=jnp.float32)
    local = local[0:TILE] + local[TILE : 2 * TILE] + local[2 * TILE : 3 * TILE]
    place = iota((TILE, LANES), 1) - iota((TILE, LANES), 0)
    rows = []
    for b in range(width // LANES):
        matrix_ref, first = matrix_refs[b // held], b % held * LANES
        block = slice(first, first + LANES)
        acc = matrix_ref[block, 0:LANES] * local[0:1]
        for t in range(1, width // LANES):
            acc = acc + matrix_ref[block, t * LANES : (t + 1) * LANES] * local[t : t + 1]
        column = jnp.sum(acc, axis=1, keepdims=True)
        row = jnp.zeros((TILE, LANES), jnp.float32)
        for k in range(LANES // TILE):
            row = row + jnp.where(place == k * TILE, column[k * TILE : (k + 1) * TILE], 0.0)
        rows.append(jnp.sum(row, axis=0, keepdims=True))
    rows.append(jnp.zeros((TILE - len(rows), LANES), jnp.float32))
    parts = bf16_parts(jnp.concatenate(rows, axis=0))
    parts = jnp.concatenate([parts, jnp.zeros((TILE, LANES), jnp.float32)], axis=0).astype(jnp.bfloat16)
    found = jnp.dot(parts, hits, preferred_element_type=jnp.float32)
    found = found[0:TILE] + found[TILE : 2 * TILE] + found[2 * TILE : 3 * TILE]
    return jnp.sum(jnp.where(ours, found, 0.0), axis=0, keepdims=True)


def coarse_load(weighted, modes_ref, near_ref, rt_ref, l_ref, chunks):
    own = jnp.sum(modes_ref[...] * weighted, axis=1, keepdims=True)
    near = near_ref[...] * weighted
    loads = [own]
    for q in range(4):
        loads.append(-jnp.sum(near[:, SLOT * q : SLOT * (q + 1)], axis=1, keepdims=True))
    loads.append(jnp.zeros((LANES - 5 * CORNERS, 1), jnp.float32))
    column = jnp.concatenate(loads, axis=0)
    return one_hot_product(rt_ref[0:chunks, :], column * l_ref[...])


def plane_edges(tile, target, ncols):
    pair, col = target // ncols, target % ncols
    same = lax.axis_index("xl") == pair
    here = lax.axis_index("sy")
    first = jnp.where(
        same,
        jnp.where(here + 1 == col, tile[0:2], jnp.where(here - 1 == col, tile[4:6], 0.0)),
        jnp.where(here == col, tile[2:4], 0.0),
    )
    second = jnp.where(same, 0.0, jnp.where(here == col, tile[6:8], 0.0))
    return first, second


def plane_arrivals(arrived, row, ncols, dense=False):
    pair, here = lax.axis_index("xl"), lax.axis_index("sy")
    base = pair * ncols
    east = arrived[base + jnp.minimum(here + 1, ncols - 1), row : row + 2, :]
    west = arrived[base + jnp.maximum(here - 1, 0), row : row + 2, :]
    other = (1 - pair) * ncols + here
    if dense:
        both = arrived[other, row : row + 3, :]
        moved = pltpu.roll(jnp.concatenate([both, jnp.zeros((TILE - 3, LANES), jnp.float32)], axis=0), LANES // 2, 1)
        low = iota((1, LANES), 1) < LANES // 2
        their_south = jnp.concatenate([both[0:1], jnp.where(low, both[1:2], 0.0)], axis=0)
        first = jnp.where(low, moved[1:2], moved[2:3])
        their_north = jnp.concatenate([first, jnp.where(low, moved[2:3], 0.0)], axis=0)
    else:
        their_south = arrived[other, row : row + 2, :]
        their_north = arrived[other, row + 2 : row + 4, :]
    south = jnp.where(pair == 0, their_north, 0.0)
    north = jnp.where(pair == 0, 0.0, their_south)
    forward = jnp.where(pair == 0, their_south, their_north)
    return jnp.concatenate([east, south, west, north], axis=0), forward


def z_edge(forward, target):
    goal = jnp.where(lax.axis_index("xl") == 0, lax.axis_index("z") + 1, lax.axis_index("z") - 1)
    return jnp.where(goal == target, forward, 0.0)


def z_arrival(arrived, row, partner):
    levels = arrived.shape[0]
    pair, level = lax.axis_index("xl"), lax.axis_index("z")
    source = jnp.where(pair == 0, jnp.maximum(level - 1, 0), jnp.minimum(level + 1, levels - 1))
    edge = arrived[source, row : row + 2, :]
    south = jnp.where(pair == 0, partner[2:4], edge)
    north = jnp.where(pair == 0, edge, partner[6:8])
    return jnp.concatenate([partner[0:2], south, partner[4:6], north], axis=0)


def apply_schur(tile, group_row, hits, mask_row, schur_refs, modes_ref, near_ref, rt_ref, l_ref, out_ref):
    chunks = out_ref.shape[0]
    y_row = apply_matrix(tile, group_row, hits, *schur_refs)
    load = coarse_load(0.25 * mask_row * y_row, modes_ref, near_ref, rt_ref, l_ref, chunks)
    y = as_tile(y_row)
    gamma = jnp.broadcast_to(0.25 * total(tile * y), (1, LANES))
    if out_ref.shape[1] > TILE:
        rest = jnp.zeros((2, LANES), jnp.float32)
        for p in range(chunks):
            first, second = plane_edges(y, p, chunks // 2)
            out_ref[p, 0:TILE, :] = jnp.concatenate([load[p : p + 1], gamma, first, second, rest], axis=0)
        return y
    heads = jnp.where(iota((chunks, LANES), 1) < NDOF * chunks // 2, load, gamma)
    pair, here, ncols = lax.axis_index("xl"), lax.axis_index("sy"), chunks // 2
    none = jnp.zeros((1, LANES), jnp.float32)
    east = jnp.concatenate([y[0:2], none], axis=0)
    west = jnp.concatenate([y[4:6], none], axis=0)
    moved = pltpu.roll(y, LANES // 2, 1)
    low = iota((1, LANES), 1) < LANES // 2
    middle = jnp.where(low, y[3:4], moved[6:7])
    both = jnp.concatenate([y[2:3], middle, jnp.where(low, moved[6:7], moved[7:8])], axis=0)
    to_east = jnp.where(here + 1 < ncols, pair * ncols + here + 1, -1)
    to_west = jnp.where(here > 0, pair * ncols + here - 1, -1)
    to_pair = (1 - pair) * ncols + here
    for p in range(chunks):
        edges = jnp.where(to_east == p, east, jnp.where(to_west == p, west, jnp.where(to_pair == p, both, 0.0)))
        out_ref[p] = jnp.concatenate([heads[p : p + 1], edges], axis=0)
    return y


def pack_kernel(
    links_hbm, modes_hbm, map_hbm, gap_hbm, cmap_hbm, schur_hbm, out_modes, col_even, col_odd, row_pair, row_cross, out_own,
    out_group, out_hits, out_cmap, out_schur, links_ref, modes_ref, map_ref, gap_ref, cmap_ref, sems,
):
    copies = [
        pltpu.make_async_copy(source, target, sems.at[k])
        for k, (source, target) in enumerate(
            (
                (map_hbm, map_ref), (modes_hbm, modes_ref), (gap_hbm, gap_ref), (cmap_hbm, cmap_ref),
                (links_hbm, links_ref),
            )
        )
    ]
    matrix = pltpu.make_async_copy(schur_hbm.at[0, 0, pl.ds(0, out_schur.shape[0])], out_schur, sems.at[len(copies)])
    for copy in copies:
        copy.start()
    matrix.start()
    copies[0].wait()
    nrows, ncols = lax.axis_size("z") * lax.axis_size("xl"), lax.axis_size("sy")
    row_here = lax.axis_index("z") * lax.axis_size("xl") + lax.axis_index("xl")
    map_row = jnp.concatenate(slots(map_ref[0], 4, -1), axis=1)
    group = lax.shift_right_arithmetic(map_row, 7)
    out_group[...] = group
    hits = jnp.where(map_row - LANES * group == iota((LANES, TILE * LANES), 0), 1.0, 0.0)
    hits = jnp.where(group >= 0, hits, 0.0).astype(jnp.bfloat16)
    out_hits[...] = hits
    copies[1].wait()
    count = modes_ref.shape[3] // LANES
    parts = [modes_ref[0, 0, :, t * LANES : (t + 1) * LANES] for t in range(count)]
    parts = bf16_parts(jnp.concatenate(parts, axis=0)).astype(jnp.bfloat16)
    found = jnp.dot(parts, hits, preferred_element_type=jnp.float32)
    acc = jnp.zeros((CORNERS, TILE * LANES), jnp.float32)
    for t in range(count):
        pieces = [found[(count * k + t) * CORNERS : (count * k + t + 1) * CORNERS] for k in range(3)]
        acc = acc + jnp.where(group == t, pieces[0] + pieces[1] + pieces[2], 0.0)
    out_modes[...] = acc
    for copy in copies[2:]:
        copy.wait()
    links = jnp.where(links_ref[0] == 1, 1.0, 0.0)
    east = jnp.where(lax.axis_index("sy") < ncols - 1, links[:, 0:1], 0.0)
    south = jnp.where(row_here < nrows - 1, links[:, 1:2], 0.0)
    gaps = slots(gap_ref[0], 2, 0.0)
    out_cmap[...] = jnp.zeros(out_cmap.shape, jnp.float32)
    out_cmap[0:1, 0:CORNERS] = cmap_ref[0].astype(jnp.float32)
    cmap = out_cmap[...]
    rest = jnp.zeros((5, SLOT), jnp.float32)
    none = jnp.zeros((1, SLOT), jnp.float32)
    parts = []
    own = []
    for q in range(4):
        values, mask = none, none
        if q < 2:
            mask = none + (east, south)[q]
            values = gaps[q] * mask
            own += [values, mask]
        parts.append(jnp.concatenate([acc[:, SLOT * q : SLOT * (q + 1)], values, mask, cmap, rest], axis=0))
    out_own[...] = jnp.concatenate(own + [jnp.zeros((4, SLOT), jnp.float32)], axis=0)
    even = lax.axis_index("sy") % 2 == 0
    first_row = lax.axis_index("xl") == 0
    col_even[...] = jnp.where(even, parts[0], parts[2])
    col_odd[...] = jnp.where(even, parts[2], parts[0])
    row_pair[...] = jnp.where(first_row, parts[1], parts[3])
    row_cross[...] = jnp.where(first_row, parts[3], parts[1])
    matrix.wait()


def column_chunk(coarse, p, block):
    start = block * p // LANES * LANES
    window = coarse[:, start : start + SLOT]
    shift = block * p - start
    if shift:
        window = pltpu.roll(window, SLOT - shift, 1)
    return jnp.where(iota((TILE, LANES), 1) < block, window[:, 0:LANES], 0.0)


def load_kernel(schur_hbm, coarse_hbm, lower_out, blocks_out, coarse_ref, sems):
    half = lower_out.shape[0]
    matrix = pltpu.make_async_copy(schur_hbm.at[0, 0, pl.ds(half, half)], lower_out, sems.at[0])
    copy = pltpu.make_async_copy(coarse_hbm, coarse_ref, sems.at[1])
    copy.start()
    matrix.start()
    copy.wait()
    chunks, ncoarse = blocks_out.shape[0], coarse_ref.shape[1]
    block = ncoarse // chunks
    wide = (-(-ncoarse // LANES) + 1) * LANES
    coarse = jnp.concatenate([coarse_ref[...], jnp.zeros((TILE - NDOF, ncoarse), jnp.float32)], axis=0)
    coarse = jnp.pad(coarse, ((0, 0), (0, wide - ncoarse)))
    for p in range(chunks):
        blocks_out[p] = column_chunk(coarse, p, block)
    matrix.wait()


def start_kernel(
    own_ref, row_cross, col_odd, row_pair, col_even, cmap_ref, group_ref, hits_ref, upper_ref, lower_ref, modes_ref, blocks_ref,
    out_ref,
    state, near, r_ref, rt_ref, l_ref, mask_row_ref,
):
    schur_refs = (upper_ref, lower_ref)
    chunks = out_ref.shape[0]
    block = NDOF * chunks // 2
    row, cm = CORNERS, CORNERS + 2
    even = lax.axis_index("sy") % 2 == 0
    first_row = lax.axis_index("xl") == 0
    from_east = jnp.where(even, col_even[...], col_odd[...])
    from_west = jnp.where(even, col_odd[...], col_even[...])
    from_south = jnp.where(first_row, row_pair[...], row_cross[...])
    from_north = jnp.where(first_row, row_cross[...], row_pair[...])
    sources = (from_east, from_south, from_west, from_north)
    for q, part in enumerate(sources):
        near[:, SLOT * q : SLOT * (q + 1)] = part[0:CORNERS]
    values = [own_ref[0:1], own_ref[2:3], -from_west[row : row + 1], -from_north[row : row + 1]]
    masks = [own_ref[1:2], own_ref[3:4], from_west[row + 1 : row + 2], from_north[row + 1 : row + 2]]
    residual = as_tile(jnp.concatenate(values, axis=1))
    mask_row = jnp.concatenate(masks, axis=1)
    mask_row_ref[...] = mask_row
    maps = [cmap_ref[:, 0:LANES]] + [part[cm : cm + 1, 0:LANES] for part in sources]
    columns = jnp.transpose(jnp.concatenate(maps + [jnp.zeros((3, LANES), jnp.float32)], axis=0))
    column = [columns[0:CORNERS, g : g + 1] for g in range(5)]
    column.append(jnp.full((LANES - 5 * CORNERS, 1), float(block * chunks), jnp.float32))
    column = jnp.concatenate(column, axis=0)
    group = jnp.floor((column + 0.5) * (1.0 / block))
    inside = column - group * block
    lanes = iota((LANES, LANES), 1).astype(jnp.float32)
    hit_row = jnp.where((group == lanes) & (lanes < chunks), 1.0, 0.0)
    r_ref[...] = hit_row.astype(jnp.bfloat16)
    rt_ref[...] = jnp.transpose(hit_row).astype(jnp.bfloat16)
    l_ref[...] = jnp.where(inside == lanes, 1.0, 0.0)
    y = apply_schur(residual, group_ref[...], hits_ref[...], mask_row, schur_refs, modes_ref, near, rt_ref, l_ref, out_ref)
    for p in range(chunks):
        out_ref[p, TILE : 2 * TILE, :] = blocks_ref[p]
    state[...] = jnp.zeros(state.shape, jnp.float32)
    state[RES : RES + TILE, :] = residual
    state[IFACE : IFACE + TILE, :] = y
    state[MASK : MASK + TILE, :] = as_tile(mask_row)


def rows_kernel(arrived, state_in, out_ref, state):
    chunks, levels = arrived.shape[0], out_ref.shape[0]
    dense = arrived.shape[1] < TILE
    summed = arrived[0, 0:4, :]
    for p in range(1, chunks):
        summed = summed + arrived[p, 0:4, :]
    load, gamma = summed[0:1], summed[1:2]
    if dense:
        gamma = jnp.broadcast_to(load[:, LANES - 1 : LANES], (1, LANES))
        load = jnp.where(iota((1, LANES), 1) < NDOF * chunks // 2, load, 0.0)
    partner, forward = plane_arrivals(arrived, 1 if dense else 2, chunks // 2, dense)
    state[...] = state_in[...]
    state[PARTNER : PARTNER + TILE, :] = partner
    for level in range(levels):
        out_ref[level] = jnp.concatenate([load, gamma, z_edge(forward, level)], axis=0)


def direction_kernel(step, arrived, state_in, group_ref, hits_ref, kinv_ref, blocks_ref, out_ref, state):
    chunks, levels = out_ref.shape[0], arrived.shape[0]
    half = chunks // 2
    summed = arrived[0]
    for level in range(1, levels):
        summed = summed + arrived[level]
    partner = z_arrival(arrived, 2, state_in[PARTNER : PARTNER + TILE, :])
    direction = 0.25 * state_in[MASK : MASK + TILE, :] * (state_in[IFACE : IFACE + TILE, :] - partner)
    load = summed[0:1]
    gamma = summed[1:2]
    if step:
        beta = gamma / state_in[GAMMA : GAMMA + 1, :]
        direction = direction + beta * state_in[DIR : DIR + TILE, :]
        load = load + beta * state_in[LOAD : LOAD + 1, :]
    inner = as_tile(apply_matrix(direction, group_ref[...], hits_ref[...], kinv_ref))
    energy = jnp.broadcast_to(total(direction * inner), (1, LANES))
    lanes = iota((TILE, LANES), 1)
    dof = iota((TILE, LANES), 0)
    solved = []
    for a in range(2):
        acc = jnp.zeros((TILE, LANES), jnp.float32)
        for p in range(half):
            column = jnp.sum(blocks_ref[a * half + p, TILE : 2 * TILE, :] * load, axis=1, keepdims=True)
            acc = acc + jnp.where((lanes == dof + p * NDOF) & (dof < NDOF), column, 0.0)
        solved.append(jnp.sum(acc, axis=0, keepdims=True))
    for p in range(chunks):
        first, second = plane_edges(inner, p, half)
        out_ref[p] = jnp.concatenate(solved + [load, energy, first, second], axis=0)
    state[...] = state_in[...]
    state[DIR : DIR + TILE, :] = direction
    state[IFACE : IFACE + TILE, :] = inner
    state[SCAL : SCAL + TILE, :] = jnp.concatenate([gamma, load, jnp.zeros((6, LANES), jnp.float32)], axis=0)


def solve_kernel(arrived, state_in, out_ref, state, whole_load):
    chunks, levels = arrived.shape[0], out_ref.shape[0]
    block = NDOF * chunks // 2
    summed = arrived[0]
    for p in range(1, chunks):
        summed = summed + arrived[p]
    whole_load[...] = jnp.concatenate([arrived[p, 2:3, :] for p in range(chunks)], axis=0)
    partner, forward = plane_arrivals(arrived, 4, chunks // 2)
    state[...] = state_in[...]
    state[PARTNER : PARTNER + TILE, :] = partner
    first = jnp.where(iota((1, LANES), 1) < block, summed[0:1], summed[3:4])
    for level in range(levels):
        out_ref[level] = jnp.concatenate([first, summed[1:2], z_edge(forward, level)], axis=0)


def advance(arrived, state_in, whole_load, modes_ref, near_ref, r_ref, l_ref):
    levels = arrived.shape[0]
    energy = arrived[0, 0:1, :]
    for level in range(1, levels):
        energy = energy + arrived[level, 0:1, :]
    partner = z_arrival(arrived, 2, state_in[PARTNER : PARTNER + TILE, :])
    solved = jnp.concatenate([arrived[level, 0:2, :] for level in range(levels)], axis=0)
    energy = energy[:, LANES - 1 : LANES] + total(whole_load[...] * solved)
    alpha = state_in[GAMMA : GAMMA + 1, :] / energy
    found = one_hot_product(r_ref[:, 0 : 2 * levels], solved)
    corners = jnp.sum(found * l_ref[...], axis=1, keepdims=True)
    coarse = jnp.sum(corners[0:CORNERS] * modes_ref[...], axis=0, keepdims=True)
    near = []
    for q in range(4):
        values = corners[CORNERS * (q + 1) : CORNERS * (q + 2)]
        near.append(jnp.sum(values * near_ref[:, SLOT * q : SLOT * (q + 1)], axis=0, keepdims=True))
    coarse = as_tile(coarse - jnp.concatenate(near, axis=1))
    image = state_in[MASK : MASK + TILE, :] * (state_in[IFACE : IFACE + TILE, :] - partner + coarse)
    multipliers = state_in[MUL : MUL + TILE, :] + alpha * state_in[DIR : DIR + TILE, :]
    residual = state_in[RES : RES + TILE, :] - alpha * image
    return multipliers, residual


def next_kernel(
    arrived, state_in, whole_load, modes_ref, near_ref, r_ref, l_ref, rt_ref, mask_row_ref, group_ref, hits_ref, upper_ref, lower_ref,
    out_ref, state,
):
    multipliers, residual = advance(arrived, state_in, whole_load, modes_ref, near_ref, r_ref, l_ref)
    y = apply_schur(
        residual, group_ref[...], hits_ref[...], mask_row_ref[...], (upper_ref, lower_ref), modes_ref, near_ref, rt_ref, l_ref, out_ref
    )
    state[...] = state_in[...]
    state[RES : RES + TILE, :] = residual
    state[MUL : MUL + TILE, :] = multipliers
    state[IFACE : IFACE + TILE, :] = y


def last_kernel(
    arrived, state_in, whole_load, modes_ref, near_ref, r_ref, l_ref, out_multipliers, out_residual, scratch, sems
):
    results = advance(arrived, state_in, whole_load, modes_ref, near_ref, r_ref, l_ref)
    width = scratch.shape[3]
    none = jnp.zeros((1, width - SLOT), jnp.float32)
    lanes = iota((1, width), 1)
    copies = []
    for k, (tile, target) in enumerate(zip(results, (out_multipliers, out_residual))):
        east = jnp.concatenate([tile[0:1], tile[1:2], none], axis=1)
        south = jnp.concatenate([tile[2:3], tile[3:4], none], axis=1)
        south = pltpu.roll(jnp.broadcast_to(south, (TILE, width)), width // 2, 1)[0:1]
        scratch[k, 0] = jnp.where(lanes < width // 2, east, south)
        copies.append(pltpu.make_async_copy(scratch.at[k], target, sems.at[k]))
        copies[k].start()
    for copy in copies:
        copy.wait()


def swapped(block, axis, first):
    count = lax.axis_size(axis)
    route = []
    for i in range(first, count - 1, 2):
        route += [(i, i + 1), (i + 1, i)]
    return lax.ppermute(block, axis, route)


def on_device(gap, kinv, schur, corner_modes, coarse_inverse, edge_map, corner_map, links):
    levels, chunks = lax.axis_size("z"), lax.axis_size("xl") * lax.axis_size("sy")
    width = kinv.shape[-1]
    kinv = kinv.reshape(width, width)
    ints = jnp.int32
    own_modes, col_even, col_odd, row_pair, row_cross, own, group, hits, cmap, upper = call(
        pack_kernel,
        in_hbm(links, corner_modes, edge_map, gap, corner_map, schur),
        [(CORNERS, TILE * LANES)]
        + [(CORNERS + 8, SLOT)] * 4
        + [(TILE, SLOT), jax.ShapeDtypeStruct((1, TILE * LANES), ints)]
        + [jax.ShapeDtypeStruct((LANES, TILE * LANES), jnp.bfloat16)]
        + [(1, SLOT), (width // 2, width)],
        in_specs=[HBM] * 6,
        scratch=[
            pltpu.VMEM(links.shape, ints),
            pltpu.VMEM(corner_modes.shape, jnp.float32),
            pltpu.VMEM(edge_map.shape, ints),
            pltpu.VMEM(gap.shape, jnp.float32),
            pltpu.VMEM(corner_map.shape, ints),
            pltpu.SemaphoreType.DMA((6,)),
        ],
        name="pack",
    )
    row_cross = swapped(row_cross, ROWS_AXES, 1)
    col_odd = swapped(col_odd, "sy", 1)
    row_pair = swapped(row_pair, ROWS_AXES, 0)
    col_even = swapped(col_even, "sy", 0)
    lower, blocks = call(
        load_kernel,
        in_hbm(schur, coarse_inverse),
        [(width // 2, width), (chunks, TILE, LANES)],
        in_specs=[HBM] * 2,
        scratch=[pltpu.VMEM(coarse_inverse.shape, jnp.float32), pltpu.SemaphoreType.DMA((2,))],
        name="load",
    )
    hits_shape = jax.ShapeDtypeStruct((LANES, LANES), jnp.bfloat16)
    state_shape = (NSTATE, LANES)
    out, state, near, r, rt, l, mask_row = call(
        start_kernel,
        (
            own, row_cross, col_odd, row_pair, col_even, cmap, group, hits, upper, lower, own_modes, blocks,
        ),
        [(chunks, 2 * TILE, LANES), state_shape, (CORNERS, TILE * LANES), hits_shape, hits_shape]
        + [(LANES, LANES), (1, TILE * LANES)],
        name="start",
    )
    to_plane, to_plane_short, to_z = (chunks, TILE, LANES), (chunks, 4, LANES), (levels, 4, LANES)
    for step in range(ITERS):
        arrived = lax.all_to_all(out, PLANE, 0, 0, tiled=True)
        if step == 0:
            solver = arrived
        out, state = call(rows_kernel, (arrived, state), [to_z, state_shape], name="rows")
        arrived = lax.all_to_all(out, "z", 0, 0, tiled=True)

        def kernel(*refs, step=step):
            direction_kernel(step, *refs)

        out, state = call(
            kernel, (arrived, state, group, hits, kinv, solver), [to_plane, state_shape], name="direction"
        )
        arrived = lax.all_to_all(out, PLANE, 0, 0, tiled=True)
        out, state, load = call(solve_kernel, (arrived, state), [to_z, state_shape, (chunks, LANES)], name="solve")
        arrived = lax.all_to_all(out, "z", 0, 0, tiled=True)
        common = (arrived, state, load, own_modes, near, r, l)
        if step + 1 < ITERS:
            out, state = call(
                next_kernel, common + (rt, mask_row, group, hits, upper, lower), [to_plane_short, state_shape], name="next"
            )
    return tuple(
        call(
            last_kernel,
            common,
            [gap.shape] * 2,
            out_specs=[HBM] * 2,
            scratch=[pltpu.VMEM((2,) + gap.shape[:2] + gap.shape[2:], jnp.float32), pltpu.SemaphoreType.DMA((2,))],
            name="last",
        )
    )


def solution(mesh):
    rows, cols = mesh.devices.shape
    split = Mesh(mesh.devices.reshape(rows // 2, 2, cols), ("z", "xl", "sy"))
    placed = (
        P(ROWS_AXES, "sy", None),
        P(ROWS_AXES, "sy", None, None),
        P(ROWS_AXES, "sy", None, None),
        P(ROWS_AXES, "sy", None, None),
        P(("z", "xl", "sy"), None),
        P(ROWS_AXES, "sy", None),
        P(ROWS_AXES, "sy", None),
        P(ROWS_AXES, "sy", None),
    )
    return jax.shard_map(
        on_device,
        mesh=split,
        in_specs=placed,
        out_specs=(P(ROWS_AXES, "sy", None), P(ROWS_AXES, "sy", None)),
        check_vma=False,
    )
```
